32 devices in a mesh: dp: 8 (over z, y), tensor: 4 (over x, core).
Axes of the slice: x: 2, y: 2, z: 4, core: 2. Of those that a mesh axis runs over, the one named last changes fastest.
Arguments:
- new_pages: bfloat16 [64, 128, 8192], P('dp', None, 'tensor'), may hold values from -6 to 6
- page_dest: int32 [64], replicated, may hold values from 0 to 63, as said below
- resident: bfloat16 [64, 128, 8192], P('dp', None, 'tensor'), may hold values from -6 to 6
- queries: bfloat16 [64, 4096], P('dp', 'tensor'), may hold values from -6 to 6
- page_table: int32 [64, 8], P('dp'), may hold values from 0 to 15, as said below
- cross_len: int32 [64], P('dp'), may hold values from 1 to 8, as said below
Outputs:
- arrived: bfloat16 [64, 128, 8192], P('dp', None, 'tensor')
- context: bfloat16 [64, 4096], P('dp', 'tensor')
The draws below stay inside these ranges and needn't reach their ends.
Inputs may be any that keep to these rules, and one draw needn't show every extreme that they name: page_dest is a permutation. There is one offset o, not zero and the same for all groups, such that every new page of group g (pages g * 8 to g * 8 + 7) goes to group g + o modulo the number of groups. `page_table`: the entries of one row are distinct slots of the request's group pool; the first entry is a resident slot; entries at or past the request's length are not read. `cross_len`: the first request of every group reads 8 pages.
All inputs are finite; a program needn't handle non-finite values.
Results may differ from the reference program's by a relative error of at most 0.0034.
Values may be sent and summed in bfloat16 or wider, within the bound.
No kernel may reach another device: no remote copies, remote signals or barrier semaphores. Data moves between devices by JAX's collectives and lax.ppermute only.
A program may use at most 128 MiB of HBM per device.

```python
import jax
import jax.numpy as jnp
from jax import lax

D = 4096
HEADS = 16
HEAD_DIM = 256
PAGE = 128
MAXP = 8
REQ_DEV = 8
RES = 8
CAP = 8
KV = 8192
SLOTS = 16
PAGES = 64
REQS = 64
N_DP = 8


def draw_page_dest(key, part):
    offset = jax.random.randint(jax.random.fold_in(key, 41), (), 1, N_DP).astype(jnp.int32)
    group_keys = jax.random.split(jax.random.fold_in(key, 42), N_DP)
    slot_rows = jax.vmap(lambda k: jax.random.permutation(k, CAP))(group_keys).astype(jnp.int32)
    targets = (jnp.arange(N_DP, dtype=jnp.int32) + offset) % N_DP
    return (targets[:, None] * CAP + slot_rows).reshape(PAGES).astype(jnp.int32)


def draw_resident(key, part):
    shape = (N_DP * RES, PAGE, HEADS, 2, HEAD_DIM)
    base = jnp.clip(jax.random.normal(jax.random.fold_in(key, 1), shape, jnp.float32), -6.0, 6.0)
    return base.reshape(N_DP * RES, PAGE, KV).astype(jnp.bfloat16)


def draw_queries(key, part):
    shape = (REQS, HEADS, HEAD_DIM)
    base = jnp.clip(0.15 * jax.random.normal(jax.random.fold_in(key, 2), shape, jnp.float32), -6.0, 6.0)
    return base.reshape(REQS, D).astype(jnp.bfloat16)


def draw_page_table(key, part):
    first = jax.random.randint(jax.random.fold_in(key, 22), (REQS,), 0, RES).astype(jnp.int32)
    row_keys = jax.random.split(jax.random.fold_in(key, 21), REQS)
    others = jax.vmap(lambda k: jax.random.permutation(k, SLOTS - 1))(row_keys)[:, :MAXP - 1].astype(jnp.int32)
    others = others + (others >= first[:, None]).astype(jnp.int32)
    return jnp.concatenate([first[:, None], others], 1).astype(jnp.int32)


def draw_cross_len(key, part):
    lengths = jax.random.randint(jax.random.fold_in(key, 31), (REQS,), 1, MAXP + 1).astype(jnp.int32)
    return lengths.at[::REQ_DEV].set(MAXP).astype(jnp.int32)


def shard_levels(rng, dims, cuts, smallest, top_value):
    def one(axis_at, shards_of):
        steps = jax.random.uniform(jax.random.fold_in(jax.random.fold_in(rng, 6), axis_at), (shards_of,), jnp.float32, smallest / len(cuts), top_value / len(cuts))
        return jnp.repeat(jnp.exp(steps), dims[axis_at] // shards_of).reshape((-1,) + (1,) * (len(dims) - axis_at - 1))

    gain = one(*cuts[0])
    for cut in cuts[1:]:
        gain = gain * one(*cut)
    return gain


def gaussian(stream_key, shape, spread, limit, pieces=(), kind=jnp.bfloat16):
    values = spread * jax.random.normal(stream_key, shape, jnp.float32)
    if pieces:
        values = values * shard_levels(stream_key, shape, pieces, -0.22, 0.18)
    return jnp.clip(values, -limit, limit).astype(kind)


def setup_inputs(seed: int = 0) -> dict:
    keys = jax.random.split(jax.random.key(seed), 7)
    new_pages = gaussian(keys[0], (PAGES, PAGE, KV), 1.0, 6.0, ((0, 8), (2, 4)))
    page_dest = draw_page_dest(jax.random.fold_in(keys[6], 71), 0)
    resident = draw_resident(jax.random.fold_in(keys[6], 71), 0)
    queries = draw_queries(jax.random.fold_in(keys[6], 71), 0)
    page_table = draw_page_table(jax.random.fold_in(keys[6], 71), 0)
    cross_len = draw_cross_len(jax.random.fold_in(keys[6], 71), 0)
    return dict(new_pages=new_pages, page_dest=page_dest, resident=resident, queries=queries, page_table=page_table, cross_len=cross_len)


def attend_group(items):
    res_pages, new_slots, query_rows, table_rows, length_rows = items
    pool = jnp.concatenate([res_pages, new_slots], 0).astype(jnp.float32)
    pool = pool.reshape(SLOTS, PAGE, HEADS, 2, HEAD_DIM)
    within = jnp.arange(MAXP, dtype=jnp.int32)[None, :] < length_rows[:, None]
    member = (table_rows[:, :, None] == jnp.arange(SLOTS, dtype=jnp.int32)[None, None, :]) & within[:, :, None]
    live = jnp.any(member, axis=1)
    scores = jnp.einsum("rhd,sphd->rhsp", query_rows.astype(jnp.float32), pool[:, :, :, 0, :], precision=lax.Precision.HIGHEST)
    scores = jnp.where(live[:, None, :, None], scores, -jnp.inf)
    peak = jnp.max(scores, axis=(2, 3), keepdims=True)
    prob = jnp.exp(scores - peak)
    total = jnp.sum(prob, axis=(2, 3))
    weights = lax.optimization_barrier(prob.astype(jnp.bfloat16)).astype(jnp.float32)
    summed = jnp.einsum("rhsp,sphd->rhd", weights, pool[:, :, :, 1, :], precision=lax.Precision.HIGHEST)
    return (summed / total[:, :, None]).astype(jnp.bfloat16).reshape(REQ_DEV, D)


def reference(new_pages, page_dest, resident, queries, page_table, cross_len):
    arrived = jnp.zeros((PAGES, PAGE, KV), jnp.bfloat16).at[page_dest].set(new_pages)
    groups = (
        resident.reshape(N_DP, RES, PAGE, KV),
        arrived.reshape(N_DP, CAP, PAGE, KV),
        queries.reshape(N_DP, REQ_DEV, HEADS, HEAD_DIM),
        page_table.reshape(N_DP, REQ_DEV, MAXP),
        cross_len.reshape(N_DP, REQ_DEV),
    )
    context = lax.map(attend_group, groups)
    return arrived, context.reshape(REQS, D)
```

```python
import functools

import jax
import jax.numpy as jnp
from jax import lax
from jax.experimental import pallas as pl
from jax.experimental.pallas import tpu as pltpu
from jax.sharding import PartitionSpec as P

HEAD_DIM = 256
RADIX = 8


def shift(block, axis, distance):
    n = lax.axis_size(axis)
    return lax.ppermute(block, axis, [(i, (i + distance) % n) for i in range(n)])


def nt_dot(a, b):
    return lax.dot_general(a, b, (((1,), (1,)), ((), ())), preferred_element_type=jnp.float32)


def head_kernel(q_ref, bias_ref, res_ref, late_ref, *rest):
    arrived_ref, context_ref = rest[-2:]
    n_res = res_ref.shape[0] * res_ref.shape[1]
    n_late = late_ref.shape[0] * late_ref.shape[1]
    d = q_ref.shape[1]
    q = q_ref[...]
    arrived_ref[...] = late_ref[...]
    early = nt_dot(q, res_ref[:, :, :d].reshape(n_res, d)) + bias_ref[:, :n_res]
    late = nt_dot(q, late_ref[:, :, :d].reshape(n_late, d)) + bias_ref[:, n_res:]
    peak = jnp.maximum(
        jnp.max(early, axis=1, keepdims=True), jnp.max(late, axis=1, keepdims=True)
    )
    early = jnp.exp(early - peak)
    late = jnp.exp(late - peak)
    total = jnp.sum(early, axis=1, keepdims=True) + jnp.sum(late, axis=1, keepdims=True)
    summed = jnp.dot(
        early.astype(jnp.bfloat16),
        res_ref[:, :, d:].reshape(n_res, d),
        preferred_element_type=jnp.float32,
    ) + jnp.dot(
        late.astype(jnp.bfloat16),
        late_ref[:, :, d:].reshape(n_late, d),
        preferred_element_type=jnp.float32,
    )
    context_ref[...] = (summed / total).astype(context_ref.dtype)


def attend_head(head, queries, bias, resident, late, arrived):
    requests = queries.shape[0]
    pages, tokens, columns = late.shape
    d = columns // 2
    n_res = resident.shape[0]
    operands = [queries, bias, resident, late]
    specs = [
        pl.BlockSpec((requests, d), lambda i: (0, head)),
        pl.BlockSpec(bias.shape, lambda i: (0, 0)),
        pl.BlockSpec((n_res, tokens, columns), lambda i: (0, 0, head)),
        pl.BlockSpec((pages, tokens, columns), lambda i: (0, 0, 0)),
    ]
    aliases = {}
    if arrived is not None:
        operands.append(arrived)
        specs.append(pl.BlockSpec(memory_space=pl.ANY))
        aliases = {len(operands) - 1: 0}
    width = resident.shape[2]
    pool = (n_res + pages) * tokens
    return pl.pallas_call(
        head_kernel,
        grid=(1,),
        in_specs=specs,
        out_specs=[
            pl.BlockSpec((pages, tokens, columns), lambda i: (0, 0, head)),
            pl.BlockSpec((requests, d), lambda i: (0, 0)),
        ],
        out_shape=[
            jax.ShapeDtypeStruct((pages, tokens, width), late.dtype),
            jax.ShapeDtypeStruct((requests, d), queries.dtype),
        ],
        input_output_aliases=aliases,
        compiler_params=pltpu.CompilerParams(vmem_limit_bytes=24 * 1024 * 1024),
        cost_estimate=pl.CostEstimate(
            flops=4 * requests * pool * d,
            bytes_accessed=2 * (pool + pages * tokens) * columns,
            transcendentals=requests * pool,
        ),
    )(*operands)


def offset_digits(n):
    digits = []
    place = 1
    while place < n:
        digits.append((place, min(RADIX, -(-n // place))))
        place *= RADIX
    return digits


def local(new_pages, page_dest, resident, queries, page_table, cross_len):
    n_groups = lax.axis_size("dp")
    group = lax.axis_index("dp")
    tokens = resident.shape[1]
    columns = 2 * HEAD_DIM
    heads_dev = resident.shape[2] // columns
    n_res = resident.shape[0]
    cap = new_pages.shape[0]
    n_slots = n_res + cap

    slots = jnp.arange(n_slots, dtype=jnp.int32)
    within = jnp.arange(page_table.shape[1], dtype=jnp.int32)[None, :] < cross_len[:, None]
    member = (page_table[:, :, None] == slots[None, None, :]) & within[:, :, None]
    bias = jnp.where(jnp.any(member, axis=1), 0.0, -jnp.inf).astype(jnp.float32)
    bias = jnp.repeat(bias, tokens, axis=1)

    offset = page_dest[0] // cap
    slot_of = lax.dynamic_slice_in_dim(page_dest, group * cap, cap) % cap
    pages = jnp.arange(cap, dtype=jnp.int32)
    source_of = jnp.sum(
        jnp.where(slot_of[None, :] == pages[:, None], pages[None, :], 0), axis=1
    )
    staged = tuple(
        new_pages[:, :, h * columns : (h + 1) * columns]
        .at[source_of]
        .get(mode="promise_in_bounds")
        for h in range(heads_dev)
    )

    digits = offset_digits(n_groups)

    def send(distance, chunks):
        return tuple(shift(c, "dp", distance) if distance else c for c in chunks)

    def send_and_attend(distance, chunks, resident, queries, bias):
        arrived = None
        parts = []
        chunks = send(distance, chunks)
        for h, chunk in enumerate(chunks):
            arrived, part = attend_head(h, queries, bias, resident, chunk, arrived)
            parts.append(part)
        return arrived, jnp.concatenate(parts, axis=1)

    for place, base in digits[:-1]:
        digit = offset // place % base
        staged = lax.switch(
            digit, [functools.partial(send, d * place) for d in range(base)], staged
        )
    place, base = digits[-1]
    digit = offset // place % base
    first = 1 if len(digits) == 1 else 0
    return lax.switch(
        digit - first,
        [functools.partial(send_and_attend, d * place) for d in range(first, base)],
        staged,
        resident,
        queries,
        bias,
    )


def solution(mesh):
    return jax.shard_map(
        local,
        mesh=mesh,
        in_specs=(
            P("dp", None, "tensor"),
            P(),
            P("dp", None, "tensor"),
            P("dp", "tensor"),
            P("dp", None),
            P("dp"),
        ),
        out_specs=(P("dp", None, "tensor"), P("dp", "tensor")),
        check_vma=False,
    )
```

```python
import functools

import jax
import jax.numpy as jnp
from jax import lax
from jax.experimental import pallas as pl
from jax.experimental.pallas import tpu as pltpu
from jax.sharding import PartitionSpec as P

HEAD_DIM = 256
RADIX = 8
VMEM_LIMIT = 24 * 1024 * 1024


def route(block, step_of):
    n = lax.axis_size("dp")
    return lax.ppermute(block, "dp", [(i, step_of(i) % n) for i in range(n)])


def stage_kernel(start, width, dest_ref, pages_ref, out_ref, sems):
    cap = pages_ref.shape[0]
    first = lax.axis_index("dp") * cap
    copies = []
    for j in range(cap):
        slot = lax.rem(dest_ref[first + j], cap)
        copy = pltpu.make_async_copy(
            pages_ref.at[j, :, pl.ds(start, width)], out_ref.at[slot], sems.at[j]
        )
        copy.start()
        copies.append(copy)
    for copy in copies:
        copy.wait()


def stage(new_pages, page_dest, start, width):
    cap, tokens, _ = new_pages.shape
    return pl.pallas_call(
        functools.partial(stage_kernel, start, width),
        in_specs=[
            pl.BlockSpec(memory_space=pltpu.SMEM),
            pl.BlockSpec(memory_space=pltpu.HBM),
        ],
        out_specs=pl.BlockSpec(memory_space=pl.ANY),
        out_shape=jax.ShapeDtypeStruct((cap, tokens, width), new_pages.dtype),
        scratch_shapes=[pltpu.SemaphoreType.DMA((cap,))],
        cost_estimate=pl.CostEstimate(
            flops=0, bytes_accessed=4 * cap * tokens * width, transcendentals=0
        ),
    )(page_dest, new_pages)


def nt_dot(a, b):
    return lax.dot_general(a, b, (((1,), (1,)), ((), ())), preferred_element_type=jnp.float32)


def rows(ref, start, width):
    return ref[:, :, start : start + width].reshape(ref.shape[0] * ref.shape[1], width)


def softmax_parts(q, k_res, k_late, bias_ref):
    n_res = k_res.shape[0]
    early = nt_dot(q, k_res) + bias_ref[:, :n_res]
    late = nt_dot(q, k_late) + bias_ref[:, n_res:]
    peak = jnp.maximum(
        jnp.max(early, axis=1, keepdims=True), jnp.max(late, axis=1, keepdims=True)
    )
    early = jnp.exp(early - peak)
    late = jnp.exp(late - peak)
    total = jnp.sum(early, axis=1, keepdims=True) + jnp.sum(late, axis=1, keepdims=True)
    return early.astype(jnp.bfloat16), late.astype(jnp.bfloat16), total


def dot(a, b):
    return jnp.dot(a, b, preferred_element_type=jnp.float32)


def head_kernel(start, q_ref, bias_ref, res_ref, late_ref, *rest):
    arrived_ref, context_ref, sem = rest[-3:]
    width = late_ref.shape[2]
    d = q_ref.shape[1]
    copy = pltpu.make_async_copy(late_ref, arrived_ref.at[:, :, pl.ds(start, width)], sem)
    copy.start()
    early, late, total = softmax_parts(
        q_ref[...], rows(res_ref, 0, d), rows(late_ref, 0, d), bias_ref
    )
    summed = dot(early, rows(res_ref, d, d)) + dot(late, rows(late_ref, d, d))
    context_ref[...] = (summed / total).astype(context_ref.dtype)
    copy.wait()


def keys_kernel(start, q_ref, bias_ref, res_ref, late_ref, *rest):
    arrived_ref, weights_ref, summed_ref, total_ref, sem = rest[-5:]
    width = late_ref.shape[2]
    d = q_ref.shape[1]
    copy = pltpu.make_async_copy(late_ref, arrived_ref.at[:, :, pl.ds(start, width)], sem)
    copy.start()
    early, late, total = softmax_parts(
        q_ref[...], rows(res_ref, 0, d), rows(late_ref, 0, d), bias_ref
    )
    weights_ref[...] = late
    summed_ref[...] = dot(early, rows(res_ref, d, d))
    total_ref[...] = jnp.broadcast_to(total, total_ref.shape)
    copy.wait()


def values_kernel(start, weights_ref, summed_ref, total_ref, late_ref, *rest):
    arrived_ref, context_ref, sem = rest[-3:]
    width = late_ref.shape[2]
    copy = pltpu.make_async_copy(late_ref, arrived_ref.at[:, :, pl.ds(start, width)], sem)
    copy.start()
    summed = summed_ref[...] + dot(weights_ref[...], rows(late_ref, 0, width))
    context_ref[...] = (summed / total_ref[...]).astype(context_ref.dtype)
    copy.wait()


def whole(array):
    return pl.BlockSpec(array.shape, lambda i: (0,) * array.ndim)


def call(kernel, head, heads, operands, specs, arrived, extra, carried, d):
    late = operands[3]
    pages, tokens, _ = late.shape
    requests = operands[0].shape[0]
    in_hbm = pl.BlockSpec(memory_space=pl.ANY)
    out_shape = [jax.ShapeDtypeStruct((pages, tokens, 2 * heads * d), late.dtype)]
    out_specs = [pl.BlockSpec(memory_space=pltpu.HBM)]
    operands, specs, aliases = list(operands), list(specs), {}
    if arrived is not None:
        aliases[len(operands)] = 0
        operands.append(arrived)
        specs.append(pl.BlockSpec(memory_space=pltpu.HBM))
    if extra:
        out_shape += extra
        out_specs += [pl.BlockSpec(e.shape, lambda i: (0, 0)) for e in extra]
    else:
        if carried is not None:
            aliases[len(operands)] = 1
            operands.append(carried)
            specs.append(in_hbm)
        out_shape.append(jax.ShapeDtypeStruct((requests, heads * d), jnp.bfloat16))
        out_specs.append(pl.BlockSpec((requests, d), lambda i: (0, head)))
    tokens_seen = pages * tokens
    return pl.pallas_call(
        kernel,
        grid=(1,),
        in_specs=specs,
        out_specs=out_specs,
        out_shape=out_shape,
        scratch_shapes=[pltpu.SemaphoreType.DMA],
        input_output_aliases=aliases,
        compiler_params=pltpu.CompilerParams(vmem_limit_bytes=VMEM_LIMIT),
        cost_estimate=pl.CostEstimate(
            flops=8 * requests * tokens_seen * d,
            bytes_accessed=12 * tokens_seen * d,
            transcendentals=2 * requests * tokens_seen,
        ),
    )(*operands)


def attend(chunks, resident, queries, bias):
    d = HEAD_DIM
    requests, width = queries.shape
    heads = width // d
    n_res, tokens, _ = resident.shape
    arrived = context = None
    for h, late in enumerate(chunks[: heads]):
        head_specs = [
            pl.BlockSpec((requests, d), lambda i, h=h: (0, h)),
            whole(bias),
            pl.BlockSpec((n_res, tokens, 2 * d), lambda i, h=h: (0, 0, h)),
            whole(late),
        ]
        operands = [queries, bias, resident, late]
        if h < heads - 1:
            arrived, context = call(
                functools.partial(head_kernel, 2 * h * d),
                h, heads, operands, head_specs, arrived, [], context, d,
            )
    last = heads - 1
    tokens_late = late.shape[0] * tokens
    extra = [
        jax.ShapeDtypeStruct((requests, tokens_late), jnp.bfloat16),
        jax.ShapeDtypeStruct((requests, d), jnp.float32),
        jax.ShapeDtypeStruct((requests, d), jnp.float32),
    ]
    arrived, weights, summed, total = call(
        functools.partial(keys_kernel, 2 * last * d),
        last, heads, operands, head_specs, arrived, extra, None, d,
    )
    late = chunks[-1]
    operands = [weights, summed, total, late]
    return call(
        functools.partial(values_kernel, (2 * last + 1) * d),
        last, heads, operands, [whole(x) for x in operands], arrived, [], context, d,
    )


def send(distance, chunks):
    n = lax.axis_size("dp")
    if distance == 0:
        return list(chunks)
    if distance % 2 == 0 or n % 2 or not 2 < distance < n - 2:
        return [route(c, lambda i: i + distance) for c in chunks]
    half = len(chunks) // 2
    swapped = [route(c, lambda i: i ^ 1) for c in chunks[half:]]
    moved = [route(c, lambda i: i + distance + (1 if i % 2 else -1)) for c in chunks[:half]]
    swapped = [route(c, lambda i: i + distance + (-1 if i % 2 else 1)) for c in swapped]
    moved = [route(c, lambda i: i ^ 1) for c in moved]
    return moved + swapped


def offset_digits(n):
    digits = []
    place = 1
    while place < n:
        digits.append((place, min(RADIX, -(-n // place))))
        place *= RADIX
    return digits


def local(new_pages, page_dest, resident, queries, page_table, cross_len):
    n_groups = lax.axis_size("dp")
    cap, tokens, _ = new_pages.shape
    d = HEAD_DIM
    heads = queries.shape[1] // d
    offset = lax.div(page_dest[0], cap)

    def bias_of(page_table, cross_len):
        slots = jnp.arange(resident.shape[0] + cap, dtype=jnp.int32)
        within = jnp.arange(page_table.shape[1], dtype=jnp.int32)[None, :] < cross_len[:, None]
        member = (page_table[:, :, None] == slots[None, None, :]) & within[:, :, None]
        bias = jnp.where(jnp.any(member, axis=1), 0.0, -jnp.inf).astype(jnp.float32)
        return jnp.repeat(bias, tokens, axis=1)

    blocks = [(2 * h * d, 2 * d) for h in range(heads - 1)]
    blocks += [(2 * (heads - 1) * d, d), ((2 * heads - 1) * d, d)]

    def staged(new_pages, page_dest):
        return [stage(new_pages, page_dest, start, width) for start, width in blocks]

    digits = offset_digits(n_groups)
    last = len(digits) - 1

    def step(distance, place_index, carry, resident, queries, page_table, cross_len):
        chunks = staged(*carry) if place_index == 0 else carry
        chunks = send(distance, chunks)
        if place_index < last:
            return chunks
        return attend(chunks, resident, queries, bias_of(page_table, cross_len))

    carry = (new_pages, page_dest)
    for index, (place, base) in enumerate(digits):
        first = 1 if last == 0 else 0
        carry = lax.switch(
            lax.rem(lax.div(offset, place), base) - first,
            [functools.partial(step, k * place, index) for k in range(first, base)],
            carry, resident, queries, page_table, cross_len,
        )
    return tuple(carry)


def solution(mesh):
    return jax.shard_map(
        local,
        mesh=mesh,
        in_specs=(
            P("dp", None, "tensor"),
            P(),
            P("dp", None, "tensor"),
            P("dp", "tensor"),
            P("dp", None),
            P("dp"),
        ),
        out_specs=(P("dp", None, "tensor"), P("dp", "tensor")),
        check_vma=False,
    )
```

```python
import functools
import math

import jax
import jax.numpy as jnp
from jax import lax
from jax.experimental import pallas as pl
from jax.experimental.pallas import tpu as pltpu
from jax.sharding import PartitionSpec as P

HEAD_DIM = 256
RADIX = 8
VMEM_LIMIT = 24 * 1024 * 1024


def route(block, step_of):
    n = lax.axis_size("dp")
    return lax.ppermute(block, "dp", [(i, step_of(i) % n) for i in range(n)])


def stage_kernel(start, width, dest_ref, pages_ref, out_ref, sems):
    cap = pages_ref.shape[0]
    first = lax.axis_index("dp") * cap
    copies = []
    for j in range(cap):
        slot = lax.rem(dest_ref[first + j], cap)
        copy = pltpu.make_async_copy(
            pages_ref.at[j, :, pl.ds(start, width)], out_ref.at[slot], sems.at[j]
        )
        copy.start()
        copies.append(copy)
    for copy in copies:
        copy.wait()


def stage(new_pages, page_dest, start, width):
    cap, tokens, _ = new_pages.shape
    return pl.pallas_call(
        functools.partial(stage_kernel, start, width),
        in_specs=[
            pl.BlockSpec(memory_space=pltpu.SMEM),
            pl.BlockSpec(memory_space=pltpu.HBM),
        ],
        out_specs=pl.BlockSpec(memory_space=pltpu.VMEM),
        out_shape=jax.ShapeDtypeStruct((cap, tokens, width), new_pages.dtype),
        scratch_shapes=[pltpu.SemaphoreType.DMA((cap,))],
        compiler_params=pltpu.CompilerParams(vmem_limit_bytes=VMEM_LIMIT),
        cost_estimate=pl.CostEstimate(
            flops=0, bytes_accessed=4 * cap * tokens * width, transcendentals=0
        ),
    )(page_dest, new_pages)


def nt_dot(a, b):
    return lax.dot_general(a, b, (((1,), (1,)), ((), ())), preferred_element_type=jnp.float32)


def rows(ref, start, width):
    return ref[:, :, start : start + width].reshape(ref.shape[0] * ref.shape[1], width)


def softmax_parts(q, k_res, k_late, bias_ref):
    n_res = k_res.shape[0]
    early = nt_dot(q, k_res) + bias_ref[:, :n_res]
    late = nt_dot(q, k_late) + bias_ref[:, n_res:]
    peak = jnp.maximum(
        jnp.max(early, axis=1, keepdims=True), jnp.max(late, axis=1, keepdims=True)
    )
    early = jnp.exp(early - peak)
    late = jnp.exp(late - peak)
    total = jnp.sum(early, axis=1, keepdims=True) + jnp.sum(late, axis=1, keepdims=True)
    return early.astype(jnp.bfloat16), late.astype(jnp.bfloat16), total


def dot(a, b):
    return jnp.dot(a, b, preferred_element_type=jnp.float32)


def head_kernel(start, q_ref, bias_ref, res_ref, late_ref, *rest):
    arrived_ref, context_ref, sem = rest[-3:]
    width = late_ref.shape[2]
    d = q_ref.shape[1]
    copy = pltpu.make_async_copy(late_ref, arrived_ref.at[:, :, pl.ds(start, width)], sem)
    copy.start()
    early, late, total = softmax_parts(
        q_ref[...], rows(res_ref, 0, d), rows(late_ref, 0, d), bias_ref
    )
    summed = dot(early, rows(res_ref, d, d)) + dot(late, rows(late_ref, d, d))
    context_ref[...] = (summed / total).astype(context_ref.dtype)
    copy.wait()


def keys_kernel(start, q_ref, bias_ref, res_ref, late_ref, *rest):
    arrived_ref, weights_ref, summed_ref, total_ref, sem = rest[-5:]
    width = late_ref.shape[2]
    d = q_ref.shape[1]
    copy = pltpu.make_async_copy(late_ref, arrived_ref.at[:, :, pl.ds(start, width)], sem)
    copy.start()
    early, late, total = softmax_parts(
        q_ref[...], rows(res_ref, 0, d), rows(late_ref, 0, d), bias_ref
    )
    weights_ref[...] = late
    summed_ref[...] = dot(early, rows(res_ref, d, d))
    total_ref[...] = jnp.broadcast_to(total, total_ref.shape)
    copy.wait()


def values_kernel(start, weights_ref, summed_ref, total_ref, late_ref, *rest):
    arrived_ref, context_ref, sem, held, in_sems, out_sems = rest[-6:]
    pages, tokens, width = late_ref.shape
    parts = in_sems.shape[0]
    size = pages // parts

    def part(ref, i):
        return ref.at[pl.ds(i * size, size)]

    def copy_in(i):
        return pltpu.make_async_copy(part(late_ref, i), part(held, i), in_sems.at[i])

    def copy_out(i):
        target = part(arrived_ref, i).at[:, :, pl.ds(start, width)]
        return pltpu.make_async_copy(part(held, i), target, out_sems.at[i])

    for i in range(parts):
        copy_in(i).start()
    summed = summed_ref[...]
    span = size * tokens
    for i in range(parts):
        copy_in(i).wait()
        copy_out(i).start()
        block = held[i * size : (i + 1) * size].reshape(span, width)
        summed += dot(weights_ref[:, i * span : (i + 1) * span], block)
    context_ref[...] = (summed / total_ref[...]).astype(context_ref.dtype)
    for i in range(parts):
        copy_out(i).wait()


def whole(array):
    return pl.BlockSpec(array.shape, lambda i: (0,) * array.ndim)


def call(kernel, head, heads, operands, specs, arrived, extra, carried, d, scratch=()):
    late = operands[3]
    pages, tokens, _ = late.shape
    requests = operands[0].shape[0]
    in_hbm = pl.BlockSpec(memory_space=pl.ANY)
    out_shape = [jax.ShapeDtypeStruct((pages, tokens, 2 * heads * d), late.dtype)]
    out_specs = [pl.BlockSpec(memory_space=pltpu.HBM)]
    operands, specs, aliases = list(operands), list(specs), {}
    if arrived is not None:
        aliases[len(operands)] = 0
        operands.append(arrived)
        specs.append(pl.BlockSpec(memory_space=pltpu.HBM))
    if extra:
        out_shape += extra
        out_specs += [pl.BlockSpec(e.shape, lambda i: (0, 0)) for e in extra]
    else:
        if carried is not None:
            aliases[len(operands)] = 1
            operands.append(carried)
            specs.append(in_hbm)
        out_shape.append(jax.ShapeDtypeStruct((requests, heads * d), jnp.bfloat16))
        out_specs.append(pl.BlockSpec((requests, d), lambda i: (0, head)))
    tokens_seen = pages * tokens
    return pl.pallas_call(
        kernel,
        grid=(1,),
        in_specs=specs,
        out_specs=out_specs,
        out_shape=out_shape,
        scratch_shapes=[pltpu.SemaphoreType.DMA, *scratch],
        input_output_aliases=aliases,
        compiler_params=pltpu.CompilerParams(vmem_limit_bytes=VMEM_LIMIT),
        cost_estimate=pl.CostEstimate(
            flops=8 * requests * tokens_seen * d,
            bytes_accessed=12 * tokens_seen * d,
            transcendentals=2 * requests * tokens_seen,
        ),
    )(*operands)


def attend(chunks, resident, queries, bias):
    d = HEAD_DIM
    requests, width = queries.shape
    heads = width // d
    n_res, tokens, _ = resident.shape
    arrived = context = None
    for h, late in enumerate(chunks[: heads]):
        head_specs = [
            pl.BlockSpec((requests, d), lambda i, h=h: (0, h)),
            whole(bias),
            pl.BlockSpec((n_res, tokens, 2 * d), lambda i, h=h: (0, 0, h)),
            whole(late),
        ]
        operands = [queries, bias, resident, late]
        if h < heads - 1:
            arrived, context = call(
                functools.partial(head_kernel, 2 * h * d),
                h, heads, operands, head_specs, arrived, [], context, d,
            )
    last = heads - 1
    tokens_late = late.shape[0] * tokens
    extra = [
        jax.ShapeDtypeStruct((requests, tokens_late), jnp.bfloat16),
        jax.ShapeDtypeStruct((requests, d), jnp.float32),
        jax.ShapeDtypeStruct((requests, d), jnp.float32),
    ]
    arrived, weights, summed, total = call(
        functools.partial(keys_kernel, 2 * last * d),
        last, heads, operands, head_specs, arrived, extra, None, d,
    )
    late = chunks[-1]
    operands = [weights, summed, total, late]
    specs = [whole(weights), whole(summed), whole(total), pl.BlockSpec(memory_space=pl.ANY)]
    parts = late.shape[0] // math.gcd(late.shape[0], 2)
    sems = pltpu.SemaphoreType.DMA((parts,))
    return call(
        functools.partial(values_kernel, (2 * last + 1) * d),
        last, heads, operands, specs, arrived, [], context, d,
        [pltpu.VMEM(late.shape, late.dtype), sems, sems],
    )


def send(distance, chunks):
    n = lax.axis_size("dp")
    if distance == 0:
        return list(chunks)
    if distance % 2 == 0 or n % 2 or not 2 < distance < n - 2:
        return [route(c, lambda i: i + distance) for c in chunks]
    half = len(chunks) // 2
    swapped = [route(c, lambda i: i ^ 1) for c in chunks[half:]]
    moved = [route(c, lambda i: i + distance + (1 if i % 2 else -1)) for c in chunks[:half]]
    swapped = [route(c, lambda i: i + distance + (-1 if i % 2 else 1)) for c in swapped]
    moved = [route(c, lambda i: i ^ 1) for c in moved]
    return moved + swapped


def offset_digits(n):
    digits = []
    place = 1
    while place < n:
        digits.append((place, min(RADIX, -(-n // place))))
        place *= RADIX
    return digits


def local(new_pages, page_dest, resident, queries, page_table, cross_len):
    n_groups = lax.axis_size("dp")
    cap, tokens, _ = new_pages.shape
    d = HEAD_DIM
    heads = queries.shape[1] // d
    offset = lax.div(page_dest[0], cap)

    def bias_of(page_table, cross_len):
        slots = jnp.arange(resident.shape[0] + cap, dtype=jnp.int32)
        within = jnp.arange(page_table.shape[1], dtype=jnp.int32)[None, :] < cross_len[:, None]
        member = (page_table[:, :, None] == slots[None, None, :]) & within[:, :, None]
        bias = jnp.where(jnp.any(member, axis=1), 0.0, -jnp.inf).astype(jnp.float32)
        return jnp.repeat(bias, tokens, axis=1)

    blocks = [(2 * h * d, 2 * d) for h in range(heads - 1)]
    blocks += [(2 * (heads - 1) * d, d), ((2 * heads - 1) * d, d)]

    def staged(new_pages, page_dest):
        return [stage(new_pages, page_dest, start, width) for start, width in blocks]

    digits = offset_digits(n_groups)
    last = len(digits) - 1

    def step(distance, place_index, carry, resident, queries, page_table, cross_len):
        chunks = staged(*carry) if place_index == 0 else carry
        chunks = send(distance, chunks)
        if place_index < last:
            return chunks
        return attend(chunks, resident, queries, bias_of(page_table, cross_len))

    carry = (new_pages, page_dest)
    for index, (place, base) in enumerate(digits):
        first = 1 if last == 0 else 0
        carry = lax.switch(
            lax.rem(lax.div(offset, place), base) - first,
            [functools.partial(step, k * place, index) for k in range(first, base)],
            carry, resident, queries, page_table, cross_len,
        )
    return tuple(carry)


def solution(mesh):
    return jax.shard_map(
        local,
        mesh=mesh,
        in_specs=(
            P("dp", None, "tensor"),
            P(),
            P("dp", None, "tensor"),
            P("dp", "tensor"),
            P("dp", None),
            P("dp"),
        ),
        out_specs=(P("dp", None, "tensor"), P("dp", "tensor")),
        check_vma=False,
    )
```

```python
import functools
import math

import jax
import jax.numpy as jnp
from jax import lax
from jax.experimental import pallas as pl
from jax.experimental.pallas import tpu as pltpu
from jax.sharding import PartitionSpec as P

HEAD_DIM = 256
RADIX = 8
VMEM_LIMIT = 12 * 1024 * 1024


def route(block, step_of):
    n = lax.axis_size("dp")
    return lax.ppermute(block, "dp", [(i, step_of(i) % n) for i in range(n)])


def stage_kernel(starts, dest_ref, pages_ref, *rest):
    out_refs, sems = rest[:-1], rest[-1]
    cap = pages_ref.shape[0]
    first = lax.axis_index("dp") * cap
    copies = []
    for j in range(cap):
        slot = lax.rem(dest_ref[first + j], cap)
        for k, (start, out_ref) in enumerate(zip(starts, out_refs)):
            copy = pltpu.make_async_copy(
                pages_ref.at[j, :, pl.ds(start, out_ref.shape[2])],
                out_ref.at[slot],
                sems.at[k, j],
            )
            copy.start()
            copies.append(copy)
    for copy in copies:
        copy.wait()


def stage(new_pages, page_dest, blocks):
    cap, tokens, _ = new_pages.shape
    return pl.pallas_call(
        functools.partial(stage_kernel, [start for start, _ in blocks]),
        in_specs=[
            pl.BlockSpec(memory_space=pltpu.SMEM),
            pl.BlockSpec(memory_space=pl.ANY),
        ],
        out_specs=[pl.BlockSpec(memory_space=pltpu.VMEM) for _ in blocks],
        out_shape=[
            jax.ShapeDtypeStruct((cap, tokens, width), new_pages.dtype) for _, width in blocks
        ],
        scratch_shapes=[pltpu.SemaphoreType.DMA((len(blocks), cap))],
        cost_estimate=pl.CostEstimate(
            flops=0,
            bytes_accessed=4 * cap * tokens * sum(width for _, width in blocks),
            transcendentals=0,
        ),
    )(page_dest, new_pages)


def nt_dot(a, b):
    return lax.dot_general(a, b, (((1,), (1,)), ((), ())), preferred_element_type=jnp.float32)


def rows(ref, start, width):
    return ref[:, :, start : start + width].reshape(ref.shape[0] * ref.shape[1], width)


def softmax_parts(q, k_res, k_late, bias_ref):
    n_res = k_res.shape[0]
    early = nt_dot(q, k_res) + bias_ref[:, :n_res]
    late = nt_dot(q, k_late) + bias_ref[:, n_res:]
    peak = jnp.maximum(
        jnp.max(early, axis=1, keepdims=True), jnp.max(late, axis=1, keepdims=True)
    )
    early = jnp.exp(early - peak)
    late = jnp.exp(late - peak)
    total = jnp.sum(early, axis=1, keepdims=True) + jnp.sum(late, axis=1, keepdims=True)
    return early.astype(jnp.bfloat16), late.astype(jnp.bfloat16), total


def dot(a, b):
    return jnp.dot(a, b, preferred_element_type=jnp.float32)


def head_kernel(start, q_ref, bias_ref, res_ref, late_ref, *rest):
    arrived_ref, context_ref, sem = rest[-3:]
    width = late_ref.shape[2]
    d = q_ref.shape[1]
    copy = pltpu.make_async_copy(late_ref, arrived_ref.at[:, :, pl.ds(start, width)], sem)
    copy.start()
    early, late, total = softmax_parts(
        q_ref[...], rows(res_ref, 0, d), rows(late_ref, 0, d), bias_ref
    )
    summed = dot(early, rows(res_ref, d, d)) + dot(late, rows(late_ref, d, d))
    context_ref[...] = (summed / total).astype(context_ref.dtype)
    copy.wait()


def keys_kernel(start, q_ref, bias_ref, res_ref, late_ref, *rest):
    arrived_ref, weights_ref, summed_ref, total_ref, sem = rest[-5:]
    width = late_ref.shape[2]
    d = q_ref.shape[1]
    copy = pltpu.make_async_copy(late_ref, arrived_ref.at[:, :, pl.ds(start, width)], sem)
    copy.start()
    early, late, total = softmax_parts(
        q_ref[...], rows(res_ref, 0, d), rows(late_ref, 0, d), bias_ref
    )
    weights_ref[...] = late
    summed_ref[...] = dot(early, rows(res_ref, d, d))
    total_ref[...] = jnp.broadcast_to(total, total_ref.shape)
    copy.wait()


def values_kernel(start, weights_ref, summed_ref, total_ref, late_ref, *rest):
    arrived_ref, context_ref, sem, held, head, in_sems, out_sems = rest[-7:]
    pages, tokens, width = late_ref.shape
    parts = in_sems.shape[0]
    size = pages // parts

    def part(ref, i):
        return ref.at[pl.ds(i * size, size)]

    def copy_in(i):
        return pltpu.make_async_copy(part(late_ref, i), part(held, i), in_sems.at[i])

    def copy_out(i):
        target = part(arrived_ref, i).at[:, :, pl.ds(start, width)]
        return pltpu.make_async_copy(part(held, i), target, out_sems.at[i])

    for i in range(parts):
        copy_in(i).start()
    summed = summed_ref[...]
    span = size * tokens
    for i in range(parts):
        copy_in(i).wait()
        copy_out(i).start()
        block = held[i * size : (i + 1) * size].reshape(span, width)
        summed += dot(weights_ref[:, i * span : (i + 1) * span], block)
    head[...] = (summed / total_ref[...]).astype(head.dtype)
    columns = pl.ds((start - width) // 2, width)
    finish = pltpu.make_async_copy(head, context_ref.at[:, columns], sem)
    finish.start()
    for i in range(parts):
        copy_out(i).wait()
    finish.wait()


def whole(array):
    return pl.BlockSpec(array.shape, lambda i: (0,) * array.ndim)


def call(kernel, head, heads, operands, specs, arrived, extra, carried, d):
    late = operands[3]
    pages, tokens, _ = late.shape
    requests = operands[0].shape[0]
    in_hbm = pl.BlockSpec(memory_space=pl.ANY)
    out_shape = [jax.ShapeDtypeStruct((pages, tokens, 2 * heads * d), late.dtype)]
    out_specs = [pl.BlockSpec(memory_space=pltpu.HBM)]
    operands, specs, aliases = list(operands), list(specs), {}
    if arrived is not None:
        aliases[len(operands)] = 0
        operands.append(arrived)
        specs.append(pl.BlockSpec(memory_space=pltpu.HBM))
    if extra:
        out_shape += extra
        out_specs += [pl.BlockSpec(e.shape, lambda i: (0, 0)) for e in extra]
    else:
        if carried is not None:
            aliases[len(operands)] = 1
            operands.append(carried)
            specs.append(in_hbm)
        out_shape.append(jax.ShapeDtypeStruct((requests, heads * d), jnp.bfloat16))
        out_specs.append(pl.BlockSpec((requests, d), lambda i: (0, head)))
    tokens_seen = pages * tokens
    return pl.pallas_call(
        kernel,
        grid=(1,),
        in_specs=specs,
        out_specs=out_specs,
        out_shape=out_shape,
        scratch_shapes=[pltpu.SemaphoreType.DMA],
        input_output_aliases=aliases,
        compiler_params=pltpu.CompilerParams(vmem_limit_bytes=VMEM_LIMIT),
        cost_estimate=pl.CostEstimate(
            flops=8 * requests * tokens_seen * d,
            bytes_accessed=12 * tokens_seen * d,
            transcendentals=2 * requests * tokens_seen,
        ),
    )(*operands)


def attend(chunks, resident, queries, bias):
    d = HEAD_DIM
    requests, width = queries.shape
    heads = width // d
    n_res, tokens, _ = resident.shape
    arrived = context = None
    for h, late in enumerate(chunks[: heads]):
        head_specs = [
            pl.BlockSpec((requests, d), lambda i, h=h: (0, h)),
            whole(bias),
            pl.BlockSpec((n_res, tokens, 2 * d), lambda i, h=h: (0, 0, h)),
            whole(late),
        ]
        operands = [queries, bias, resident, late]
        if h < heads - 1:
            arrived, context = call(
                functools.partial(head_kernel, 2 * h * d),
                h, heads, operands, head_specs, arrived, [], context, d,
            )
    last = heads - 1
    tokens_late = late.shape[0] * tokens
    extra = [
        jax.ShapeDtypeStruct((requests, tokens_late), jnp.bfloat16),
        jax.ShapeDtypeStruct((requests, d), jnp.float32),
        jax.ShapeDtypeStruct((requests, d), jnp.float32),
    ]
    arrived, weights, summed, total = call(
        functools.partial(keys_kernel, 2 * last * d),
        last, heads, operands, head_specs, arrived, extra, None, d,
    )
    late = chunks[-1]
    parts = late.shape[0] // math.gcd(late.shape[0], 2)
    sems = pltpu.SemaphoreType.DMA((parts,))
    in_vmem = pl.BlockSpec(memory_space=pltpu.VMEM)
    anywhere = pl.BlockSpec(memory_space=pl.ANY)
    in_hbm = pl.BlockSpec(memory_space=pltpu.HBM)
    return pl.pallas_call(
        functools.partial(values_kernel, (2 * last + 1) * d),
        in_specs=[in_vmem, in_vmem, in_vmem, anywhere, in_hbm, in_hbm],
        out_specs=[in_hbm, in_hbm],
        out_shape=[jax.ShapeDtypeStruct(x.shape, x.dtype) for x in (arrived, context)],
        scratch_shapes=[
            pltpu.SemaphoreType.DMA,
            pltpu.VMEM(late.shape, late.dtype),
            pltpu.VMEM((requests, d), context.dtype),
            sems,
            sems,
        ],
        input_output_aliases={4: 0, 5: 1},
        compiler_params=pltpu.CompilerParams(vmem_limit_bytes=VMEM_LIMIT),
        cost_estimate=pl.CostEstimate(
            flops=2 * requests * tokens_late * d,
            bytes_accessed=4 * tokens_late * d,
            transcendentals=0,
        ),
    )(weights, summed, total, late, arrived, context)


def send(distance, chunks):
    n = lax.axis_size("dp")
    if distance == 0:
        return list(chunks)
    if distance % 2 == 0 or n % 2 or not 2 < distance < n - 2:
        return [route(c, lambda i: i + distance) for c in chunks]
    pairs = n // 2
    far, near = (distance + 1) // 2, (distance - 1) // 2
    odd_is_far = min(far, pairs - far) > min(near, pairs - near)
    far_side = 1 if odd_is_far else 0
    rest = distance + 1 if odd_is_far else distance - 1
    direct = [route(c, lambda i: i + distance) for c in chunks[:-2]]
    halfway = [
        route(c, lambda i: i ^ 1 if i % 2 == far_side else i + distance) for c in chunks[-2:]
    ]
    direct[0], *halfway = lax.optimization_barrier((direct[0], *halfway))
    return direct + [route(c, lambda i: i if i % 2 == far_side else i + rest) for c in halfway]


def offset_digits(n):
    digits = []
    place = 1
    while place < n:
        digits.append((place, min(RADIX, -(-n // place))))
        place *= RADIX
    return digits


def local(new_pages, page_dest, resident, queries, page_table, cross_len):
    n_groups = lax.axis_size("dp")
    cap, tokens, _ = new_pages.shape
    d = HEAD_DIM
    heads = queries.shape[1] // d
    offset = lax.div(page_dest[0], cap)

    def bias_of(page_table, cross_len):
        slots = jnp.arange(resident.shape[0] + cap, dtype=jnp.int32)
        within = jnp.arange(page_table.shape[1], dtype=jnp.int32)[None, :] < cross_len[:, None]
        member = (page_table[:, :, None] == slots[None, None, :]) & within[:, :, None]
        bias = jnp.where(jnp.any(member, axis=1), 0.0, -jnp.inf).astype(jnp.float32)
        return jnp.repeat(bias, tokens, axis=1)

    blocks = [(2 * h * d, 2 * d) for h in range(heads - 1)]
    blocks += [(2 * (heads - 1) * d, d), ((2 * heads - 1) * d, d)]

    def staged(new_pages, page_dest):
        first = stage(new_pages, page_dest, blocks[:1])
        return [*first, *stage(new_pages, page_dest, blocks[1:])]

    digits = offset_digits(n_groups)
    last = len(digits) - 1

    def step(distance, place_index, carry, resident, queries, page_table, cross_len):
        chunks = staged(*carry) if place_index == 0 else carry
        chunks = send(distance, chunks)
        if place_index < last:
            return chunks
        return attend(chunks, resident, queries, bias_of(page_table, cross_len))

    carry = (new_pages, page_dest)
    for index, (place, base) in enumerate(digits):
        first = 1 if last == 0 else 0
        carry = lax.switch(
            lax.rem(lax.div(offset, place), base) - first,
            [functools.partial(step, k * place, index) for k in range(first, base)],
            carry, resident, queries, page_table, cross_len,
        )
    return tuple(carry)


def solution(mesh):
    return jax.shard_map(
        local,
        mesh=mesh,
        in_specs=(
            P("dp", None, "tensor"),
            P(),
            P("dp", None, "tensor"),
            P("dp", "tensor"),
            P("dp", None),
            P("dp"),
        ),
        out_specs=(P("dp", None, "tensor"), P("dp", "tensor")),
        check_vma=False,
    )
```

```python
import functools
import math

import jax
import jax.numpy as jnp
from jax import lax
from jax.experimental import pallas as pl
from jax.experimental.pallas import tpu as pltpu
from jax.sharding import PartitionSpec as P

HEAD_DIM = 256
RADIX = 8
VMEM_LIMIT = 8 * 1024 * 1024
GROUP = 2


def route(block, step_of):
    n = lax.axis_size("dp")
    return lax.ppermute(block, "dp", [(i, step_of(i) % n) for i in range(n)])


def stage_kernel(starts, dest_ref, pages_ref, *rest):
    out_refs, sems = rest[:-1], rest[-1]
    cap = pages_ref.shape[0]
    first = lax.axis_index("dp") * cap
    copies = []
    for j in range(cap):
        slot = lax.rem(dest_ref[first + j], cap)
        for k, (start, out_ref) in enumerate(zip(starts, out_refs)):
            copy = pltpu.make_async_copy(
                pages_ref.at[j, :, pl.ds(start, out_ref.shape[2])],
                out_ref.at[slot],
                sems.at[k, j],
            )
            copy.start()
            copies.append(copy)
    for copy in copies:
        copy.wait()


def stage(new_pages, page_dest, blocks):
    cap, tokens, _ = new_pages.shape
    return pl.pallas_call(
        functools.partial(stage_kernel, [start for start, _ in blocks]),
        in_specs=[
            pl.BlockSpec(memory_space=pltpu.SMEM),
            pl.BlockSpec(memory_space=pl.ANY),
        ],
        out_specs=[pl.BlockSpec(memory_space=pltpu.VMEM) for _ in blocks],
        out_shape=[
            jax.ShapeDtypeStruct((cap, tokens, width), new_pages.dtype) for _, width in blocks
        ],
        scratch_shapes=[pltpu.SemaphoreType.DMA((len(blocks), cap))],
        cost_estimate=pl.CostEstimate(
            flops=0,
            bytes_accessed=4 * cap * tokens * sum(width for _, width in blocks),
            transcendentals=0,
        ),
    )(page_dest, new_pages)


def nt_dot(a, b):
    return lax.dot_general(a, b, (((1,), (1,)), ((), ())), preferred_element_type=jnp.float32)


def dot(a, b):
    return jnp.dot(a, b, preferred_element_type=jnp.float32)


def page_rows(ref, first, pages, start, width):
    block = ref[pl.ds(first, pages), :, start : start + width]
    return block.reshape(pages * ref.shape[1], width)


def weigh(q_ref, bias_ref, scores_ref, sources):
    d = q_ref.shape[1]
    for ref, start, at in sources:
        pages, tokens, _ = ref.shape
        group = math.gcd(pages, GROUP)

        def score(i, _, ref=ref, start=start, at=at, group=group, tokens=tokens):
            width = group * tokens
            columns = pl.ds(pl.multiple_of((at + i * group) * tokens, width), width)
            keys = page_rows(ref, i * group, group, start, d)
            scores_ref[:, columns] = nt_dot(q_ref[...], keys) + bias_ref[:, columns]
            return 0

        lax.fori_loop(0, pages // group, score, 0)
    scores = scores_ref[...]
    prob = jnp.exp(scores - jnp.max(scores, axis=1, keepdims=True))
    scores_ref[...] = prob
    return jnp.sum(prob, axis=1, keepdims=True)


def gather_values(weights_ref, sources, d):
    summed = jnp.zeros((weights_ref.shape[0], d), jnp.float32)
    for ref, start, at in sources:
        pages, tokens, _ = ref.shape
        group = math.gcd(pages, GROUP)

        def add(i, summed, ref=ref, start=start, at=at, group=group, tokens=tokens):
            width = group * tokens
            columns = pl.ds(pl.multiple_of((at + i * group) * tokens, width), width)
            weights = weights_ref[:, columns].astype(jnp.bfloat16)
            return summed + dot(weights, page_rows(ref, i * group, group, start, d))

        summed = lax.fori_loop(0, pages // group, add, summed)
    return summed


def first_kernel(
    cap, slots_ref, q_ref, bias_ref, res_ref, keys_ref, values_ref,
    arrived_ref, context_ref, scores_ref, sems,
):
    d = q_ref.shape[1]
    n_res = res_ref.shape[0]
    copies = []
    for k, ref in enumerate((keys_ref, values_ref)):
        for j in range(cap):
            target = arrived_ref.at[slots_ref[j], :, pl.ds(k * d, d)]
            copies.append(pltpu.make_async_copy(ref.at[j], target, sems.at[k, j]))
            copies[-1].start()
    total = weigh(q_ref, bias_ref, scores_ref, [(res_ref, 0, 0), (keys_ref, 0, n_res)])
    summed = gather_values(scores_ref, [(res_ref, d, 0), (values_ref, 0, n_res)], d)
    context_ref[...] = (summed / total).astype(context_ref.dtype)
    for copy in copies:
        copy.wait()


def head_kernel(
    start, q_ref, bias_ref, res_ref, late_ref, _, _too,
    arrived_ref, context_ref, scores_ref, sem,
):
    width = late_ref.shape[2]
    d = q_ref.shape[1]
    n_res = res_ref.shape[0]
    copy = pltpu.make_async_copy(late_ref, arrived_ref.at[:, :, pl.ds(start, width)], sem)
    copy.start()
    total = weigh(q_ref, bias_ref, scores_ref, [(res_ref, 0, 0), (late_ref, 0, n_res)])
    summed = gather_values(scores_ref, [(res_ref, d, 0), (late_ref, d, n_res)], d)
    context_ref[...] = (summed / total).astype(context_ref.dtype)
    copy.wait()


def keys_kernel(
    start, q_ref, bias_ref, res_ref, late_ref, _,
    arrived_ref, weights_ref, summed_ref, total_ref, scores_ref, sem,
):
    width = late_ref.shape[2]
    d = q_ref.shape[1]
    n_res, tokens, _ = res_ref.shape
    copy = pltpu.make_async_copy(late_ref, arrived_ref.at[:, :, pl.ds(start, width)], sem)
    copy.start()
    total = weigh(q_ref, bias_ref, scores_ref, [(res_ref, 0, 0), (late_ref, 0, n_res)])
    weights_ref[...] = scores_ref[:, n_res * tokens :].astype(weights_ref.dtype)
    summed_ref[...] = gather_values(scores_ref, [(res_ref, d, 0)], d)
    total_ref[...] = jnp.broadcast_to(total, total_ref.shape)
    copy.wait()


def values_kernel(start, weights_ref, summed_ref, total_ref, late_ref, *rest):
    arrived_ref, context_ref, sem, held, head, in_sems, out_sems = rest[-7:]
    pages, tokens, width = late_ref.shape
    parts = in_sems.shape[0]
    size = pages // parts

    def part(ref, i):
        return ref.at[pl.ds(i * size, size)]

    def copy_in(i):
        return pltpu.make_async_copy(part(late_ref, i), part(held, i), in_sems.at[i])

    def copy_out(i):
        target = part(arrived_ref, i).at[:, :, pl.ds(start, width)]
        return pltpu.make_async_copy(part(held, i), target, out_sems.at[i])

    for i in range(parts):
        copy_in(i).start()
    summed = summed_ref[...]
    span = size * tokens
    for i in range(parts):
        copy_in(i).wait()
        copy_out(i).start()
        block = held[i * size : (i + 1) * size].reshape(span, width)
        summed += dot(weights_ref[:, i * span : (i + 1) * span], block)
    head[...] = (summed / total_ref[...]).astype(head.dtype)
    columns = pl.ds((start - width) // 2, width)
    finish = pltpu.make_async_copy(head, context_ref.at[:, columns], sem)
    finish.start()
    for i in range(parts):
        copy_out(i).wait()
    finish.wait()


def whole(array):
    return pl.BlockSpec(array.shape, lambda i: (0,) * array.ndim)


def attend(chunks, resident, queries, first_bias, bias, slots):
    d = HEAD_DIM
    requests, width = queries.shape
    heads = width // d
    last = heads - 1
    n_res, tokens, _ = resident.shape
    cap = chunks[0].shape[0]
    pool = (n_res + cap) * tokens
    in_hbm = pl.BlockSpec(memory_space=pltpu.HBM)
    in_vmem = pl.BlockSpec(memory_space=pltpu.VMEM)
    anywhere = pl.BlockSpec(memory_space=pl.ANY)
    arrived_shape = jax.ShapeDtypeStruct((cap, tokens, 2 * width), resident.dtype)
    context_shape = jax.ShapeDtypeStruct((requests, width), jnp.bfloat16)
    scores = pltpu.VMEM((requests, pool), jnp.float32)
    params = pltpu.CompilerParams(vmem_limit_bytes=VMEM_LIMIT)
    cost = pl.CostEstimate(
        flops=4 * requests * pool * d,
        bytes_accessed=6 * pool * d,
        transcendentals=requests * pool,
    )

    def head_specs(h):
        return [
            pl.BlockSpec((requests, d), lambda i: (0, h)),
            whole(bias),
            pl.BlockSpec((n_res, tokens, 2 * d), lambda i: (0, 0, h)),
        ]

    arrived, context = pl.pallas_call(
        functools.partial(first_kernel, cap),
        grid=(1,),
        in_specs=[
            pl.BlockSpec(memory_space=pltpu.SMEM),
            *head_specs(0),
            whole(chunks[0]),
            whole(chunks[1]),
        ],
        out_specs=[in_hbm, pl.BlockSpec((requests, d), lambda i: (0, 0))],
        out_shape=[arrived_shape, context_shape],
        scratch_shapes=[scores, pltpu.SemaphoreType.DMA((2, cap))],
        compiler_params=params,
        cost_estimate=cost,
    )(slots, queries, first_bias, resident, chunks[0], chunks[1])
    for h, late in enumerate(chunks[2:-2], 1):
        arrived, context = pl.pallas_call(
            functools.partial(head_kernel, 2 * h * d),
            grid=(1,),
            in_specs=[*head_specs(h), whole(late), in_hbm, anywhere],
            out_specs=[in_hbm, pl.BlockSpec((requests, d), lambda i, h=h: (0, h))],
            out_shape=[arrived_shape, context_shape],
            scratch_shapes=[scores, pltpu.SemaphoreType.DMA],
            input_output_aliases={4: 0, 5: 1},
            compiler_params=params,
            cost_estimate=cost,
        )(queries, bias, resident, late, arrived, context)
    parts_shape = [
        jax.ShapeDtypeStruct((requests, cap * tokens), jnp.bfloat16),
        jax.ShapeDtypeStruct((requests, d), jnp.float32),
        jax.ShapeDtypeStruct((requests, d), jnp.float32),
    ]
    late = chunks[-2]
    arrived, *parts = pl.pallas_call(
        functools.partial(keys_kernel, 2 * last * d),
        grid=(1,),
        in_specs=[*head_specs(last), whole(late), in_hbm],
        out_specs=[in_hbm, *(whole(x) for x in parts_shape)],
        out_shape=[arrived_shape, *parts_shape],
        scratch_shapes=[scores, pltpu.SemaphoreType.DMA],
        input_output_aliases={4: 0},
        compiler_params=params,
        cost_estimate=cost,
    )(queries, bias, resident, late, arrived)
    late = chunks[-1]
    n_parts = cap // math.gcd(cap, GROUP)
    sems = pltpu.SemaphoreType.DMA((n_parts,))
    arrived, context = pl.pallas_call(
        functools.partial(values_kernel, (2 * last + 1) * d),
        in_specs=[in_vmem, in_vmem, in_vmem, anywhere, in_hbm, in_hbm],
        out_specs=[in_hbm, in_hbm],
        out_shape=[arrived_shape, context_shape],
        scratch_shapes=[
            pltpu.SemaphoreType.DMA,
            pltpu.VMEM(late.shape, late.dtype),
            pltpu.VMEM((requests, d), context.dtype),
            sems,
            sems,
        ],
        input_output_aliases={4: 0, 5: 1},
        compiler_params=params,
        cost_estimate=pl.CostEstimate(
            flops=2 * requests * cap * tokens * d,
            bytes_accessed=4 * cap * tokens * d,
            transcendentals=0,
        ),
    )(*parts, late, arrived, context)
    return arrived, context


def send(distance, chunks):
    n = lax.axis_size("dp")
    if distance == 0:
        return list(chunks)
    if distance % 2 == 0 or n % 2 or not 2 < distance < n - 2:
        return [route(c, lambda i: i + distance) for c in chunks]
    pairs = n // 2
    far, near = (distance + 1) // 2, (distance - 1) // 2
    odd_is_far = min(far, pairs - far) > min(near, pairs - near)
    far_side = 1 if odd_is_far else 0
    rest = distance + 1 if odd_is_far else distance - 1
    direct = [route(c, lambda i: i + distance) for c in chunks[:-2]]
    halfway = [
        route(c, lambda i: i ^ 1 if i % 2 == far_side else i + distance) for c in chunks[-2:]
    ]
    direct[0], *halfway = lax.optimization_barrier((direct[0], *halfway))
    return direct + [route(c, lambda i: i if i % 2 == far_side else i + rest) for c in halfway]


def offset_digits(n):
    digits = []
    place = 1
    while place < n:
        digits.append((place, min(RADIX, -(-n // place))))
        place *= RADIX
    return digits


def quotient(value, by):
    if by & (by - 1) == 0:
        return lax.shift_right_logical(value, by.bit_length() - 1)
    return lax.div(value, by)


def local(new_pages, page_dest, resident, queries, page_table, cross_len):
    n_groups = lax.axis_size("dp")
    cap, tokens, _ = new_pages.shape
    d = HEAD_DIM
    heads = queries.shape[1] // d
    n_res = resident.shape[0]
    offset = quotient(page_dest[0], cap)

    def bias_of(late_slots, page_table, cross_len):
        slots = jnp.concatenate([jnp.arange(n_res, dtype=jnp.int32), n_res + late_slots])
        within = jnp.arange(page_table.shape[1], dtype=jnp.int32)[None, :] < cross_len[:, None]
        member = (page_table[:, :, None] == slots[None, None, :]) & within[:, :, None]
        bias = jnp.where(jnp.any(member, axis=1), 0.0, -jnp.inf).astype(jnp.float32)
        return jnp.repeat(bias, tokens, axis=1)

    blocks = [(2 * h * d, 2 * d) for h in range(1, heads - 1)]
    blocks += [(2 * (heads - 1) * d, d), ((2 * heads - 1) * d, d)]

    digits = offset_digits(n_groups)
    last = len(digits) - 1

    def step(distance, index, carry, new_pages, page_dest, resident, queries, page_table, cross_len):
        if index == 0:
            carry = [new_pages[:, :, :d], new_pages[:, :, d : 2 * d]]
            carry += stage(new_pages, page_dest, blocks)
        carry = send(distance, carry)
        if index < last:
            return tuple(carry)
        source = lax.rem(lax.axis_index("dp") - quotient(page_dest[0], cap) + n_groups, n_groups)
        slots = lax.rem(lax.dynamic_slice_in_dim(page_dest, source * cap, cap), cap)
        in_order = jnp.arange(cap, dtype=jnp.int32)
        return attend(
            carry,
            resident,
            queries,
            bias_of(slots, page_table, cross_len),
            bias_of(in_order, page_table, cross_len),
            slots,
        )

    carry = ()
    for index, (place, base) in enumerate(digits):
        digit = quotient(offset, place)
        first = 1 if last == 0 else 0
        if index < last:
            digit = lax.rem(digit, base)
        carry = lax.switch(
            digit - first,
            [functools.partial(step, k * place, index) for k in range(first, base)],
            carry, new_pages, page_dest, resident, queries, page_table, cross_len,
        )
    return carry


def solution(mesh):
    return jax.shard_map(
        local,
        mesh=mesh,
        in_specs=(
            P("dp", None, "tensor"),
            P(),
            P("dp", None, "tensor"),
            P("dp", "tensor"),
            P("dp", None),
            P("dp"),
        ),
        out_specs=(P("dp", None, "tensor"), P("dp", "tensor")),
        check_vma=False,
    )
```

```python
import functools
import math

import jax
import jax.numpy as jnp
from jax import lax
from jax.experimental import pallas as pl
from jax.experimental.pallas import tpu as pltpu
from jax.sharding import PartitionSpec as P

HEAD_DIM = 256
RADIX = 8
VMEM_LIMIT = 8 * 1024 * 1024
GROUP = 2


def route(block, step_of):
    n = lax.axis_size("dp")
    return lax.ppermute(block, "dp", [(i, step_of(i) % n) for i in range(n)])


def stage_kernel(start, dest_ref, pages_ref, _, out_ref, sems):
    cap = pages_ref.shape[0]
    first = lax.axis_index("dp") * cap
    copies = []
    for j in range(cap):
        slot = lax.rem(dest_ref[first + j], cap)
        source = pages_ref.at[j, :, pl.ds(start, out_ref.shape[2])]
        copies.append(pltpu.make_async_copy(source, out_ref.at[slot], sems.at[j]))
        copies[-1].start()
    for copy in copies:
        copy.wait()


def stage(new_pages, page_dest, start, width, after):
    cap, tokens, _ = new_pages.shape
    return pl.pallas_call(
        functools.partial(stage_kernel, start),
        in_specs=[
            pl.BlockSpec(memory_space=pltpu.SMEM),
            pl.BlockSpec(memory_space=pl.ANY),
            pl.BlockSpec(memory_space=pl.ANY),
        ],
        out_specs=pl.BlockSpec(memory_space=pltpu.VMEM),
        out_shape=jax.ShapeDtypeStruct((cap, tokens, width), new_pages.dtype),
        scratch_shapes=[pltpu.SemaphoreType.DMA((cap,))],
        cost_estimate=pl.CostEstimate(
            flops=0, bytes_accessed=4 * cap * tokens * width, transcendentals=0
        ),
    )(page_dest, new_pages, after)


def nt_dot(a, b):
    return lax.dot_general(a, b, (((1,), (1,)), ((), ())), preferred_element_type=jnp.float32)


def dot(a, b):
    return jnp.dot(a, b, preferred_element_type=jnp.float32)


def page_rows(ref, first, pages, start, width):
    block = ref[pl.ds(first, pages), :, start : start + width]
    return block.reshape(pages * ref.shape[1], width)


def weigh(q_ref, bias_ref, res_ref, keys_ref, start, scores_ref, slots_ref=None):
    d = q_ref.shape[1]
    n_res, tokens, _ = res_ref.shape
    q = q_ref[...]

    def score(ref, i, group, column, to):
        columns = pl.ds(pl.multiple_of(to * tokens, tokens), group * tokens)
        keys = page_rows(ref, i * group, group, column, d)
        scores_ref[:, columns] = nt_dot(q, keys) + bias_ref[:, columns]

    group = math.gcd(n_res, GROUP)
    for i in range(n_res // group):
        score(res_ref, i, group, 0, i * group)
    cap = keys_ref.shape[0]
    group = math.gcd(cap, GROUP) if slots_ref is None else 1
    for i in range(cap // group):
        score(keys_ref, i, group, start, n_res + (i * group if slots_ref is None else slots_ref[i]))
    scores = scores_ref[...]
    prob = jnp.exp(scores - jnp.max(scores, axis=1, keepdims=True))
    scores_ref[...] = prob
    return jnp.sum(prob, axis=1, keepdims=True)


def begin_head(q_ref, bias_ref, res_ref, keys_ref, start, scores_ref, out_refs, slots_ref=None):
    weights_ref, summed_ref, total_ref = out_refs
    d = q_ref.shape[1]
    n_res, tokens, _ = res_ref.shape
    total = weigh(q_ref, bias_ref, res_ref, keys_ref, start, scores_ref, slots_ref)
    total_ref[...] = jnp.broadcast_to(total, total_ref.shape)
    weights_ref[...] = scores_ref[:, n_res * tokens :].astype(weights_ref.dtype)
    early = scores_ref[:, : n_res * tokens].astype(weights_ref.dtype)
    summed_ref[...] = dot(early, page_rows(res_ref, 0, n_res, d, d))


def first_kernel(
    slots_ref, q_ref, bias_ref, res_ref, keys_ref,
    arrived_ref, weights_ref, summed_ref, total_ref, scores_ref, sems,
):
    d = q_ref.shape[1]
    copies = []
    for j in range(keys_ref.shape[0]):
        target = arrived_ref.at[slots_ref[j], :, pl.ds(0, d)]
        copies.append(pltpu.make_async_copy(keys_ref.at[j], target, sems.at[j]))
        copies[-1].start()
    out_refs = (weights_ref, summed_ref, total_ref)
    begin_head(q_ref, bias_ref, res_ref, keys_ref, 0, scores_ref, out_refs, slots_ref)
    for copy in copies:
        copy.wait()


def middle_kernel(
    start, q_ref, bias_ref, res_ref, late_ref, old_weights_ref, old_summed_ref, old_total_ref, *rest
):
    arrived_ref, context_ref, weights_ref, summed_ref, total_ref, scores_ref, sems = rest[-7:]
    cap, _, width = late_ref.shape
    d = q_ref.shape[1]
    copies = []
    for j in range(cap):
        target = arrived_ref.at[j, :, pl.ds(start, width)]
        copies.append(pltpu.make_async_copy(late_ref.at[j], target, sems.at[j]))
        copies[-1].start()
    summed = old_summed_ref[...] + dot(old_weights_ref[...], page_rows(late_ref, 0, cap, 0, d))
    context_ref[...] = (summed / old_total_ref[...]).astype(context_ref.dtype)
    out_refs = (weights_ref, summed_ref, total_ref)
    begin_head(q_ref, bias_ref, res_ref, late_ref, d, scores_ref, out_refs)
    for copy in copies:
        copy.wait()


def last_kernel(start, weights_ref, summed_ref, total_ref, late_ref, *rest):
    arrived_ref, context_ref, sem, held, head, in_sems, out_sems = rest[-7:]
    pages, tokens, width = late_ref.shape
    parts = in_sems.shape[0]
    size = pages // parts

    def part(ref, i):
        return ref.at[pl.ds(i * size, size)]

    def copy_in(i):
        return pltpu.make_async_copy(part(late_ref, i), part(held, i), in_sems.at[i])

    def copy_out(i):
        target = part(arrived_ref, i).at[:, :, pl.ds(start, width)]
        return pltpu.make_async_copy(part(held, i), target, out_sems.at[i])

    for i in range(parts):
        copy_in(i).start()
    summed = summed_ref[...]
    span = size * tokens
    for i in range(parts):
        copy_in(i).wait()
        copy_out(i).start()
        block = held[i * size : (i + 1) * size].reshape(span, width)
        summed += dot(weights_ref[:, i * span : (i + 1) * span], block)
    head[...] = (summed / total_ref[...]).astype(head.dtype)
    columns = pl.ds((start - width) // 2, width)
    finish = pltpu.make_async_copy(head, context_ref.at[:, columns], sem)
    finish.start()
    for i in range(parts):
        copy_out(i).wait()
    finish.wait()


def whole(array):
    return pl.BlockSpec(array.shape, lambda i: (0,) * array.ndim)


def attend(chunks, resident, queries, bias, slots):
    d = HEAD_DIM
    requests, width = queries.shape
    last = width // d - 1
    n_res, tokens, _ = resident.shape
    cap = chunks[0].shape[0]
    pool = (n_res + cap) * tokens
    in_hbm = pl.BlockSpec(memory_space=pltpu.HBM)
    in_vmem = pl.BlockSpec(memory_space=pltpu.VMEM)
    anywhere = pl.BlockSpec(memory_space=pl.ANY)
    arrived_shape = jax.ShapeDtypeStruct((cap, tokens, 2 * width), resident.dtype)
    context_shape = jax.ShapeDtypeStruct((requests, width), jnp.bfloat16)
    parts_shape = [
        jax.ShapeDtypeStruct((requests, cap * tokens), jnp.bfloat16),
        jax.ShapeDtypeStruct((requests, d), jnp.float32),
        jax.ShapeDtypeStruct((requests, d), jnp.float32),
    ]
    scratch = [pltpu.VMEM((requests, pool), jnp.float32), pltpu.SemaphoreType.DMA((cap,))]
    params = pltpu.CompilerParams(vmem_limit_bytes=VMEM_LIMIT)
    cost = pl.CostEstimate(
        flops=4 * requests * pool * d,
        bytes_accessed=6 * pool * d,
        transcendentals=requests * pool,
    )

    def head_specs(h):
        return [
            pl.BlockSpec((requests, d), lambda i: (0, h)),
            whole(bias),
            pl.BlockSpec((n_res, tokens, 2 * d), lambda i: (0, 0, h)),
        ]

    arrived, *parts = pl.pallas_call(
        first_kernel,
        grid=(1,),
        in_specs=[pl.BlockSpec(memory_space=pltpu.SMEM), *head_specs(0), whole(chunks[0])],
        out_specs=[in_hbm, *(whole(x) for x in parts_shape)],
        out_shape=[arrived_shape, *parts_shape],
        scratch_shapes=scratch,
        compiler_params=params,
        cost_estimate=cost,
    )(slots, queries, bias, resident, chunks[0])
    context = None
    for h, late in enumerate(chunks[1:-1], 1):
        carried = [arrived] if context is None else [arrived, context]
        arrived, context, *parts = pl.pallas_call(
            functools.partial(middle_kernel, (2 * h - 1) * d),
            grid=(1,),
            in_specs=[
                *head_specs(h),
                whole(late),
                *(whole(x) for x in parts),
                *[in_hbm, anywhere][: len(carried)],
            ],
            out_specs=[
                in_hbm,
                pl.BlockSpec((requests, d), lambda i, h=h: (0, h - 1)),
                *(whole(x) for x in parts_shape),
            ],
            out_shape=[arrived_shape, context_shape, *parts_shape],
            scratch_shapes=scratch,
            input_output_aliases={7 + i: i for i in range(len(carried))},
            compiler_params=params,
            cost_estimate=cost,
        )(queries, bias, resident, late, *parts, *carried)
    late = chunks[-1]
    n_parts = cap // math.gcd(cap, GROUP)
    sems = pltpu.SemaphoreType.DMA((n_parts,))
    return pl.pallas_call(
        functools.partial(last_kernel, (2 * last + 1) * d),
        in_specs=[in_vmem, in_vmem, in_vmem, anywhere, in_hbm, in_hbm],
        out_specs=[in_hbm, in_hbm],
        out_shape=[arrived_shape, context_shape],
        scratch_shapes=[
            pltpu.SemaphoreType.DMA,
            pltpu.VMEM(late.shape, late.dtype),
            pltpu.VMEM((requests, d), context.dtype),
            sems,
            sems,
        ],
        input_output_aliases={4: 0, 5: 1},
        compiler_params=params,
        cost_estimate=pl.CostEstimate(
            flops=2 * requests * cap * tokens * d,
            bytes_accessed=4 * cap * tokens * d,
            transcendentals=0,
        ),
    )(*parts, late, arrived, context)


def two_ways(distance, n):
    return distance % 2 == 1 and n % 2 == 0 and 2 < distance < n - 2


def send(distance, chunks):
    n = lax.axis_size("dp")
    if distance == 0:
        return list(chunks)
    if not two_ways(distance, n):
        return [route(c, lambda i: i + distance) for c in chunks]
    pairs = n // 2
    far, near = (distance + 1) // 2, (distance - 1) // 2
    odd_is_far = min(far, pairs - far) > min(near, pairs - near)
    far_side = 1 if odd_is_far else 0
    rest = distance + 1 if odd_is_far else distance - 1
    *direct, halfway, final = chunks
    first, *direct, final = [route(c, lambda i: i + distance) for c in (*direct, final)]
    halfway = route(halfway, lambda i: i ^ 1 if i % 2 == far_side else i + distance)
    first, _ = lax.optimization_barrier((first, halfway))
    halfway = route(halfway, lambda i: i if i % 2 == far_side else i + rest)
    return [first, *direct, halfway, final]


def offset_digits(n):
    digits = []
    place = 1
    while place < n:
        digits.append((place, min(RADIX, -(-n // place))))
        place *= RADIX
    return digits


def quotient(value, by):
    if by & (by - 1) == 0:
        return lax.shift_right_logical(value, by.bit_length() - 1)
    return lax.div(value, by)


def local(new_pages, page_dest, resident, queries, page_table, cross_len):
    n_groups = lax.axis_size("dp")
    cap, tokens, _ = new_pages.shape
    d = HEAD_DIM
    heads = queries.shape[1] // d
    n_res = resident.shape[0]
    offset = quotient(page_dest[0], cap)

    def bias_of(page_table, cross_len):
        slots = jnp.arange(n_res + cap, dtype=jnp.int32)
        within = jnp.arange(page_table.shape[1], dtype=jnp.int32)[None, :] < cross_len[:, None]
        member = (page_table[:, :, None] == slots[None, None, :]) & within[:, :, None]
        bias = jnp.where(jnp.any(member, axis=1), 0.0, -jnp.inf).astype(jnp.float32)
        return jnp.repeat(bias, tokens, axis=1)

    blocks = [((2 * h - 1) * d, 2 * d) for h in range(1, heads)] + [((2 * heads - 1) * d, d)]

    digits = offset_digits(n_groups)
    last = len(digits) - 1

    def step(distance, index, carry, new_pages, page_dest, resident, queries, page_table, cross_len):
        if index == 0:
            carry = [new_pages[:, :, :d]] + [None] * len(blocks)
            order = list(range(1, len(carry)))
            if two_ways(distance, n_groups):
                order.insert(0, order.pop(-2))
            after = carry[0]
            for c in order:
                after = carry[c] = stage(new_pages, page_dest, *blocks[c - 1], after)
        carry = send(distance, carry)
        if index < last:
            return tuple(carry)
        source = lax.rem(lax.axis_index("dp") - quotient(page_dest[0], cap) + n_groups, n_groups)
        slots = lax.rem(lax.dynamic_slice_in_dim(page_dest, source * cap, cap), cap)
        return attend(carry, resident, queries, bias_of(page_table, cross_len), slots)

    carry = ()
    for index, (place, base) in enumerate(digits):
        digit = quotient(offset, place)
        first = 1 if last == 0 else 0
        if index < last:
            digit = lax.rem(digit, base)
        carry = lax.switch(
            digit - first,
            [functools.partial(step, k * place, index) for k in range(first, base)],
            carry, new_pages, page_dest, resident, queries, page_table, cross_len,
        )
    return carry


def solution(mesh):
    return jax.shard_map(
        local,
        mesh=mesh,
        in_specs=(
            P("dp", None, "tensor"),
            P(),
            P("dp", None, "tensor"),
            P("dp", "tensor"),
            P("dp", None),
            P("dp"),
        ),
        out_specs=(P("dp", None, "tensor"), P("dp", "tensor")),
        check_vma=False,
    )
```

```python
import functools
import math

import jax
import jax.numpy as jnp
from jax import lax
from jax.experimental import pallas as pl
from jax.experimental.pallas import tpu as pltpu
from jax.sharding import PartitionSpec as P

HEAD_DIM = 256
RADIX = 8
VMEM_LIMIT = 8 * 1024 * 1024
STAGE_LIMIT = 4 * 1024 * 1024
GROUP = 2


def stage_kernel(start, dest_ref, pages_ref, _, out_ref, sems):
    cap = pages_ref.shape[0]
    first = lax.axis_index("dp") * cap
    copies = []
    for j in range(cap):
        slot = lax.rem(dest_ref[first + j], cap)
        source = pages_ref.at[j, :, pl.ds(start, out_ref.shape[2])]
        copies.append(pltpu.make_async_copy(source, out_ref.at[slot], sems.at[j]))
        copies[-1].start()
    for copy in copies:
        copy.wait()


def stage(new_pages, page_dest, start, width, after):
    cap, tokens, _ = new_pages.shape
    return pl.pallas_call(
        functools.partial(stage_kernel, start),
        in_specs=[
            pl.BlockSpec(memory_space=pltpu.SMEM),
            pl.BlockSpec(memory_space=pl.ANY),
            pl.BlockSpec(memory_space=pl.ANY),
        ],
        out_specs=pl.BlockSpec(memory_space=pltpu.VMEM),
        out_shape=jax.ShapeDtypeStruct((cap, tokens, width), new_pages.dtype),
        scratch_shapes=[pltpu.SemaphoreType.DMA((cap,))],
        compiler_params=pltpu.CompilerParams(vmem_limit_bytes=STAGE_LIMIT),
        cost_estimate=pl.CostEstimate(
            flops=0, bytes_accessed=4 * cap * tokens * width, transcendentals=0
        ),
    )(page_dest, new_pages, after)


def nt_dot(a, b):
    return lax.dot_general(a, b, (((1,), (1,)), ((), ())), preferred_element_type=jnp.float32)


def dot(a, b):
    return jnp.dot(a, b, preferred_element_type=jnp.float32)


def page_rows(ref, first, pages, start, width):
    block = ref[pl.ds(first, pages), :, start : start + width]
    return block.reshape(pages * ref.shape[1], width)


def weigh(q_ref, bias_ref, res_ref, keys_ref, start, scores_ref, slots_ref=None):
    d = q_ref.shape[1]
    n_res, tokens, _ = res_ref.shape
    q = q_ref[...]

    def score(ref, i, group, column, to):
        columns = pl.ds(pl.multiple_of(to * tokens, tokens), group * tokens)
        keys = page_rows(ref, i * group, group, column, d)
        scores_ref[:, columns] = nt_dot(q, keys) + bias_ref[:, columns]

    group = math.gcd(n_res, GROUP)
    for i in range(n_res // group):
        score(res_ref, i, group, 0, i * group)
    cap = keys_ref.shape[0]
    group = math.gcd(cap, GROUP) if slots_ref is None else 1
    for i in range(cap // group):
        score(keys_ref, i, group, start, n_res + (i * group if slots_ref is None else slots_ref[i]))
    scores = scores_ref[...]
    prob = jnp.exp(scores - jnp.max(scores, axis=1, keepdims=True))
    scores_ref[...] = prob
    return jnp.sum(prob, axis=1, keepdims=True)


def begin_head(q_ref, bias_ref, res_ref, keys_ref, start, scores_ref, out_refs, slots_ref=None):
    weights_ref, summed_ref, total_ref = out_refs
    d = q_ref.shape[1]
    n_res, tokens, _ = res_ref.shape
    total = weigh(q_ref, bias_ref, res_ref, keys_ref, start, scores_ref, slots_ref)
    total_ref[...] = jnp.broadcast_to(total, total_ref.shape)
    weights_ref[...] = scores_ref[:, n_res * tokens :].astype(weights_ref.dtype)
    early = scores_ref[:, : n_res * tokens].astype(weights_ref.dtype)
    summed_ref[...] = dot(early, page_rows(res_ref, 0, n_res, d, d))


def first_kernel(
    slots_ref, q_ref, bias_ref, res_ref, keys_ref,
    arrived_ref, weights_ref, summed_ref, total_ref, scores_ref, sems,
):
    d = q_ref.shape[1]
    copies = []
    for j in range(keys_ref.shape[0]):
        target = arrived_ref.at[slots_ref[j], :, pl.ds(0, d)]
        copies.append(pltpu.make_async_copy(keys_ref.at[j], target, sems.at[j]))
        copies[-1].start()
    out_refs = (weights_ref, summed_ref, total_ref)
    begin_head(q_ref, bias_ref, res_ref, keys_ref, 0, scores_ref, out_refs, slots_ref)
    for copy in copies:
        copy.wait()


def middle_kernel(
    start, q_ref, bias_ref, res_ref, late_ref, old_weights_ref, old_summed_ref, old_total_ref, *rest
):
    arrived_ref, context_ref, weights_ref, summed_ref, total_ref, scores_ref, sems = rest[-7:]
    cap, _, width = late_ref.shape
    d = q_ref.shape[1]
    copies = []
    for j in range(cap):
        target = arrived_ref.at[j, :, pl.ds(start, width)]
        copies.append(pltpu.make_async_copy(late_ref.at[j], target, sems.at[j]))
        copies[-1].start()
    summed = old_summed_ref[...] + dot(old_weights_ref[...], page_rows(late_ref, 0, cap, 0, d))
    context_ref[...] = (summed / old_total_ref[...]).astype(context_ref.dtype)
    out_refs = (weights_ref, summed_ref, total_ref)
    begin_head(q_ref, bias_ref, res_ref, late_ref, d, scores_ref, out_refs)
    for copy in copies:
        copy.wait()


def last_kernel(start, weights_ref, summed_ref, total_ref, late_ref, *rest):
    arrived_ref, context_ref, sem, held, head, in_sems, out_sems = rest[-7:]
    pages, tokens, width = late_ref.shape
    parts = in_sems.shape[0]
    size = pages // parts

    def part(ref, i):
        return ref.at[pl.ds(i * size, size)]

    def copy_in(i):
        return pltpu.make_async_copy(part(late_ref, i), part(held, i), in_sems.at[i])

    def copy_out(i):
        target = part(arrived_ref, i).at[:, :, pl.ds(start, width)]
        return pltpu.make_async_copy(part(held, i), target, out_sems.at[i])

    for i in range(parts):
        copy_in(i).start()
    summed = summed_ref[...]
    span = size * tokens
    for i in range(parts):
        copy_in(i).wait()
        copy_out(i).start()
        block = held[i * size : (i + 1) * size].reshape(span, width)
        summed += dot(weights_ref[:, i * span : (i + 1) * span], block)
    head[...] = (summed / total_ref[...]).astype(head.dtype)
    columns = pl.ds((start - width) // 2, width)
    finish = pltpu.make_async_copy(head, context_ref.at[:, columns], sem)
    finish.start()
    for i in range(parts):
        copy_out(i).wait()
    finish.wait()


def whole(array):
    return pl.BlockSpec(array.shape, lambda i: (0,) * array.ndim)


def attend(chunks, resident, queries, bias, slots):
    d = HEAD_DIM
    requests, width = queries.shape
    last = width // d - 1
    n_res, tokens, _ = resident.shape
    cap = chunks[0].shape[0]
    pool = (n_res + cap) * tokens
    in_hbm = pl.BlockSpec(memory_space=pltpu.HBM)
    in_vmem = pl.BlockSpec(memory_space=pltpu.VMEM)
    anywhere = pl.BlockSpec(memory_space=pl.ANY)
    arrived_shape = jax.ShapeDtypeStruct((cap, tokens, 2 * width), resident.dtype)
    context_shape = jax.ShapeDtypeStruct((requests, width), jnp.bfloat16)
    parts_shape = [
        jax.ShapeDtypeStruct((requests, cap * tokens), jnp.bfloat16),
        jax.ShapeDtypeStruct((requests, d), jnp.float32),
        jax.ShapeDtypeStruct((requests, d), jnp.float32),
    ]
    scratch = [pltpu.VMEM((requests, pool), jnp.float32), pltpu.SemaphoreType.DMA((cap,))]
    params = pltpu.CompilerParams(vmem_limit_bytes=VMEM_LIMIT)
    cost = pl.CostEstimate(
        flops=4 * requests * pool * d,
        bytes_accessed=6 * pool * d,
        transcendentals=requests * pool,
    )

    def head_specs(h):
        return [
            pl.BlockSpec((requests, d), lambda i: (0, h)),
            whole(bias),
            pl.BlockSpec((n_res, tokens, 2 * d), lambda i: (0, 0, h)),
        ]

    arrived, *parts = pl.pallas_call(
        first_kernel,
        grid=(1,),
        in_specs=[pl.BlockSpec(memory_space=pltpu.SMEM), *head_specs(0), whole(chunks[0])],
        out_specs=[in_hbm, *(whole(x) for x in parts_shape)],
        out_shape=[arrived_shape, *parts_shape],
        scratch_shapes=scratch,
        compiler_params=params,
        cost_estimate=cost,
    )(slots, queries, bias, resident, chunks[0])
    context = None
    pieces = [(c, k) for c in chunks[1:-1] for k in range(c.shape[2] // (2 * d))]
    for h, (late, piece) in enumerate(pieces, 1):
        carried = [arrived] if context is None else [arrived, context]
        arrived, context, *parts = pl.pallas_call(
            functools.partial(middle_kernel, (2 * h - 1) * d),
            grid=(1,),
            in_specs=[
                *head_specs(h),
                pl.BlockSpec((cap, tokens, 2 * d), lambda i, piece=piece: (0, 0, piece)),
                *(whole(x) for x in parts),
                *[in_hbm, anywhere][: len(carried)],
            ],
            out_specs=[
                in_hbm,
                pl.BlockSpec((requests, d), lambda i, h=h: (0, h - 1)),
                *(whole(x) for x in parts_shape),
            ],
            out_shape=[arrived_shape, context_shape, *parts_shape],
            scratch_shapes=scratch,
            input_output_aliases={7 + i: i for i in range(len(carried))},
            compiler_params=params,
            cost_estimate=cost,
        )(queries, bias, resident, late, *parts, *carried)
    late = chunks[-1]
    n_parts = cap // math.gcd(cap, GROUP)
    sems = pltpu.SemaphoreType.DMA((n_parts,))
    return pl.pallas_call(
        functools.partial(last_kernel, (2 * last + 1) * d),
        in_specs=[in_vmem, in_vmem, in_vmem, anywhere, in_hbm, in_hbm],
        out_specs=[in_hbm, in_hbm],
        out_shape=[arrived_shape, context_shape],
        scratch_shapes=[
            pltpu.SemaphoreType.DMA,
            pltpu.VMEM(late.shape, late.dtype),
            pltpu.VMEM((requests, d), context.dtype),
            sems,
            sems,
        ],
        input_output_aliases={4: 0, 5: 1},
        compiler_params=params,
        cost_estimate=pl.CostEstimate(
            flops=2 * requests * cap * tokens * d,
            bytes_accessed=4 * cap * tokens * d,
            transcendentals=0,
        ),
    )(*parts, late, arrived, context)


def two_ways(distance, n):
    return n <= RADIX and n % 2 == 0 and distance % 2 == 1 and 2 < distance < n - 2


def send(distance, chunks):
    n = lax.axis_size("dp")
    if distance == 0:
        return list(chunks)

    def direct(chunk, without=()):
        route = [(i, (i + distance) % n) for i in range(n) if i not in without]
        return lax.ppermute(chunk, "dp", route)

    if not two_ways(distance, n):
        return [direct(c) for c in chunks]
    pairs = n // 2
    far, near = (distance + 1) // 2, (distance - 1) // 2
    side = 1 if min(far, pairs - far) > min(near, pairs - near) else 0
    ends = [i for i in (side, n - 2 + side)]
    first, *others, large, final = chunks
    first = direct(first)
    turned = lax.ppermute(large, "dp", [(i, i ^ 1) for i in ends])
    large = direct(large, ends)
    others = [direct(c) for c in others]
    final = direct(final)
    first, turned = lax.optimization_barrier((first, turned))
    targets = [(i + distance) % n for i in ends]
    turned = lax.ppermute(turned, "dp", [(i ^ 1, t) for i, t in zip(ends, targets)])
    group = lax.axis_index("dp")
    is_target = functools.reduce(jnp.logical_or, [group == t for t in targets])
    return [first, *others, jnp.where(is_target, turned, large), final]


def offset_digits(n):
    digits = []
    place = 1
    while place < n:
        digits.append((place, min(RADIX, -(-n // place))))
        place *= RADIX
    return digits


def quotient(value, by):
    if by & (by - 1) == 0:
        return lax.shift_right_logical(value, by.bit_length() - 1)
    return lax.div(value, by)


def local(new_pages, page_dest, resident, queries, page_table, cross_len):
    n_groups = lax.axis_size("dp")
    cap, tokens, _ = new_pages.shape
    d = HEAD_DIM
    heads = queries.shape[1] // d
    n_res = resident.shape[0]
    offset = quotient(page_dest[0], cap)

    def bias_of(page_table, cross_len):
        slots = jnp.arange(n_res + cap, dtype=jnp.int32)
        within = jnp.arange(page_table.shape[1], dtype=jnp.int32)[None, :] < cross_len[:, None]
        member = (page_table[:, :, None] == slots[None, None, :]) & within[:, :, None]
        bias = jnp.where(jnp.any(member, axis=1), 0.0, -jnp.inf).astype(jnp.float32)
        return jnp.repeat(bias, tokens, axis=1)

    def blocks_of(distance):
        blocks = [((2 * h - 1) * d, 2 * d) for h in range(1, heads)]
        if two_ways(distance, n_groups):
            large = heads // 2
            blocks[-large:] = [(blocks[-large][0], 2 * d * large)]
        return [*blocks, ((2 * heads - 1) * d, d)]

    digits = offset_digits(n_groups)
    last = len(digits) - 1

    def step(distance, index, carry, new_pages, page_dest, resident, queries, page_table, cross_len):
        if index == 0:
            blocks = blocks_of(distance)
            order = list(range(len(blocks)))
            if two_ways(distance, n_groups):
                order.insert(0, order.pop(-2))
            after = new_pages[:, :, :d]
            carry = [after] + [None] * len(blocks)
            for c in order:
                after = carry[c + 1] = stage(new_pages, page_dest, *blocks[c], after)
        carry = send(distance, carry)
        if index < last:
            return tuple(carry)
        source = lax.rem(lax.axis_index("dp") - quotient(page_dest[0], cap) + n_groups, n_groups)
        slots = lax.rem(lax.dynamic_slice_in_dim(page_dest, source * cap, cap), cap)
        return attend(carry, resident, queries, bias_of(page_table, cross_len), slots)

    carry = ()
    for index, (place, base) in enumerate(digits):
        digit = quotient(offset, place)
        first = 1 if last == 0 else 0
        if index < last:
            digit = lax.rem(digit, base)
        carry = lax.switch(
            digit - first,
            [functools.partial(step, k * place, index) for k in range(first, base)],
            carry, new_pages, page_dest, resident, queries, page_table, cross_len,
        )
    return carry


def solution(mesh):
    return jax.shard_map(
        local,
        mesh=mesh,
        in_specs=(
            P("dp", None, "tensor"),
            P(),
            P("dp", None, "tensor"),
            P("dp", "tensor"),
            P("dp", None),
            P("dp"),
        ),
        out_specs=(P("dp", None, "tensor"), P("dp", "tensor")),
        check_vma=False,
    )
```

```python
import functools
import math

import jax
import jax.numpy as jnp
from jax import lax
from jax.experimental import pallas as pl
from jax.experimental.pallas import tpu as pltpu
from jax.sharding import PartitionSpec as P

HEAD_DIM = 256
RADIX = 8
VMEM_LIMIT = 8 * 1024 * 1024
GROUP = 4


def stage_kernel(start, dest_ref, pages_ref, _, out_ref, sems):
    cap = pages_ref.shape[0]
    first = lax.axis_index("dp") * cap

    def copy(j):
        source = pages_ref.at[j, :, pl.ds(start, out_ref.shape[2])]
        slot = lax.rem(dest_ref[first + j], cap)
        return pltpu.make_async_copy(source, out_ref.at[slot], sems.at[j])

    pl.loop(0, cap)(lambda j: copy(j).start())
    pl.loop(0, cap)(lambda j: copy(j).wait())


def stage(new_pages, page_dest, start, width, after):
    cap, tokens, _ = new_pages.shape
    return pl.pallas_call(
        functools.partial(stage_kernel, start),
        in_specs=[
            pl.BlockSpec(memory_space=pltpu.SMEM),
            pl.BlockSpec(memory_space=pl.ANY),
            pl.BlockSpec(memory_space=pl.ANY),
        ],
        out_specs=pl.BlockSpec(memory_space=pltpu.VMEM),
        out_shape=jax.ShapeDtypeStruct((cap, tokens, width), new_pages.dtype),
        scratch_shapes=[pltpu.SemaphoreType.DMA((cap,))],
        cost_estimate=pl.CostEstimate(
            flops=0, bytes_accessed=4 * cap * tokens * width, transcendentals=0
        ),
    )(page_dest, new_pages, after)


def nt_dot(a, b):
    return lax.dot_general(a, b, (((1,), (1,)), ((), ())), preferred_element_type=jnp.float32)


def dot(a, b):
    return jnp.dot(a, b, preferred_element_type=jnp.float32)


def page_rows(ref, first, pages, start, width):
    block = ref[pl.ds(first, pages), :, start : start + width]
    return block.reshape(pages * ref.shape[1], width)


def weigh(q_ref, bias_ref, res_ref, keys_ref, start, scores_ref, slots_ref=None):
    d = q_ref.shape[1]
    n_res, tokens, _ = res_ref.shape
    q = q_ref[...]

    def score(ref, i, group, column, to):
        columns = pl.ds(pl.multiple_of(to * tokens, tokens), group * tokens)
        keys = page_rows(ref, i * group, group, column, d)
        scores_ref[:, columns] = nt_dot(q, keys) + bias_ref[:, columns]

    group = math.gcd(n_res, GROUP)
    pl.loop(0, n_res // group)(lambda i: score(res_ref, i, group, 0, i * group))
    cap = keys_ref.shape[0]
    if slots_ref is None:
        group = math.gcd(cap, GROUP)
        pl.loop(0, cap // group)(
            lambda i: score(keys_ref, i, group, start, n_res + i * group)
        )
    else:
        pl.loop(0, cap)(lambda i: score(keys_ref, i, 1, start, n_res + slots_ref[i]))
    scores = scores_ref[...]
    prob = jnp.exp(scores - jnp.max(scores, axis=1, keepdims=True))
    scores_ref[...] = prob
    return jnp.sum(prob, axis=1, keepdims=True)


def begin_head(q_ref, bias_ref, res_ref, keys_ref, start, scores_ref, out_refs, slots_ref=None):
    weights_ref, summed_ref, total_ref = out_refs
    d = q_ref.shape[1]
    n_res, tokens, _ = res_ref.shape
    total = weigh(q_ref, bias_ref, res_ref, keys_ref, start, scores_ref, slots_ref)
    total_ref[...] = jnp.broadcast_to(total, total_ref.shape)
    weights_ref[...] = scores_ref[:, n_res * tokens :].astype(weights_ref.dtype)
    group = math.gcd(n_res, GROUP)

    def add(i, summed):
        columns = pl.ds(pl.multiple_of(i * group * tokens, tokens), group * tokens)
        early = scores_ref[:, columns].astype(weights_ref.dtype)
        return summed + dot(early, page_rows(res_ref, i * group, group, d, d))

    zero = jnp.zeros(summed_ref.shape, jnp.float32)
    summed_ref[...] = lax.fori_loop(0, n_res // group, add, zero)


def first_kernel(
    slots_ref, q_ref, bias_ref, res_ref, keys_ref,
    arrived_ref, weights_ref, summed_ref, total_ref, scores_ref, sems,
):
    cap = keys_ref.shape[0]

    def copy(j):
        target = arrived_ref.at[slots_ref[j], :, pl.ds(0, q_ref.shape[1])]
        return pltpu.make_async_copy(keys_ref.at[j], target, sems.at[j])

    pl.loop(0, cap)(lambda j: copy(j).start())
    out_refs = (weights_ref, summed_ref, total_ref)
    begin_head(q_ref, bias_ref, res_ref, keys_ref, 0, scores_ref, out_refs, slots_ref)
    pl.loop(0, cap)(lambda j: copy(j).wait())


def middle_kernel(
    start, q_ref, bias_ref, res_ref, late_ref, old_weights_ref, old_summed_ref, old_total_ref, *rest
):
    arrived_ref, context_ref, weights_ref, summed_ref, total_ref, scores_ref, sems = rest[-7:]
    cap, _, width = late_ref.shape
    d = q_ref.shape[1]
    group = math.gcd(cap, GROUP)

    def copy(j):
        target = arrived_ref.at[j, :, pl.ds(start, width)]
        return pltpu.make_async_copy(late_ref.at[j], target, sems.at[j])

    pl.loop(0, cap)(lambda j: copy(j).start())

    def add(i, summed):
        tokens = group * late_ref.shape[1]
        weights = old_weights_ref[:, pl.ds(pl.multiple_of(i * tokens, tokens), tokens)]
        return summed + dot(weights, page_rows(late_ref, i * group, group, 0, d))

    summed = lax.fori_loop(0, cap // group, add, old_summed_ref[...])
    context_ref[...] = (summed / old_total_ref[...]).astype(context_ref.dtype)
    out_refs = (weights_ref, summed_ref, total_ref)
    begin_head(q_ref, bias_ref, res_ref, late_ref, d, scores_ref, out_refs)
    pl.loop(0, cap)(lambda j: copy(j).wait())


def last_kernel(start, weights_ref, summed_ref, total_ref, late_ref, *rest):
    arrived_ref, context_ref, sem, held, head, in_sems, out_sems = rest[-7:]
    pages, tokens, width = late_ref.shape
    parts = in_sems.shape[0]
    size = pages // parts

    def part(ref, i):
        return ref.at[pl.ds(i * size, size)]

    def copy_in(i):
        return pltpu.make_async_copy(part(late_ref, i), part(held, i), in_sems.at[i])

    def copy_out(i):
        target = part(arrived_ref, i).at[:, :, pl.ds(start, width)]
        return pltpu.make_async_copy(part(held, i), target, out_sems.at[i])

    for i in range(parts):
        copy_in(i).start()
    summed = summed_ref[...]
    span = size * tokens
    for i in range(parts):
        copy_in(i).wait()
        copy_out(i).start()
        block = held[i * size : (i + 1) * size].reshape(span, width)
        summed += dot(weights_ref[:, i * span : (i + 1) * span], block)
    head[...] = (summed / total_ref[...]).astype(head.dtype)
    columns = pl.ds((start - width) // 2, width)
    finish = pltpu.make_async_copy(head, context_ref.at[:, columns], sem)
    finish.start()
    for i in range(parts):
        copy_out(i).wait()
    finish.wait()


def whole(array):
    return pl.BlockSpec(array.shape, lambda i: (0,) * array.ndim)


def attend(chunks, resident, queries, bias, slots):
    d = HEAD_DIM
    requests, width = queries.shape
    last = width // d - 1
    n_res, tokens, _ = resident.shape
    cap = chunks[0].shape[0]
    pool = (n_res + cap) * tokens
    in_hbm = pl.BlockSpec(memory_space=pltpu.HBM)
    in_vmem = pl.BlockSpec(memory_space=pltpu.VMEM)
    anywhere = pl.BlockSpec(memory_space=pl.ANY)
    arrived_shape = jax.ShapeDtypeStruct((cap, tokens, 2 * width), resident.dtype)
    context_shape = jax.ShapeDtypeStruct((requests, width), jnp.bfloat16)
    parts_shape = [
        jax.ShapeDtypeStruct((requests, cap * tokens), jnp.bfloat16),
        jax.ShapeDtypeStruct((requests, d), jnp.float32),
        jax.ShapeDtypeStruct((requests, d), jnp.float32),
    ]
    scratch = [pltpu.VMEM((requests, pool), jnp.float32), pltpu.SemaphoreType.DMA((cap,))]
    params = pltpu.CompilerParams(vmem_limit_bytes=VMEM_LIMIT)
    cost = pl.CostEstimate(
        flops=4 * requests * pool * d,
        bytes_accessed=6 * pool * d,
        transcendentals=requests * pool,
    )

    def head_specs(h):
        return [
            pl.BlockSpec((requests, d), lambda i: (0, h)),
            whole(bias),
            pl.BlockSpec((n_res, tokens, 2 * d), lambda i: (0, 0, h)),
        ]

    arrived, *parts = pl.pallas_call(
        first_kernel,
        grid=(1,),
        in_specs=[pl.BlockSpec(memory_space=pltpu.SMEM), *head_specs(0), whole(chunks[0])],
        out_specs=[in_hbm, *(whole(x) for x in parts_shape)],
        out_shape=[arrived_shape, *parts_shape],
        scratch_shapes=scratch,
        compiler_params=params,
        cost_estimate=cost,
    )(slots, queries, bias, resident, chunks[0])
    context = None
    pieces = [(c, k) for c in chunks[1:-1] for k in range(c.shape[2] // (2 * d))]
    for h, (late, piece) in enumerate(pieces, 1):
        carried = [arrived] if context is None else [arrived, context]
        arrived, context, *parts = pl.pallas_call(
            functools.partial(middle_kernel, (2 * h - 1) * d),
            grid=(1,),
            in_specs=[
                *head_specs(h),
                pl.BlockSpec((cap, tokens, 2 * d), lambda i, piece=piece: (0, 0, piece)),
                *(whole(x) for x in parts),
                *[in_hbm, anywhere][: len(carried)],
            ],
            out_specs=[
                in_hbm,
                pl.BlockSpec((requests, d), lambda i, h=h: (0, h - 1)),
                *(whole(x) for x in parts_shape),
            ],
            out_shape=[arrived_shape, context_shape, *parts_shape],
            scratch_shapes=scratch,
            input_output_aliases={7 + i: i for i in range(len(carried))},
            compiler_params=params,
            cost_estimate=cost,
        )(queries, bias, resident, late, *parts, *carried)
    late = chunks[-1]
    n_parts = cap // math.gcd(cap, 2)
    sems = pltpu.SemaphoreType.DMA((n_parts,))
    return pl.pallas_call(
        functools.partial(last_kernel, (2 * last + 1) * d),
        in_specs=[in_vmem, in_vmem, in_vmem, anywhere, in_hbm, in_hbm],
        out_specs=[in_hbm, in_hbm],
        out_shape=[arrived_shape, context_shape],
        scratch_shapes=[
            pltpu.SemaphoreType.DMA,
            pltpu.VMEM(late.shape, late.dtype),
            pltpu.VMEM((requests, d), context.dtype),
            sems,
            sems,
        ],
        input_output_aliases={4: 0, 5: 1},
        compiler_params=params,
        cost_estimate=pl.CostEstimate(
            flops=2 * requests * cap * tokens * d,
            bytes_accessed=4 * cap * tokens * d,
            transcendentals=0,
        ),
    )(*parts, late, arrived, context)


def two_ways(distance, n):
    return n <= RADIX and n % 2 == 0 and distance % 2 == 1 and 2 < distance < n - 2


def send(distance, chunks):
    n = lax.axis_size("dp")
    if distance == 0:
        return list(chunks)

    def direct(chunk, without=()):
        route = [(i, (i + distance) % n) for i in range(n) if i not in without]
        return lax.ppermute(chunk, "dp", route)

    if not two_ways(distance, n):
        return [direct(c) for c in chunks]
    pairs = n // 2
    far, near = (distance + 1) // 2, (distance - 1) // 2
    side = 1 if min(far, pairs - far) > min(near, pairs - near) else 0
    ends = [i for i in (side, n - 2 + side)]
    first, *others, large, final = chunks
    first = direct(first)
    turned = lax.ppermute(large, "dp", [(i, i ^ 1) for i in ends])
    large = direct(large, ends)
    others = [direct(c) for c in others]
    final = direct(final)
    first, turned = lax.optimization_barrier((first, turned))
    targets = [(i + distance) % n for i in ends]
    turned = lax.ppermute(turned, "dp", [(i ^ 1, t) for i, t in zip(ends, targets)])
    group = lax.axis_index("dp")
    is_target = functools.reduce(jnp.logical_or, [group == t for t in targets])
    return [first, *others, jnp.where(is_target, turned, large), final]


def offset_digits(n):
    digits = []
    place = 1
    while place < n:
        digits.append((place, min(RADIX, -(-n // place))))
        place *= RADIX
    return digits


def quotient(value, by):
    if by & (by - 1) == 0:
        return lax.shift_right_logical(value, by.bit_length() - 1)
    return lax.div(value, by)


def local(new_pages, page_dest, resident, queries, page_table, cross_len):
    n_groups = lax.axis_size("dp")
    cap, tokens, _ = new_pages.shape
    d = HEAD_DIM
    heads = queries.shape[1] // d
    n_res = resident.shape[0]
    offset = quotient(page_dest[0], cap)

    def bias_of(page_table, cross_len):
        slots = jnp.arange(n_res + cap, dtype=jnp.int32)
        within = jnp.arange(page_table.shape[1], dtype=jnp.int32)[None, :] < cross_len[:, None]
        member = (page_table[:, :, None] == slots[None, None, :]) & within[:, :, None]
        bias = jnp.where(jnp.any(member, axis=1), 0.0, -jnp.inf).astype(jnp.float32)
        return jnp.repeat(bias, tokens, axis=1)

    def blocks_of(distance):
        blocks = [((2 * h - 1) * d, 2 * d) for h in range(1, heads)]
        if two_ways(distance, n_groups):
            large = heads // 2
            blocks[-large:] = [(blocks[-large][0], 2 * d * large)]
        return [*blocks, ((2 * heads - 1) * d, d)]

    digits = offset_digits(n_groups)
    last = len(digits) - 1

    def step(distance, index, carry, new_pages, page_dest, resident, queries, page_table, cross_len):
        if index == 0:
            blocks = blocks_of(distance)
            order = list(range(len(blocks)))
            if two_ways(distance, n_groups):
                order.insert(0, order.pop(-2))
            after = new_pages[:, :, :d]
            carry = [after] + [None] * len(blocks)
            for c in order:
                after = carry[c + 1] = stage(new_pages, page_dest, *blocks[c], after)
        carry = send(distance, carry)
        if index < last:
            return tuple(carry)
        source = lax.rem(lax.axis_index("dp") - quotient(page_dest[0], cap) + n_groups, n_groups)
        slots = lax.rem(lax.dynamic_slice_in_dim(page_dest, source * cap, cap), cap)
        return attend(carry, resident, queries, bias_of(page_table, cross_len), slots)

    carry = ()
    for index, (place, base) in enumerate(digits):
        digit = quotient(offset, place)
        first = 1 if last == 0 else 0
        if index < last:
            digit = lax.rem(digit, base)
        carry = lax.switch(
            digit - first,
            [functools.partial(step, k * place, index) for k in range(first, base)],
            carry, new_pages, page_dest, resident, queries, page_table, cross_len,
        )
    return carry


def solution(mesh):
    return jax.shard_map(
        local,
        mesh=mesh,
        in_specs=(
            P("dp", None, "tensor"),
            P(),
            P("dp", None, "tensor"),
            P("dp", "tensor"),
            P("dp", None),
            P("dp"),
        ),
        out_specs=(P("dp", None, "tensor"), P("dp", "tensor")),
        check_vma=False,
    )
```

```python
import functools
import math

import jax
import jax.numpy as jnp
from jax import lax
from jax.experimental import pallas as pl
from jax.experimental.pallas import tpu as pltpu
from jax.sharding import PartitionSpec as P

HEAD_DIM = 256
RADIX = 8
VMEM_LIMIT = 8 * 1024 * 1024
GROUP = 4


def stage_kernel(start, dest_ref, pages_ref, _, out_ref, sems):
    cap = pages_ref.shape[0]
    first = lax.axis_index("dp") * cap

    def copy(j):
        source = pages_ref.at[j, :, pl.ds(start, out_ref.shape[2])]
        slot = lax.rem(dest_ref[first + j], cap)
        return pltpu.make_async_copy(source, out_ref.at[slot], sems.at[j])

    pl.loop(0, cap)(lambda j: copy(j).start())
    pl.loop(0, cap)(lambda j: copy(j).wait())


def stage(new_pages, page_dest, start, width, after):
    cap, tokens, _ = new_pages.shape
    return pl.pallas_call(
        functools.partial(stage_kernel, start),
        in_specs=[
            pl.BlockSpec(memory_space=pltpu.SMEM),
            pl.BlockSpec(memory_space=pl.ANY),
            pl.BlockSpec(memory_space=pl.ANY),
        ],
        out_specs=pl.BlockSpec(memory_space=pltpu.VMEM),
        out_shape=jax.ShapeDtypeStruct((cap, tokens, width), new_pages.dtype),
        scratch_shapes=[pltpu.SemaphoreType.DMA((cap,))],
        cost_estimate=pl.CostEstimate(
            flops=0, bytes_accessed=4 * cap * tokens * width, transcendentals=0
        ),
    )(page_dest, new_pages, after)


def nt_dot(a, b):
    return lax.dot_general(a, b, (((1,), (1,)), ((), ())), preferred_element_type=jnp.float32)


def dot(a, b):
    return jnp.dot(a, b, preferred_element_type=jnp.float32)


def page_rows(ref, first, pages, start, width):
    block = ref[pl.ds(first, pages), :, start : start + width]
    return block.reshape(pages * ref.shape[1], width)


def weigh(q_ref, bias_ref, res_ref, keys_ref, start, scores_ref, slots_ref=None):
    d = q_ref.shape[1]
    n_res, tokens, _ = res_ref.shape
    q = q_ref[...]

    def score(ref, i, group, column, to):
        columns = pl.ds(pl.multiple_of(to * tokens, tokens), group * tokens)
        keys = page_rows(ref, i * group, group, column, d)
        scores_ref[:, columns] = nt_dot(q, keys) + bias_ref[:, columns]

    group = math.gcd(n_res, GROUP)
    pl.loop(0, n_res // group)(lambda i: score(res_ref, i, group, 0, i * group))
    cap = keys_ref.shape[0]
    if slots_ref is None:
        group = math.gcd(cap, GROUP)
        pl.loop(0, cap // group)(
            lambda i: score(keys_ref, i, group, start, n_res + i * group)
        )
    else:
        pl.loop(0, cap)(lambda i: score(keys_ref, i, 1, start, n_res + slots_ref[i]))
    scores = scores_ref[...]
    prob = jnp.exp(scores - jnp.max(scores, axis=1, keepdims=True))
    scores_ref[...] = prob
    return jnp.sum(prob, axis=1, keepdims=True)


def begin_head(q_ref, bias_ref, res_ref, keys_ref, start, scores_ref, out_refs, slots_ref=None):
    weights_ref, summed_ref, total_ref = out_refs
    d = q_ref.shape[1]
    n_res, tokens, _ = res_ref.shape
    total = weigh(q_ref, bias_ref, res_ref, keys_ref, start, scores_ref, slots_ref)
    total_ref[...] = jnp.broadcast_to(total, total_ref.shape)
    weights_ref[...] = scores_ref[:, n_res * tokens :].astype(weights_ref.dtype)
    group = math.gcd(n_res, GROUP)

    def add(i, summed):
        columns = pl.ds(pl.multiple_of(i * group * tokens, tokens), group * tokens)
        early = scores_ref[:, columns].astype(weights_ref.dtype)
        return summed + dot(early, page_rows(res_ref, i * group, group, d, d))

    zero = jnp.zeros(summed_ref.shape, jnp.float32)
    summed_ref[...] = lax.fori_loop(0, n_res // group, add, zero)


def first_kernel(
    slots_ref, q_ref, bias_ref, res_ref, keys_ref,
    arrived_ref, weights_ref, summed_ref, total_ref, scores_ref, sems,
):
    cap = keys_ref.shape[0]

    def copy(j):
        target = arrived_ref.at[slots_ref[j], :, pl.ds(0, q_ref.shape[1])]
        return pltpu.make_async_copy(keys_ref.at[j], target, sems.at[j])

    pl.loop(0, cap)(lambda j: copy(j).start())
    out_refs = (weights_ref, summed_ref, total_ref)
    begin_head(q_ref, bias_ref, res_ref, keys_ref, 0, scores_ref, out_refs, slots_ref)
    pl.loop(0, cap)(lambda j: copy(j).wait())


def middle_kernel(
    start, q_ref, bias_ref, res_ref, late_ref, old_weights_ref, old_summed_ref, old_total_ref, *rest
):
    arrived_ref, context_ref, weights_ref, summed_ref, total_ref, scores_ref, sems = rest[-7:]
    cap, _, width = late_ref.shape
    d = q_ref.shape[1]
    group = math.gcd(cap, GROUP)

    def copy(j):
        target = arrived_ref.at[j, :, pl.ds(start, width)]
        return pltpu.make_async_copy(late_ref.at[j], target, sems.at[j])

    pl.loop(0, cap)(lambda j: copy(j).start())

    def add(i, summed):
        tokens = group * late_ref.shape[1]
        weights = old_weights_ref[:, pl.ds(pl.multiple_of(i * tokens, tokens), tokens)]
        return summed + dot(weights, page_rows(late_ref, i * group, group, 0, d))

    summed = lax.fori_loop(0, cap // group, add, old_summed_ref[...])
    context_ref[...] = (summed / old_total_ref[...]).astype(context_ref.dtype)
    out_refs = (weights_ref, summed_ref, total_ref)
    begin_head(q_ref, bias_ref, res_ref, late_ref, d, scores_ref, out_refs)
    pl.loop(0, cap)(lambda j: copy(j).wait())


def last_kernel(start, weights_ref, summed_ref, total_ref, late_ref, *rest):
    arrived_ref, context_ref, sem, held, head, in_sems, out_sems = rest[-7:]
    pages, tokens, width = late_ref.shape
    parts = in_sems.shape[0]
    size = pages // parts

    def part(ref, i):
        return ref.at[pl.ds(i * size, size)]

    def copy_in(i):
        return pltpu.make_async_copy(part(late_ref, i), part(held, i), in_sems.at[i])

    def copy_out(i):
        target = part(arrived_ref, i).at[:, :, pl.ds(start, width)]
        return pltpu.make_async_copy(part(held, i), target, out_sems.at[i])

    for i in range(parts):
        copy_in(i).start()
    summed = summed_ref[...]
    span = size * tokens
    for i in range(parts):
        copy_in(i).wait()
        copy_out(i).start()
        block = held[i * size : (i + 1) * size].reshape(span, width)
        summed += dot(weights_ref[:, i * span : (i + 1) * span], block)
    head[...] = (summed / total_ref[...]).astype(head.dtype)
    columns = pl.ds((start - width) // 2, width)
    finish = pltpu.make_async_copy(head, context_ref.at[:, columns], sem)
    finish.start()
    for i in range(parts):
        copy_out(i).wait()
    finish.wait()


def whole(array):
    return pl.BlockSpec(array.shape, lambda i: (0,) * array.ndim)


def attend(chunks, resident, queries, bias, slots):
    d = HEAD_DIM
    requests, width = queries.shape
    last = width // d - 1
    n_res, tokens, _ = resident.shape
    cap = chunks[0].shape[0]
    pool = (n_res + cap) * tokens
    in_hbm = pl.BlockSpec(memory_space=pltpu.HBM)
    in_vmem = pl.BlockSpec(memory_space=pltpu.VMEM)
    anywhere = pl.BlockSpec(memory_space=pl.ANY)
    arrived_shape = jax.ShapeDtypeStruct((cap, tokens, 2 * width), resident.dtype)
    context_shape = jax.ShapeDtypeStruct((requests, width), jnp.bfloat16)
    parts_shape = [
        jax.ShapeDtypeStruct((requests, cap * tokens), jnp.bfloat16),
        jax.ShapeDtypeStruct((requests, d), jnp.float32),
        jax.ShapeDtypeStruct((requests, d), jnp.float32),
    ]
    scratch = [pltpu.VMEM((requests, pool), jnp.float32), pltpu.SemaphoreType.DMA((cap,))]
    params = pltpu.CompilerParams(vmem_limit_bytes=VMEM_LIMIT)
    cost = pl.CostEstimate(
        flops=4 * requests * pool * d,
        bytes_accessed=6 * pool * d,
        transcendentals=requests * pool,
    )

    def head_specs(h):
        return [
            pl.BlockSpec((requests, d), lambda i: (0, h)),
            whole(bias),
            pl.BlockSpec((n_res, tokens, 2 * d), lambda i: (0, 0, h)),
        ]

    arrived, *parts = pl.pallas_call(
        first_kernel,
        grid=(1,),
        in_specs=[pl.BlockSpec(memory_space=pltpu.SMEM), *head_specs(0), whole(chunks[0])],
        out_specs=[in_hbm, *(whole(x) for x in parts_shape)],
        out_shape=[arrived_shape, *parts_shape],
        scratch_shapes=scratch,
        compiler_params=params,
        cost_estimate=cost,
    )(slots, queries, bias, resident, chunks[0])
    context = None
    pieces = [(c, k) for c in chunks[1:-1] for k in range(c.shape[2] // (2 * d))]
    for h, (late, piece) in enumerate(pieces, 1):
        carried = [arrived] if context is None else [arrived, context]
        arrived, context, *parts = pl.pallas_call(
            functools.partial(middle_kernel, (2 * h - 1) * d),
            grid=(1,),
            in_specs=[
                *head_specs(h),
                pl.BlockSpec((cap, tokens, 2 * d), lambda i, piece=piece: (0, 0, piece)),
                *(whole(x) for x in parts),
                *[in_hbm, anywhere][: len(carried)],
            ],
            out_specs=[
                in_hbm,
                pl.BlockSpec((requests, d), lambda i, h=h: (0, h - 1)),
                *(whole(x) for x in parts_shape),
            ],
            out_shape=[arrived_shape, context_shape, *parts_shape],
            scratch_shapes=scratch,
            input_output_aliases={7 + i: i for i in range(len(carried))},
            compiler_params=params,
            cost_estimate=cost,
        )(queries, bias, resident, late, *parts, *carried)
    late = chunks[-1]
    n_parts = cap // math.gcd(cap, 2)
    sems = pltpu.SemaphoreType.DMA((n_parts,))
    return pl.pallas_call(
        functools.partial(last_kernel, (2 * last + 1) * d),
        in_specs=[in_vmem, in_vmem, in_vmem, anywhere, in_hbm, in_hbm],
        out_specs=[in_hbm, in_hbm],
        out_shape=[arrived_shape, context_shape],
        scratch_shapes=[
            pltpu.SemaphoreType.DMA,
            pltpu.VMEM(late.shape, late.dtype),
            pltpu.VMEM((requests, d), context.dtype),
            sems,
            sems,
        ],
        input_output_aliases={4: 0, 5: 1},
        compiler_params=params,
        cost_estimate=pl.CostEstimate(
            flops=2 * requests * cap * tokens * d,
            bytes_accessed=4 * cap * tokens * d,
            transcendentals=0,
        ),
    )(*parts, late, arrived, context)


def two_ways(distance, n):
    return n <= RADIX and n % 2 == 0 and distance % 2 == 1 and 2 < distance < n - 2


def send(distance, chunks):
    n = lax.axis_size("dp")
    if distance == 0:
        return list(chunks)

    def direct(chunk, without=()):
        route = [(i, (i + distance) % n) for i in range(n) if i not in without]
        return lax.ppermute(chunk, "dp", route)

    if not two_ways(distance, n):
        return [direct(c) for c in chunks]
    pairs = n // 2
    far, near = (distance + 1) // 2, (distance - 1) // 2
    side = 1 if min(far, pairs - far) > min(near, pairs - near) else 0
    ends = [i for i in (side, n - 2 + side)]
    targets = [(i + distance) % n for i in ends]
    inner = [i for i in range(side, n, 2) if i not in ends]
    others = [i for i in range(1 - side, n, 2)]
    *chunks, turning, final = chunks
    first, *chunks, final = [direct(c) for c in (*chunks, final)]
    from_inner = lax.ppermute(
        turning, "dp", [(i, i ^ 1) for i in inner] + [(i, (i + distance) % n) for i in others]
    )
    from_ends = lax.ppermute(turning, "dp", [(i, i ^ 1) for i in ends])
    first, _, _ = lax.optimization_barrier((first, from_inner, from_ends))
    from_inner = lax.ppermute(
        from_inner,
        "dp",
        [(i ^ 1, (i + distance) % n) for i in inner] + [(i, i) for i in range(side, n, 2)],
    )
    from_ends = lax.ppermute(from_ends, "dp", [(i ^ 1, t) for i, t in zip(ends, targets)])
    group = lax.axis_index("dp")
    not_target = functools.reduce(jnp.logical_and, [group != t for t in targets])
    return [first, *chunks, jnp.where(not_target, from_inner, from_ends), final]


def offset_digits(n):
    digits = []
    place = 1
    while place < n:
        digits.append((place, min(RADIX, -(-n // place))))
        place *= RADIX
    return digits


def quotient(value, by):
    if by & (by - 1) == 0:
        return lax.shift_right_logical(value, by.bit_length() - 1)
    return lax.div(value, by)


def local(new_pages, page_dest, resident, queries, page_table, cross_len):
    n_groups = lax.axis_size("dp")
    cap, tokens, _ = new_pages.shape
    d = HEAD_DIM
    heads = queries.shape[1] // d
    n_res = resident.shape[0]
    offset = quotient(page_dest[0], cap)

    def bias_of(page_table, cross_len):
        slots = jnp.arange(n_res + cap, dtype=jnp.int32)
        within = jnp.arange(page_table.shape[1], dtype=jnp.int32)[None, :] < cross_len[:, None]
        member = (page_table[:, :, None] == slots[None, None, :]) & within[:, :, None]
        bias = jnp.where(jnp.any(member, axis=1), 0.0, -jnp.inf).astype(jnp.float32)
        return jnp.repeat(bias, tokens, axis=1)

    def blocks_of():
        blocks = [((2 * h - 1) * d, 2 * d) for h in range(1, heads)]
        return [*blocks, ((2 * heads - 1) * d, d)]

    digits = offset_digits(n_groups)
    last = len(digits) - 1

    def step(distance, index, carry, new_pages, page_dest, resident, queries, page_table, cross_len):
        if index == 0:
            blocks = blocks_of()
            order = list(range(len(blocks)))
            if two_ways(distance, n_groups):
                order.insert(0, order.pop(-2))
            after = new_pages[:, :, :d]
            carry = [after] + [None] * len(blocks)
            for c in order:
                after = carry[c + 1] = stage(new_pages, page_dest, *blocks[c], after)
        carry = send(distance, carry)
        if index < last:
            return tuple(carry)
        source = lax.rem(lax.axis_index("dp") - quotient(page_dest[0], cap) + n_groups, n_groups)
        slots = lax.rem(lax.dynamic_slice_in_dim(page_dest, source * cap, cap), cap)
        return attend(carry, resident, queries, bias_of(page_table, cross_len), slots)

    carry = ()
    for index, (place, base) in enumerate(digits):
        digit = quotient(offset, place)
        first = 1 if last == 0 else 0
        if index < last:
            digit = lax.rem(digit, base)
        carry = lax.switch(
            digit - first,
            [functools.partial(step, k * place, index) for k in range(first, base)],
            carry, new_pages, page_dest, resident, queries, page_table, cross_len,
        )
    return carry


def solution(mesh):
    return jax.shard_map(
        local,
        mesh=mesh,
        in_specs=(
            P("dp", None, "tensor"),
            P(),
            P("dp", None, "tensor"),
            P("dp", "tensor"),
            P("dp", None),
            P("dp"),
        ),
        out_specs=(P("dp", None, "tensor"), P("dp", "tensor")),
        check_vma=False,
    )
```

```python
import functools
import math

import jax
import jax.numpy as jnp
from jax import lax
from jax.experimental import pallas as pl
from jax.experimental.pallas import tpu as pltpu
from jax.sharding import PartitionSpec as P

HEAD_DIM = 256
RADIX = 8
VMEM_LIMIT = 8 * 1024 * 1024
GROUP = 4


def stage_kernel(start, dest_ref, pages_ref, _, out_ref, sems):
    cap = pages_ref.shape[0]
    first = lax.axis_index("dp") * cap

    def copy(j):
        source = pages_ref.at[j, :, pl.ds(start, out_ref.shape[2])]
        slot = lax.rem(dest_ref[first + j], cap)
        return pltpu.make_async_copy(source, out_ref.at[slot], sems.at[j])

    pl.loop(0, cap)(lambda j: copy(j).start())
    pl.loop(0, cap)(lambda j: copy(j).wait())


def stage(new_pages, page_dest, start, width, after):
    cap, tokens, _ = new_pages.shape
    return pl.pallas_call(
        functools.partial(stage_kernel, start),
        in_specs=[
            pl.BlockSpec(memory_space=pltpu.SMEM),
            pl.BlockSpec(memory_space=pl.ANY),
            pl.BlockSpec(memory_space=pl.ANY),
        ],
        out_specs=pl.BlockSpec(memory_space=pltpu.VMEM),
        out_shape=jax.ShapeDtypeStruct((cap, tokens, width), new_pages.dtype),
        scratch_shapes=[pltpu.SemaphoreType.DMA((cap,))],
        cost_estimate=pl.CostEstimate(
            flops=0, bytes_accessed=4 * cap * tokens * width, transcendentals=0
        ),
    )(page_dest, new_pages, after)


def nt_dot(a, b):
    return lax.dot_general(a, b, (((1,), (1,)), ((), ())), preferred_element_type=jnp.float32)


def dot(a, b):
    return jnp.dot(a, b, preferred_element_type=jnp.float32)


def page_rows(ref, first, pages, start, width):
    block = ref[pl.ds(first, pages), :, start : start + width]
    return block.reshape(pages * ref.shape[1], width)


def weigh(q_ref, bias_ref, res_ref, keys_ref, start, scores_ref, slots_ref=None):
    d = q_ref.shape[1]
    n_res, tokens, _ = res_ref.shape
    q = q_ref[...]

    def score(ref, i, group, column, to):
        columns = pl.ds(pl.multiple_of(to * tokens, tokens), group * tokens)
        keys = page_rows(ref, i * group, group, column, d)
        scores_ref[:, columns] = nt_dot(q, keys) + bias_ref[:, columns]

    group = math.gcd(n_res, GROUP)
    pl.loop(0, n_res // group)(lambda i: score(res_ref, i, group, 0, i * group))
    cap = keys_ref.shape[0]
    if slots_ref is None:
        group = math.gcd(cap, GROUP)
        pl.loop(0, cap // group)(
            lambda i: score(keys_ref, i, group, start, n_res + i * group)
        )
    else:
        pl.loop(0, cap)(lambda i: score(keys_ref, i, 1, start, n_res + slots_ref[i]))
    scores = scores_ref[...]
    prob = jnp.exp(scores - jnp.max(scores, axis=1, keepdims=True))
    scores_ref[...] = prob
    return jnp.sum(prob, axis=1, keepdims=True)


def begin_head(q_ref, bias_ref, res_ref, keys_ref, start, scores_ref, out_refs, slots_ref=None):
    weights_ref, summed_ref, total_ref = out_refs
    d = q_ref.shape[1]
    n_res, tokens, _ = res_ref.shape
    total = weigh(q_ref, bias_ref, res_ref, keys_ref, start, scores_ref, slots_ref)
    total_ref[...] = jnp.broadcast_to(total, total_ref.shape)
    weights_ref[...] = scores_ref[:, n_res * tokens :].astype(weights_ref.dtype)
    group = math.gcd(n_res, GROUP)

    def add(i, summed):
        columns = pl.ds(pl.multiple_of(i * group * tokens, tokens), group * tokens)
        early = scores_ref[:, columns].astype(weights_ref.dtype)
        return summed + dot(early, page_rows(res_ref, i * group, group, d, d))

    zero = jnp.zeros(summed_ref.shape, jnp.float32)
    summed_ref[...] = lax.fori_loop(0, n_res // group, add, zero)


def first_kernel(
    slots_ref, q_ref, bias_ref, res_ref, keys_ref,
    arrived_ref, weights_ref, summed_ref, total_ref, scores_ref, sems,
):
    cap = keys_ref.shape[0]

    def copy(j):
        target = arrived_ref.at[slots_ref[j], :, pl.ds(0, q_ref.shape[1])]
        return pltpu.make_async_copy(keys_ref.at[j], target, sems.at[j])

    pl.loop(0, cap)(lambda j: copy(j).start())
    out_refs = (weights_ref, summed_ref, total_ref)
    begin_head(q_ref, bias_ref, res_ref, keys_ref, 0, scores_ref, out_refs, slots_ref)
    pl.loop(0, cap)(lambda j: copy(j).wait())


def middle_kernel(
    start, q_ref, bias_ref, res_ref, late_ref, old_weights_ref, old_summed_ref, old_total_ref, *rest
):
    arrived_ref, context_ref, weights_ref, summed_ref, total_ref, scores_ref, sems = rest[-7:]
    cap, _, width = late_ref.shape
    d = q_ref.shape[1]
    group = math.gcd(cap, GROUP)

    def copy(j):
        target = arrived_ref.at[j, :, pl.ds(start, width)]
        return pltpu.make_async_copy(late_ref.at[j], target, sems.at[j])

    pl.loop(0, cap)(lambda j: copy(j).start())

    def add(i, summed):
        tokens = group * late_ref.shape[1]
        weights = old_weights_ref[:, pl.ds(pl.multiple_of(i * tokens, tokens), tokens)]
        return summed + dot(weights, page_rows(late_ref, i * group, group, 0, d))

    summed = lax.fori_loop(0, cap // group, add, old_summed_ref[...])
    context_ref[...] = (summed / old_total_ref[...]).astype(context_ref.dtype)
    out_refs = (weights_ref, summed_ref, total_ref)
    begin_head(q_ref, bias_ref, res_ref, late_ref, d, scores_ref, out_refs)
    pl.loop(0, cap)(lambda j: copy(j).wait())


def last_kernel(start, weights_ref, summed_ref, total_ref, late_ref, *rest):
    arrived_ref, context_ref, sem, held, head, in_sems, out_sems = rest[-7:]
    pages, tokens, width = late_ref.shape
    parts = in_sems.shape[0]
    size = pages // parts

    def part(ref, i):
        return ref.at[pl.ds(i * size, size)]

    def copy_in(i):
        return pltpu.make_async_copy(part(late_ref, i), part(held, i), in_sems.at[i])

    def copy_out(i):
        target = part(arrived_ref, i).at[:, :, pl.ds(start, width)]
        return pltpu.make_async_copy(part(held, i), target, out_sems.at[i])

    for i in range(parts):
        copy_in(i).start()
    summed = summed_ref[...]
    span = size * tokens
    for i in range(parts):
        copy_in(i).wait()
        copy_out(i).start()
        block = held[i * size : (i + 1) * size].reshape(span, width)
        summed += dot(weights_ref[:, i * span : (i + 1) * span], block)
    head[...] = (summed / total_ref[...]).astype(head.dtype)
    columns = pl.ds((start - width) // 2, width)
    finish = pltpu.make_async_copy(head, context_ref.at[:, columns], sem)
    finish.start()
    for i in range(parts):
        copy_out(i).wait()
    finish.wait()


def whole(array):
    return pl.BlockSpec(array.shape, lambda i: (0,) * array.ndim)


def attend(chunks, resident, queries, bias, slots):
    d = HEAD_DIM
    requests, width = queries.shape
    last = width // d - 1
    n_res, tokens, _ = resident.shape
    cap = chunks[0].shape[0]
    pool = (n_res + cap) * tokens
    in_hbm = pl.BlockSpec(memory_space=pltpu.HBM)
    in_vmem = pl.BlockSpec(memory_space=pltpu.VMEM)
    anywhere = pl.BlockSpec(memory_space=pl.ANY)
    arrived_shape = jax.ShapeDtypeStruct((cap, tokens, 2 * width), resident.dtype)
    context_shape = jax.ShapeDtypeStruct((requests, width), jnp.bfloat16)
    parts_shape = [
        jax.ShapeDtypeStruct((requests, cap * tokens), jnp.bfloat16),
        jax.ShapeDtypeStruct((requests, d), jnp.float32),
        jax.ShapeDtypeStruct((requests, d), jnp.float32),
    ]
    scratch = [pltpu.VMEM((requests, pool), jnp.float32), pltpu.SemaphoreType.DMA((cap,))]
    params = pltpu.CompilerParams(vmem_limit_bytes=VMEM_LIMIT)
    cost = pl.CostEstimate(
        flops=4 * requests * pool * d,
        bytes_accessed=6 * pool * d,
        transcendentals=requests * pool,
    )

    def head_specs(h):
        return [
            pl.BlockSpec((requests, d), lambda i: (0, h)),
            whole(bias),
            pl.BlockSpec((n_res, tokens, 2 * d), lambda i: (0, 0, h)),
        ]

    arrived, *parts = pl.pallas_call(
        first_kernel,
        grid=(1,),
        in_specs=[pl.BlockSpec(memory_space=pltpu.SMEM), *head_specs(0), whole(chunks[0])],
        out_specs=[in_hbm, *(whole(x) for x in parts_shape)],
        out_shape=[arrived_shape, *parts_shape],
        scratch_shapes=scratch,
        compiler_params=params,
        cost_estimate=cost,
    )(slots, queries, bias, resident, chunks[0])
    context = None
    pieces = [(c, k) for c in chunks[1:-1] for k in range(c.shape[2] // (2 * d))]
    for h, (late, piece) in enumerate(pieces, 1):
        carried = [arrived] if context is None else [arrived, context]
        arrived, context, *parts = pl.pallas_call(
            functools.partial(middle_kernel, (2 * h - 1) * d),
            grid=(1,),
            in_specs=[
                *head_specs(h),
                pl.BlockSpec((cap, tokens, 2 * d), lambda i, piece=piece: (0, 0, piece)),
                *(whole(x) for x in parts),
                *[in_hbm, anywhere][: len(carried)],
            ],
            out_specs=[
                in_hbm,
                pl.BlockSpec((requests, d), lambda i, h=h: (0, h - 1)),
                *(whole(x) for x in parts_shape),
            ],
            out_shape=[arrived_shape, context_shape, *parts_shape],
            scratch_shapes=scratch,
            input_output_aliases={7 + i: i for i in range(len(carried))},
            compiler_params=params,
            cost_estimate=cost,
        )(queries, bias, resident, late, *parts, *carried)
    late = chunks[-1]
    n_parts = cap // math.gcd(cap, 2)
    sems = pltpu.SemaphoreType.DMA((n_parts,))
    return pl.pallas_call(
        functools.partial(last_kernel, (2 * last + 1) * d),
        in_specs=[in_vmem, in_vmem, in_vmem, anywhere, in_hbm, in_hbm],
        out_specs=[in_hbm, in_hbm],
        out_shape=[arrived_shape, context_shape],
        scratch_shapes=[
            pltpu.SemaphoreType.DMA,
            pltpu.VMEM(late.shape, late.dtype),
            pltpu.VMEM((requests, d), context.dtype),
            sems,
            sems,
        ],
        input_output_aliases={4: 0, 5: 1},
        compiler_params=params,
        cost_estimate=pl.CostEstimate(
            flops=2 * requests * cap * tokens * d,
            bytes_accessed=4 * cap * tokens * d,
            transcendentals=0,
        ),
    )(*parts, late, arrived, context)


def two_ways(distance, n):
    return n <= RADIX and n % 2 == 0 and distance % 2 == 1 and 2 < distance < n - 2


def send(distance, chunks):
    n = lax.axis_size("dp")
    if distance == 0:
        return list(chunks)

    def direct(chunk, without=()):
        route = [(i, (i + distance) % n) for i in range(n) if i not in without]
        return lax.ppermute(chunk, "dp", route)

    if not two_ways(distance, n):
        return [direct(c) for c in chunks]
    pairs = n // 2
    far, near = (distance + 1) // 2, (distance - 1) // 2
    side = 1 if min(far, pairs - far) > min(near, pairs - near) else 0
    ends = [i for i in (side, n - 2 + side)]
    targets = [(i + distance) % n for i in ends]
    inner = [i for i in range(side, n, 2) if i not in ends]
    others = [i for i in range(1 - side, n, 2)]
    *chunks, turning, final = chunks
    first, *chunks, final = [direct(c) for c in (*chunks, final)]
    from_inner = lax.ppermute(
        turning, "dp", [(i, i ^ 1) for i in inner] + [(i, (i + distance) % n) for i in others]
    )
    from_ends = lax.ppermute(turning, "dp", [(i, i ^ 1) for i in ends])
    first, _, _ = lax.optimization_barrier((first, from_inner, from_ends))
    from_inner = lax.ppermute(
        from_inner,
        "dp",
        [(i ^ 1, (i + distance) % n) for i in inner] + [(i, i) for i in range(side, n, 2)],
    )
    from_ends = lax.ppermute(from_ends, "dp", [(i ^ 1, t) for i, t in zip(ends, targets)])
    group = lax.axis_index("dp")
    not_target = functools.reduce(jnp.logical_and, [group != t for t in targets])
    return [first, *chunks, jnp.where(not_target, from_inner, from_ends), final]


def offset_digits(n):
    digits = []
    place = 1
    while place < n:
        digits.append((place, min(RADIX, -(-n // place))))
        place *= RADIX
    return digits


def quotient(value, by):
    if by & (by - 1) == 0:
        return lax.shift_right_logical(value, by.bit_length() - 1)
    return lax.div(value, by)


def local(new_pages, page_dest, resident, queries, page_table, cross_len):
    n_groups = lax.axis_size("dp")
    cap, tokens, _ = new_pages.shape
    d = HEAD_DIM
    heads = queries.shape[1] // d
    n_res = resident.shape[0]
    offset = quotient(page_dest[0], cap)

    def bias_of(page_table, cross_len):
        slots = jnp.arange(n_res + cap, dtype=jnp.int32)
        within = jnp.arange(page_table.shape[1], dtype=jnp.int32)[None, :] < cross_len[:, None]
        member = (page_table[:, :, None] == slots[None, None, :]) & within[:, :, None]
        bias = jnp.where(jnp.any(member, axis=1), 0.0, -jnp.inf).astype(jnp.float32)
        return jnp.repeat(bias, tokens, axis=1)

    def blocks_of(distance):
        blocks = [((2 * h - 1) * d, 2 * d) for h in range(1, heads)]
        if two_ways(distance, n_groups):
            blocks[:-1] = [(d, 2 * d * len(blocks[:-1]))]
        return [*blocks, ((2 * heads - 1) * d, d)]

    digits = offset_digits(n_groups)
    last = len(digits) - 1

    def step(distance, index, carry, new_pages, page_dest, resident, queries, page_table, cross_len):
        if index == 0:
            blocks = blocks_of(distance)
            order = list(range(len(blocks)))
            if two_ways(distance, n_groups):
                order.insert(0, order.pop(-2))
            after = new_pages[:, :, :d]
            carry = [after] + [None] * len(blocks)
            for c in order:
                after = carry[c + 1] = stage(new_pages, page_dest, *blocks[c], after)
        carry = send(distance, carry)
        if index < last:
            return tuple(carry)
        source = lax.rem(lax.axis_index("dp") - quotient(page_dest[0], cap) + n_groups, n_groups)
        slots = lax.rem(lax.dynamic_slice_in_dim(page_dest, source * cap, cap), cap)
        return attend(carry, resident, queries, bias_of(page_table, cross_len), slots)

    carry = ()
    for index, (place, base) in enumerate(digits):
        digit = quotient(offset, place)
        first = 1 if last == 0 else 0
        if index < last:
            digit = lax.rem(digit, base)
        carry = lax.switch(
            digit - first,
            [functools.partial(step, k * place, index) for k in range(first, base)],
            carry, new_pages, page_dest, resident, queries, page_table, cross_len,
        )
    return carry


def solution(mesh):
    return jax.shard_map(
        local,
        mesh=mesh,
        in_specs=(
            P("dp", None, "tensor"),
            P(),
            P("dp", None, "tensor"),
            P("dp", "tensor"),
            P("dp", None),
            P("dp"),
        ),
        out_specs=(P("dp", None, "tensor"), P("dp", "tensor")),
        check_vma=False,
    )
```

```python
import functools
import math

import jax
import jax.numpy as jnp
from jax import lax
from jax.experimental import pallas as pl
from jax.experimental.pallas import tpu as pltpu
from jax.sharding import PartitionSpec as P

HEAD_DIM = 256
RADIX = 8
VMEM_LIMIT = 8 * 1024 * 1024
GROUP = 2


def stage_kernel(start, dest_ref, pages_ref, _, out_ref, sems):
    cap = pages_ref.shape[0]
    first = lax.axis_index("dp") * cap

    def copy(j):
        source = pages_ref.at[j, :, pl.ds(start, out_ref.shape[2])]
        slot = lax.rem(dest_ref[first + j], cap)
        return pltpu.make_async_copy(source, out_ref.at[slot], sems.at[j])

    pl.loop(0, cap)(lambda j: copy(j).start())
    pl.loop(0, cap)(lambda j: copy(j).wait())


def stage(new_pages, page_dest, start, width, after):
    cap, tokens, _ = new_pages.shape
    return pl.pallas_call(
        functools.partial(stage_kernel, start),
        in_specs=[
            pl.BlockSpec(memory_space=pltpu.SMEM),
            pl.BlockSpec(memory_space=pl.ANY),
            pl.BlockSpec(memory_space=pl.ANY),
        ],
        out_specs=pl.BlockSpec(memory_space=pltpu.VMEM),
        out_shape=jax.ShapeDtypeStruct((cap, tokens, width), new_pages.dtype),
        scratch_shapes=[pltpu.SemaphoreType.DMA((cap,))],
        cost_estimate=pl.CostEstimate(
            flops=0, bytes_accessed=4 * cap * tokens * width, transcendentals=0
        ),
    )(page_dest, new_pages, after)


def nt_dot(a, b):
    return lax.dot_general(a, b, (((1,), (1,)), ((), ())), preferred_element_type=jnp.float32)


def dot(a, b):
    return jnp.dot(a, b, preferred_element_type=jnp.float32)


def page_rows(ref, first, pages, start, width):
    block = ref[pl.ds(first, pages), :, start : start + width]
    return block.reshape(pages * ref.shape[1], width)


def weigh(q_ref, bias_ref, res_ref, keys_ref, start, scores_ref, slots_ref=None):
    d = q_ref.shape[1]
    n_res, tokens, _ = res_ref.shape
    q = q_ref[...]

    def score(ref, i, group, column, to):
        columns = pl.ds(pl.multiple_of(to * tokens, tokens), group * tokens)
        keys = page_rows(ref, i * group, group, column, d)
        scores_ref[:, columns] = nt_dot(q, keys) + bias_ref[:, columns]

    group = math.gcd(n_res, GROUP)
    pl.loop(0, n_res // group)(lambda i: score(res_ref, i, group, 0, i * group))
    cap = keys_ref.shape[0]
    if slots_ref is None:
        group = math.gcd(cap, GROUP)
        pl.loop(0, cap // group)(
            lambda i: score(keys_ref, i, group, start, n_res + i * group)
        )
    else:
        pl.loop(0, cap)(lambda i: score(keys_ref, i, 1, start, n_res + slots_ref[i]))
    scores = scores_ref[...]
    prob = jnp.exp(scores - jnp.max(scores, axis=1, keepdims=True))
    scores_ref[...] = prob
    return jnp.sum(prob, axis=1, keepdims=True)


def begin_head(q_ref, bias_ref, res_ref, keys_ref, start, scores_ref, out_refs, slots_ref=None):
    weights_ref, summed_ref, total_ref = out_refs
    d = q_ref.shape[1]
    n_res, tokens, _ = res_ref.shape
    total = weigh(q_ref, bias_ref, res_ref, keys_ref, start, scores_ref, slots_ref)
    total_ref[...] = jnp.broadcast_to(total, total_ref.shape)
    weights_ref[...] = scores_ref[:, n_res * tokens :].astype(weights_ref.dtype)
    group = math.gcd(n_res, GROUP)

    def add(i, summed):
        columns = pl.ds(pl.multiple_of(i * group * tokens, tokens), group * tokens)
        early = scores_ref[:, columns].astype(weights_ref.dtype)
        return summed + dot(early, page_rows(res_ref, i * group, group, d, d))

    zero = jnp.zeros(summed_ref.shape, jnp.float32)
    summed_ref[...] = lax.fori_loop(0, n_res // group, add, zero)


def first_kernel(
    slots_ref, q_ref, bias_ref, res_ref, keys_ref,
    arrived_ref, weights_ref, summed_ref, total_ref, scores_ref, sems,
):
    cap = keys_ref.shape[0]

    def copy(j):
        target = arrived_ref.at[slots_ref[j], :, pl.ds(0, q_ref.shape[1])]
        return pltpu.make_async_copy(keys_ref.at[j], target, sems.at[j])

    pl.loop(0, cap)(lambda j: copy(j).start())
    out_refs = (weights_ref, summed_ref, total_ref)
    begin_head(q_ref, bias_ref, res_ref, keys_ref, 0, scores_ref, out_refs, slots_ref)
    pl.loop(0, cap)(lambda j: copy(j).wait())


def middle_kernel(
    start, q_ref, bias_ref, res_ref, late_ref, old_weights_ref, old_summed_ref, old_total_ref, *rest
):
    arrived_ref, context_ref, weights_ref, summed_ref, total_ref, scores_ref, sems = rest[-7:]
    cap, _, width = late_ref.shape
    d = q_ref.shape[1]
    group = math.gcd(cap, GROUP)

    def copy(j):
        target = arrived_ref.at[j, :, pl.ds(start, width)]
        return pltpu.make_async_copy(late_ref.at[j], target, sems.at[j])

    pl.loop(0, cap)(lambda j: copy(j).start())

    def add(i, summed):
        tokens = group * late_ref.shape[1]
        weights = old_weights_ref[:, pl.ds(pl.multiple_of(i * tokens, tokens), tokens)]
        return summed + dot(weights, page_rows(late_ref, i * group, group, 0, d))

    summed = lax.fori_loop(0, cap // group, add, old_summed_ref[...])
    context_ref[...] = (summed / old_total_ref[...]).astype(context_ref.dtype)
    out_refs = (weights_ref, summed_ref, total_ref)
    begin_head(q_ref, bias_ref, res_ref, late_ref, d, scores_ref, out_refs)
    pl.loop(0, cap)(lambda j: copy(j).wait())


def last_kernel(start, weights_ref, summed_ref, total_ref, late_ref, *rest):
    arrived_ref, context_ref, sem, held, head, in_sems, out_sems = rest[-7:]
    pages, tokens, width = late_ref.shape
    parts = in_sems.shape[0]
    size = pages // parts

    def part(ref, i):
        return ref.at[pl.ds(i * size, size)]

    def copy_in(i):
        return pltpu.make_async_copy(part(late_ref, i), part(held, i), in_sems.at[i])

    def copy_out(i):
        target = part(arrived_ref, i).at[:, :, pl.ds(start, width)]
        return pltpu.make_async_copy(part(held, i), target, out_sems.at[i])

    for i in range(parts):
        copy_in(i).start()
    summed = summed_ref[...]
    span = size * tokens
    for i in range(parts):
        copy_in(i).wait()
        copy_out(i).start()
        block = held[i * size : (i + 1) * size].reshape(span, width)
        summed += dot(weights_ref[:, i * span : (i + 1) * span], block)
    head[...] = (summed / total_ref[...]).astype(head.dtype)
    columns = pl.ds((start - width) // 2, width)
    finish = pltpu.make_async_copy(head, context_ref.at[:, columns], sem)
    finish.start()
    for i in range(parts):
        copy_out(i).wait()
    finish.wait()


def whole(array):
    return pl.BlockSpec(array.shape, lambda i: (0,) * array.ndim)


def attend(chunks, resident, queries, bias, slots):
    d = HEAD_DIM
    requests, width = queries.shape
    last = width // d - 1
    n_res, tokens, _ = resident.shape
    cap = chunks[0].shape[0]
    pool = (n_res + cap) * tokens
    in_hbm = pl.BlockSpec(memory_space=pltpu.HBM)
    in_vmem = pl.BlockSpec(memory_space=pltpu.VMEM)
    anywhere = pl.BlockSpec(memory_space=pl.ANY)
    arrived_shape = jax.ShapeDtypeStruct((cap, tokens, 2 * width), resident.dtype)
    context_shape = jax.ShapeDtypeStruct((requests, width), jnp.bfloat16)
    parts_shape = [
        jax.ShapeDtypeStruct((requests, cap * tokens), jnp.bfloat16),
        jax.ShapeDtypeStruct((requests, d), jnp.float32),
        jax.ShapeDtypeStruct((requests, d), jnp.float32),
    ]
    scratch = [pltpu.VMEM((requests, pool), jnp.float32), pltpu.SemaphoreType.DMA((cap,))]
    params = pltpu.CompilerParams(vmem_limit_bytes=VMEM_LIMIT)
    cost = pl.CostEstimate(
        flops=4 * requests * pool * d,
        bytes_accessed=6 * pool * d,
        transcendentals=requests * pool,
    )

    def head_specs(h):
        return [
            pl.BlockSpec((requests, d), lambda i: (0, h)),
            whole(bias),
            pl.BlockSpec((n_res, tokens, 2 * d), lambda i: (0, 0, h)),
        ]

    arrived, *parts = pl.pallas_call(
        first_kernel,
        grid=(1,),
        in_specs=[pl.BlockSpec(memory_space=pltpu.SMEM), *head_specs(0), whole(chunks[0])],
        out_specs=[in_hbm, *(whole(x) for x in parts_shape)],
        out_shape=[arrived_shape, *parts_shape],
        scratch_shapes=scratch,
        compiler_params=params,
        cost_estimate=cost,
    )(slots, queries, bias, resident, chunks[0])
    context = None
    pieces = [(c, k) for c in chunks[1:-1] for k in range(c.shape[2] // (2 * d))]
    for h, (late, piece) in enumerate(pieces, 1):
        carried = [arrived] if context is None else [arrived, context]
        arrived, context, *parts = pl.pallas_call(
            functools.partial(middle_kernel, (2 * h - 1) * d),
            grid=(1,),
            in_specs=[
                *head_specs(h),
                pl.BlockSpec((cap, tokens, 2 * d), lambda i, piece=piece: (0, 0, piece)),
                *(whole(x) for x in parts),
                *[in_hbm, anywhere][: len(carried)],
            ],
            out_specs=[
                in_hbm,
                pl.BlockSpec((requests, d), lambda i, h=h: (0, h - 1)),
                *(whole(x) for x in parts_shape),
            ],
            out_shape=[arrived_shape, context_shape, *parts_shape],
            scratch_shapes=scratch,
            input_output_aliases={7 + i: i for i in range(len(carried))},
            compiler_params=params,
            cost_estimate=cost,
        )(queries, bias, resident, late, *parts, *carried)
    late = chunks[-1]
    n_parts = cap // math.gcd(cap, 2)
    sems = pltpu.SemaphoreType.DMA((n_parts,))
    return pl.pallas_call(
        functools.partial(last_kernel, (2 * last + 1) * d),
        in_specs=[in_vmem, in_vmem, in_vmem, anywhere, in_hbm, in_hbm],
        out_specs=[in_hbm, in_hbm],
        out_shape=[arrived_shape, context_shape],
        scratch_shapes=[
            pltpu.SemaphoreType.DMA,
            pltpu.VMEM(late.shape, late.dtype),
            pltpu.VMEM((requests, d), context.dtype),
            sems,
            sems,
        ],
        input_output_aliases={4: 0, 5: 1},
        compiler_params=params,
        cost_estimate=pl.CostEstimate(
            flops=2 * requests * cap * tokens * d,
            bytes_accessed=4 * cap * tokens * d,
            transcendentals=0,
        ),
    )(*parts, late, arrived, context)


def two_ways(distance, n):
    return n <= RADIX and n % 2 == 0 and distance % 2 == 1 and 2 < distance < n - 2


def send(distance, chunks):
    n = lax.axis_size("dp")
    if distance == 0:
        return list(chunks)

    def route(chunk, step_of):
        return lax.ppermute(chunk, "dp", [(i, step_of(i) % n) for i in range(n)])

    def direct(chunk):
        return route(chunk, lambda i: i + distance)

    if not two_ways(distance, n):
        return [direct(c) for c in chunks]
    pairs = n // 2
    far, near = (distance + 1) // 2, (distance - 1) // 2
    odd_is_far = min(far, pairs - far) > min(near, pairs - near)
    far_side = 1 if odd_is_far else 0
    rest = distance + 1 if odd_is_far else distance - 1
    *chunks, halfway, final = chunks
    first, *chunks, final = [direct(c) for c in (*chunks, final)]
    halfway = route(halfway, lambda i: i ^ 1 if i % 2 == far_side else i + distance)
    first, _ = lax.optimization_barrier((first, halfway))
    halfway = route(halfway, lambda i: i if i % 2 == far_side else i + rest)
    return [first, *chunks, halfway, final]


def offset_digits(n):
    digits = []
    place = 1
    while place < n:
        digits.append((place, min(RADIX, -(-n // place))))
        place *= RADIX
    return digits


def quotient(value, by):
    if by & (by - 1) == 0:
        return lax.shift_right_logical(value, by.bit_length() - 1)
    return lax.div(value, by)


def local(new_pages, page_dest, resident, queries, page_table, cross_len):
    n_groups = lax.axis_size("dp")
    cap, tokens, _ = new_pages.shape
    d = HEAD_DIM
    heads = queries.shape[1] // d
    n_res = resident.shape[0]
    offset = quotient(page_dest[0], cap)

    def bias_of(page_table, cross_len):
        slots = jnp.arange(n_res + cap, dtype=jnp.int32)
        within = jnp.arange(page_table.shape[1], dtype=jnp.int32)[None, :] < cross_len[:, None]
        member = (page_table[:, :, None] == slots[None, None, :]) & within[:, :, None]
        bias = jnp.where(jnp.any(member, axis=1), 0.0, -jnp.inf).astype(jnp.float32)
        return jnp.repeat(bias, tokens, axis=1)

    blocks = [((2 * h - 1) * d, 2 * d) for h in range(1, heads)] + [((2 * heads - 1) * d, d)]

    digits = offset_digits(n_groups)
    last = len(digits) - 1

    def step(distance, index, carry, new_pages, page_dest, resident, queries, page_table, cross_len):
        if index == 0:
            order = list(range(len(blocks)))
            if two_ways(distance, n_groups):
                order.insert(0, order.pop(-2))
            after = new_pages[:, :, :d]
            carry = [after] + [None] * len(blocks)
            for c in order:
                after = carry[c + 1] = stage(new_pages, page_dest, *blocks[c], after)
        carry = send(distance, carry)
        if index < last:
            return tuple(carry)
        source = lax.rem(lax.axis_index("dp") - quotient(page_dest[0], cap) + n_groups, n_groups)
        slots = lax.rem(lax.dynamic_slice_in_dim(page_dest, source * cap, cap), cap)
        return attend(carry, resident, queries, bias_of(page_table, cross_len), slots)

    carry = ()
    for index, (place, base) in enumerate(digits):
        digit = quotient(offset, place)
        first = 1 if last == 0 else 0
        if index < last:
            digit = lax.rem(digit, base)
        carry = lax.switch(
            digit - first,
            [functools.partial(step, k * place, index) for k in range(first, base)],
            carry, new_pages, page_dest, resident, queries, page_table, cross_len,
        )
    return carry


def solution(mesh):
    return jax.shard_map(
        local,
        mesh=mesh,
        in_specs=(
            P("dp", None, "tensor"),
            P(),
            P("dp", None, "tensor"),
            P("dp", "tensor"),
            P("dp", None),
            P("dp"),
        ),
        out_specs=(P("dp", None, "tensor"), P("dp", "tensor")),
        check_vma=False,
    )
```

```python
import functools
import math

import jax
import jax.numpy as jnp
from jax import lax
from jax.experimental import pallas as pl
from jax.experimental.pallas import tpu as pltpu
from jax.sharding import PartitionSpec as P

HEAD_DIM = 256
RADIX = 8
VMEM_LIMIT = 8 * 1024 * 1024
GROUP = 2
LARGE_GROUP = 4


def stage_kernel(start, dest_ref, pages_ref, _, out_ref, sems):
    cap = pages_ref.shape[0]
    first = lax.axis_index("dp") * cap

    def copy(j):
        source = pages_ref.at[j, :, pl.ds(start, out_ref.shape[2])]
        slot = lax.rem(dest_ref[first + j], cap)
        return pltpu.make_async_copy(source, out_ref.at[slot], sems.at[j])

    pl.loop(0, cap)(lambda j: copy(j).start())
    pl.loop(0, cap)(lambda j: copy(j).wait())


def stage(new_pages, page_dest, start, width, after):
    cap, tokens, _ = new_pages.shape
    return pl.pallas_call(
        functools.partial(stage_kernel, start),
        in_specs=[
            pl.BlockSpec(memory_space=pltpu.SMEM),
            pl.BlockSpec(memory_space=pl.ANY),
            pl.BlockSpec(memory_space=pl.ANY),
        ],
        out_specs=pl.BlockSpec(memory_space=pltpu.VMEM),
        out_shape=jax.ShapeDtypeStruct((cap, tokens, width), new_pages.dtype),
        scratch_shapes=[pltpu.SemaphoreType.DMA((cap,))],
        cost_estimate=pl.CostEstimate(
            flops=0, bytes_accessed=4 * cap * tokens * width, transcendentals=0
        ),
    )(page_dest, new_pages, after)


def nt_dot(a, b):
    return lax.dot_general(a, b, (((1,), (1,)), ((), ())), preferred_element_type=jnp.float32)


def dot(a, b):
    return jnp.dot(a, b, preferred_element_type=jnp.float32)


def page_rows(ref, first, pages, start, width):
    block = ref[pl.ds(first, pages), :, start : start + width]
    return block.reshape(pages * ref.shape[1], width)


def weigh(most, q_ref, bias_ref, res_ref, keys_ref, start, scores_ref, slots_ref=None):
    d = q_ref.shape[1]
    n_res, tokens, _ = res_ref.shape
    q = q_ref[...]

    def score(ref, i, group, column, to):
        columns = pl.ds(pl.multiple_of(to * tokens, tokens), group * tokens)
        keys = page_rows(ref, i * group, group, column, d)
        scores_ref[:, columns] = nt_dot(q, keys) + bias_ref[:, columns]

    group = math.gcd(n_res, most)
    pl.loop(0, n_res // group)(lambda i: score(res_ref, i, group, 0, i * group))
    cap = keys_ref.shape[0]
    if slots_ref is None:
        group = math.gcd(cap, most)
        pl.loop(0, cap // group)(
            lambda i: score(keys_ref, i, group, start, n_res + i * group)
        )
    else:
        pl.loop(0, cap)(lambda i: score(keys_ref, i, 1, start, n_res + slots_ref[i]))
    scores = scores_ref[...]
    prob = jnp.exp(scores - jnp.max(scores, axis=1, keepdims=True))
    scores_ref[...] = prob
    return jnp.sum(prob, axis=1, keepdims=True)


def begin_head(
    most, q_ref, bias_ref, res_ref, keys_ref, start, scores_ref, out_refs, slots_ref=None
):
    weights_ref, summed_ref, total_ref = out_refs
    d = q_ref.shape[1]
    n_res, tokens, _ = res_ref.shape
    total = weigh(most, q_ref, bias_ref, res_ref, keys_ref, start, scores_ref, slots_ref)
    total_ref[...] = jnp.broadcast_to(total, total_ref.shape)
    weights_ref[...] = scores_ref[:, n_res * tokens :].astype(weights_ref.dtype)
    group = math.gcd(n_res, most)

    def add(i, summed):
        columns = pl.ds(pl.multiple_of(i * group * tokens, tokens), group * tokens)
        early = scores_ref[:, columns].astype(weights_ref.dtype)
        return summed + dot(early, page_rows(res_ref, i * group, group, d, d))

    zero = jnp.zeros(summed_ref.shape, jnp.float32)
    summed_ref[...] = lax.fori_loop(0, n_res // group, add, zero)


def first_kernel(
    most, slots_ref, q_ref, bias_ref, res_ref, keys_ref,
    arrived_ref, weights_ref, summed_ref, total_ref, scores_ref, sems,
):
    cap = keys_ref.shape[0]

    def copy(j):
        target = arrived_ref.at[slots_ref[j], :, pl.ds(0, q_ref.shape[1])]
        return pltpu.make_async_copy(keys_ref.at[j], target, sems.at[j])

    pl.loop(0, cap)(lambda j: copy(j).start())
    out_refs = (weights_ref, summed_ref, total_ref)
    begin_head(most, q_ref, bias_ref, res_ref, keys_ref, 0, scores_ref, out_refs, slots_ref)
    pl.loop(0, cap)(lambda j: copy(j).wait())


def middle_kernel(
    most, start, q_ref, bias_ref, res_ref, late_ref,
    old_weights_ref, old_summed_ref, old_total_ref, *rest,
):
    arrived_ref, context_ref, weights_ref, summed_ref, total_ref, scores_ref, sems = rest[-7:]
    cap, _, width = late_ref.shape
    d = q_ref.shape[1]
    group = math.gcd(cap, most)

    def copy(j):
        target = arrived_ref.at[j, :, pl.ds(start, width)]
        return pltpu.make_async_copy(late_ref.at[j], target, sems.at[j])

    pl.loop(0, cap)(lambda j: copy(j).start())

    def add(i, summed):
        tokens = group * late_ref.shape[1]
        weights = old_weights_ref[:, pl.ds(pl.multiple_of(i * tokens, tokens), tokens)]
        return summed + dot(weights, page_rows(late_ref, i * group, group, 0, d))

    summed = lax.fori_loop(0, cap // group, add, old_summed_ref[...])
    context_ref[...] = (summed / old_total_ref[...]).astype(context_ref.dtype)
    out_refs = (weights_ref, summed_ref, total_ref)
    begin_head(most, q_ref, bias_ref, res_ref, late_ref, d, scores_ref, out_refs)
    pl.loop(0, cap)(lambda j: copy(j).wait())


def last_kernel(start, weights_ref, summed_ref, total_ref, late_ref, *rest):
    arrived_ref, context_ref, sem, held, head, in_sems, out_sems = rest[-7:]
    pages, tokens, width = late_ref.shape
    parts = in_sems.shape[0]
    size = pages // parts

    def part(ref, i):
        return ref.at[pl.ds(i * size, size)]

    def copy_in(i):
        return pltpu.make_async_copy(part(late_ref, i), part(held, i), in_sems.at[i])

    def copy_out(i):
        target = part(arrived_ref, i).at[:, :, pl.ds(start, width)]
        return pltpu.make_async_copy(part(held, i), target, out_sems.at[i])

    for i in range(parts):
        copy_in(i).start()
    summed = summed_ref[...]
    span = size * tokens
    for i in range(parts):
        copy_in(i).wait()
        copy_out(i).start()
        block = held[i * size : (i + 1) * size].reshape(span, width)
        summed += dot(weights_ref[:, i * span : (i + 1) * span], block)
    head[...] = (summed / total_ref[...]).astype(head.dtype)
    columns = pl.ds((start - width) // 2, width)
    finish = pltpu.make_async_copy(head, context_ref.at[:, columns], sem)
    finish.start()
    for i in range(parts):
        copy_out(i).wait()
    finish.wait()


def whole(array):
    return pl.BlockSpec(array.shape, lambda i: (0,) * array.ndim)


def attend(most, chunks, resident, queries, bias, slots):
    d = HEAD_DIM
    requests, width = queries.shape
    last = width // d - 1
    n_res, tokens, _ = resident.shape
    cap = chunks[0].shape[0]
    pool = (n_res + cap) * tokens
    in_hbm = pl.BlockSpec(memory_space=pltpu.HBM)
    in_vmem = pl.BlockSpec(memory_space=pltpu.VMEM)
    anywhere = pl.BlockSpec(memory_space=pl.ANY)
    arrived_shape = jax.ShapeDtypeStruct((cap, tokens, 2 * width), resident.dtype)
    context_shape = jax.ShapeDtypeStruct((requests, width), jnp.bfloat16)
    parts_shape = [
        jax.ShapeDtypeStruct((requests, cap * tokens), jnp.bfloat16),
        jax.ShapeDtypeStruct((requests, d), jnp.float32),
        jax.ShapeDtypeStruct((requests, d), jnp.float32),
    ]
    scratch = [pltpu.VMEM((requests, pool), jnp.float32), pltpu.SemaphoreType.DMA((cap,))]
    params = pltpu.CompilerParams(vmem_limit_bytes=VMEM_LIMIT)
    cost = pl.CostEstimate(
        flops=4 * requests * pool * d,
        bytes_accessed=6 * pool * d,
        transcendentals=requests * pool,
    )

    def head_specs(h):
        return [
            pl.BlockSpec((requests, d), lambda i: (0, h)),
            whole(bias),
            pl.BlockSpec((n_res, tokens, 2 * d), lambda i: (0, 0, h)),
        ]

    arrived, *parts = pl.pallas_call(
        functools.partial(first_kernel, most),
        grid=(1,),
        in_specs=[pl.BlockSpec(memory_space=pltpu.SMEM), *head_specs(0), whole(chunks[0])],
        out_specs=[in_hbm, *(whole(x) for x in parts_shape)],
        out_shape=[arrived_shape, *parts_shape],
        scratch_shapes=scratch,
        compiler_params=params,
        cost_estimate=cost,
    )(slots, queries, bias, resident, chunks[0])
    context = None
    pieces = [(c, k) for c in chunks[1:-1] for k in range(c.shape[2] // (2 * d))]
    for h, (late, piece) in enumerate(pieces, 1):
        carried = [arrived] if context is None else [arrived, context]
        arrived, context, *parts = pl.pallas_call(
            functools.partial(middle_kernel, most, (2 * h - 1) * d),
            grid=(1,),
            in_specs=[
                *head_specs(h),
                pl.BlockSpec((cap, tokens, 2 * d), lambda i, piece=piece: (0, 0, piece)),
                *(whole(x) for x in parts),
                *[in_hbm, anywhere][: len(carried)],
            ],
            out_specs=[
                in_hbm,
                pl.BlockSpec((requests, d), lambda i, h=h: (0, h - 1)),
                *(whole(x) for x in parts_shape),
            ],
            out_shape=[arrived_shape, context_shape, *parts_shape],
            scratch_shapes=scratch,
            input_output_aliases={7 + i: i for i in range(len(carried))},
            compiler_params=params,
            cost_estimate=cost,
        )(queries, bias, resident, late, *parts, *carried)
    late = chunks[-1]
    n_parts = cap // math.gcd(cap, 2)
    sems = pltpu.SemaphoreType.DMA((n_parts,))
    return pl.pallas_call(
        functools.partial(last_kernel, (2 * last + 1) * d),
        in_specs=[in_vmem, in_vmem, in_vmem, anywhere, in_hbm, in_hbm],
        out_specs=[in_hbm, in_hbm],
        out_shape=[arrived_shape, context_shape],
        scratch_shapes=[
            pltpu.SemaphoreType.DMA,
            pltpu.VMEM(late.shape, late.dtype),
            pltpu.VMEM((requests, d), context.dtype),
            sems,
            sems,
        ],
        input_output_aliases={4: 0, 5: 1},
        compiler_params=params,
        cost_estimate=pl.CostEstimate(
            flops=2 * requests * cap * tokens * d,
            bytes_accessed=4 * cap * tokens * d,
            transcendentals=0,
        ),
    )(*parts, late, arrived, context)


def two_ways(distance, n):
    return n <= RADIX and n % 2 == 0 and distance % 2 == 1 and 2 < distance < n - 2


def send(distance, chunks):
    n = lax.axis_size("dp")
    if distance == 0:
        return list(chunks)

    def route(chunk, step_of):
        return lax.ppermute(chunk, "dp", [(i, step_of(i) % n) for i in range(n)])

    def direct(chunk):
        return route(chunk, lambda i: i + distance)

    if not two_ways(distance, n):
        return [direct(c) for c in chunks]
    pairs = n // 2
    far, near = (distance + 1) // 2, (distance - 1) // 2
    odd_is_far = min(far, pairs - far) > min(near, pairs - near)
    far_side = 1 if odd_is_far else 0
    rest = distance + 1 if odd_is_far else distance - 1
    *chunks, halfway, final = chunks
    first, *chunks, final = [direct(c) for c in (*chunks, final)]
    halfway = route(halfway, lambda i: i ^ 1 if i % 2 == far_side else i + distance)
    first, _ = lax.optimization_barrier((first, halfway))
    halfway = route(halfway, lambda i: i if i % 2 == far_side else i + rest)
    return [first, *chunks, halfway, final]


def offset_digits(n):
    digits = []
    place = 1
    while place < n:
        digits.append((place, min(RADIX, -(-n // place))))
        place *= RADIX
    return digits


def quotient(value, by):
    if by & (by - 1) == 0:
        return lax.shift_right_logical(value, by.bit_length() - 1)
    return lax.div(value, by)


def local(new_pages, page_dest, resident, queries, page_table, cross_len):
    n_groups = lax.axis_size("dp")
    cap, tokens, _ = new_pages.shape
    d = HEAD_DIM
    heads = queries.shape[1] // d
    n_res = resident.shape[0]
    offset = quotient(page_dest[0], cap)

    def bias_of(page_table, cross_len):
        slots = jnp.arange(n_res + cap, dtype=jnp.int32)
        within = jnp.arange(page_table.shape[1], dtype=jnp.int32)[None, :] < cross_len[:, None]
        member = (page_table[:, :, None] == slots[None, None, :]) & within[:, :, None]
        bias = jnp.where(jnp.any(member, axis=1), 0.0, -jnp.inf).astype(jnp.float32)
        return jnp.repeat(bias, tokens, axis=1)

    blocks = [((2 * h - 1) * d, 2 * d) for h in range(1, heads)] + [((2 * heads - 1) * d, d)]

    digits = offset_digits(n_groups)
    last = len(digits) - 1

    def step(distance, index, carry, new_pages, page_dest, resident, queries, page_table, cross_len):
        if index == 0:
            order = list(range(len(blocks)))
            if two_ways(distance, n_groups):
                order.insert(0, order.pop(-2))
            after = new_pages[:, :, :d]
            carry = [after] + [None] * len(blocks)
            for c in order:
                after = carry[c + 1] = stage(new_pages, page_dest, *blocks[c], after)
        carry = send(distance, carry)
        if index < last:
            return tuple(carry)
        source = lax.rem(lax.axis_index("dp") - quotient(page_dest[0], cap) + n_groups, n_groups)
        slots = lax.rem(lax.dynamic_slice_in_dim(page_dest, source * cap, cap), cap)
        most = LARGE_GROUP if two_ways(distance, n_groups) else GROUP
        return attend(most, carry, resident, queries, bias_of(page_table, cross_len), slots)

    carry = ()
    for index, (place, base) in enumerate(digits):
        digit = quotient(offset, place)
        first = 1 if last == 0 else 0
        if index < last:
            digit = lax.rem(digit, base)
        carry = lax.switch(
            digit - first,
            [functools.partial(step, k * place, index) for k in range(first, base)],
            carry, new_pages, page_dest, resident, queries, page_table, cross_len,
        )
    return carry


def solution(mesh):
    return jax.shard_map(
        local,
        mesh=mesh,
        in_specs=(
            P("dp", None, "tensor"),
            P(),
            P("dp", None, "tensor"),
            P("dp", "tensor"),
            P("dp", None),
            P("dp"),
        ),
        out_specs=(P("dp", None, "tensor"), P("dp", "tensor")),
        check_vma=False,
    )
```

```python
import functools
import math

import jax
import jax.numpy as jnp
from jax import lax
from jax.experimental import pallas as pl
from jax.experimental.pallas import tpu as pltpu
from jax.sharding import PartitionSpec as P

HEAD_DIM = 256
RADIX = 8
VMEM_LIMIT = 8 * 1024 * 1024
GROUP = 1
LARGE_GROUP = 4


def stage_kernel(start, dest_ref, pages_ref, _, out_ref, sems):
    cap = pages_ref.shape[0]
    first = lax.axis_index("dp") * cap

    def copy(j):
        source = pages_ref.at[j, :, pl.ds(start, out_ref.shape[2])]
        slot = lax.rem(dest_ref[first + j], cap)
        return pltpu.make_async_copy(source, out_ref.at[slot], sems.at[j])

    pl.loop(0, cap)(lambda j: copy(j).start())
    pl.loop(0, cap)(lambda j: copy(j).wait())


def stage(new_pages, page_dest, start, width, after):
    cap, tokens, _ = new_pages.shape
    return pl.pallas_call(
        functools.partial(stage_kernel, start),
        in_specs=[
            pl.BlockSpec(memory_space=pltpu.SMEM),
            pl.BlockSpec(memory_space=pl.ANY),
            pl.BlockSpec(memory_space=pl.ANY),
        ],
        out_specs=pl.BlockSpec(memory_space=pltpu.VMEM),
        out_shape=jax.ShapeDtypeStruct((cap, tokens, width), new_pages.dtype),
        scratch_shapes=[pltpu.SemaphoreType.DMA((cap,))],
        cost_estimate=pl.CostEstimate(
            flops=0, bytes_accessed=4 * cap * tokens * width, transcendentals=0
        ),
    )(page_dest, new_pages, after)


def nt_dot(a, b):
    return lax.dot_general(a, b, (((1,), (1,)), ((), ())), preferred_element_type=jnp.float32)


def dot(a, b):
    return jnp.dot(a, b, preferred_element_type=jnp.float32)


def page_rows(ref, first, pages, start, width):
    block = ref[pl.ds(first, pages), :, start : start + width]
    return block.reshape(pages * ref.shape[1], width)


def weigh(most, q_ref, bias_ref, res_ref, keys_ref, start, scores_ref, slots_ref=None):
    d = q_ref.shape[1]
    n_res, tokens, _ = res_ref.shape
    q = q_ref[...]

    def score(ref, i, group, column, to):
        columns = pl.ds(pl.multiple_of(to * tokens, tokens), group * tokens)
        keys = page_rows(ref, i * group, group, column, d)
        scores_ref[:, columns] = nt_dot(q, keys) + bias_ref[:, columns]

    group = math.gcd(n_res, most)
    pl.loop(0, n_res // group)(lambda i: score(res_ref, i, group, 0, i * group))
    cap = keys_ref.shape[0]
    if slots_ref is None:
        group = math.gcd(cap, most)
        pl.loop(0, cap // group)(
            lambda i: score(keys_ref, i, group, start, n_res + i * group)
        )
    else:
        pl.loop(0, cap)(lambda i: score(keys_ref, i, 1, start, n_res + slots_ref[i]))
    scores = scores_ref[...]
    prob = jnp.exp(scores - jnp.max(scores, axis=1, keepdims=True))
    scores_ref[...] = prob
    return jnp.sum(prob, axis=1, keepdims=True)


def begin_head(
    most, q_ref, bias_ref, res_ref, keys_ref, start, scores_ref, out_refs, slots_ref=None
):
    weights_ref, summed_ref, total_ref = out_refs
    d = q_ref.shape[1]
    n_res, tokens, _ = res_ref.shape
    total = weigh(most, q_ref, bias_ref, res_ref, keys_ref, start, scores_ref, slots_ref)
    total_ref[...] = jnp.broadcast_to(total, total_ref.shape)
    weights_ref[...] = scores_ref[:, n_res * tokens :].astype(weights_ref.dtype)
    group = math.gcd(n_res, most)

    def add(i, summed):
        columns = pl.ds(pl.multiple_of(i * group * tokens, tokens), group * tokens)
        early = scores_ref[:, columns].astype(weights_ref.dtype)
        return summed + dot(early, page_rows(res_ref, i * group, group, d, d))

    zero = jnp.zeros(summed_ref.shape, jnp.float32)
    summed_ref[...] = lax.fori_loop(0, n_res // group, add, zero)


def first_kernel(
    most, slots_ref, q_ref, bias_ref, res_ref, keys_ref,
    arrived_ref, weights_ref, summed_ref, total_ref, scores_ref, sems,
):
    cap = keys_ref.shape[0]

    def copy(j):
        target = arrived_ref.at[slots_ref[j], :, pl.ds(0, q_ref.shape[1])]
        return pltpu.make_async_copy(keys_ref.at[j], target, sems.at[j])

    pl.loop(0, cap)(lambda j: copy(j).start())
    out_refs = (weights_ref, summed_ref, total_ref)
    begin_head(most, q_ref, bias_ref, res_ref, keys_ref, 0, scores_ref, out_refs, slots_ref)
    pl.loop(0, cap)(lambda j: copy(j).wait())


def middle_kernel(
    most, start, q_ref, bias_ref, res_ref, late_ref,
    old_weights_ref, old_summed_ref, old_total_ref, *rest,
):
    arrived_ref, context_ref, weights_ref, summed_ref, total_ref, scores_ref, sems = rest[-7:]
    cap, _, width = late_ref.shape
    d = q_ref.shape[1]
    group = math.gcd(cap, most)

    def copy(j):
        target = arrived_ref.at[j, :, pl.ds(start, width)]
        return pltpu.make_async_copy(late_ref.at[j], target, sems.at[j])

    pl.loop(0, cap)(lambda j: copy(j).start())

    def add(i, summed):
        tokens = group * late_ref.shape[1]
        weights = old_weights_ref[:, pl.ds(pl.multiple_of(i * tokens, tokens), tokens)]
        return summed + dot(weights, page_rows(late_ref, i * group, group, 0, d))

    summed = lax.fori_loop(0, cap // group, add, old_summed_ref[...])
    context_ref[...] = (summed / old_total_ref[...]).astype(context_ref.dtype)
    out_refs = (weights_ref, summed_ref, total_ref)
    begin_head(most, q_ref, bias_ref, res_ref, late_ref, d, scores_ref, out_refs)
    pl.loop(0, cap)(lambda j: copy(j).wait())


def last_kernel(start, weights_ref, summed_ref, total_ref, late_ref, *rest):
    arrived_ref, context_ref, sem, held, head, in_sems, out_sems = rest[-7:]
    pages, tokens, width = late_ref.shape
    parts = in_sems.shape[0]
    size = pages // parts

    def part(ref, i):
        return ref.at[pl.ds(i * size, size)]

    def copy_in(i):
        return pltpu.make_async_copy(part(late_ref, i), part(held, i), in_sems.at[i])

    def copy_out(i):
        target = part(arrived_ref, i).at[:, :, pl.ds(start, width)]
        return pltpu.make_async_copy(part(held, i), target, out_sems.at[i])

    for i in range(parts):
        copy_in(i).start()
    summed = summed_ref[...]
    span = size * tokens
    for i in range(parts):
        copy_in(i).wait()
        copy_out(i).start()
        block = held[i * size : (i + 1) * size].reshape(span, width)
        summed += dot(weights_ref[:, i * span : (i + 1) * span], block)
    head[...] = (summed / total_ref[...]).astype(head.dtype)
    columns = pl.ds((start - width) // 2, width)
    finish = pltpu.make_async_copy(head, context_ref.at[:, columns], sem)
    finish.start()
    for i in range(parts):
        copy_out(i).wait()
    finish.wait()


def whole(array):
    return pl.BlockSpec(array.shape, lambda i: (0,) * array.ndim)


def attend(most, chunks, resident, queries, bias, slots):
    d = HEAD_DIM
    requests, width = queries.shape
    last = width // d - 1
    n_res, tokens, _ = resident.shape
    cap = chunks[0].shape[0]
    pool = (n_res + cap) * tokens
    in_hbm = pl.BlockSpec(memory_space=pltpu.HBM)
    in_vmem = pl.BlockSpec(memory_space=pltpu.VMEM)
    anywhere = pl.BlockSpec(memory_space=pl.ANY)
    arrived_shape = jax.ShapeDtypeStruct((cap, tokens, 2 * width), resident.dtype)
    context_shape = jax.ShapeDtypeStruct((requests, width), jnp.bfloat16)
    parts_shape = [
        jax.ShapeDtypeStruct((requests, cap * tokens), jnp.bfloat16),
        jax.ShapeDtypeStruct((requests, d), jnp.float32),
        jax.ShapeDtypeStruct((requests, d), jnp.float32),
    ]
    scratch = [pltpu.VMEM((requests, pool), jnp.float32), pltpu.SemaphoreType.DMA((cap,))]
    params = pltpu.CompilerParams(vmem_limit_bytes=VMEM_LIMIT)
    cost = pl.CostEstimate(
        flops=4 * requests * pool * d,
        bytes_accessed=6 * pool * d,
        transcendentals=requests * pool,
    )

    def head_specs(h):
        return [
            pl.BlockSpec((requests, d), lambda i: (0, h)),
            whole(bias),
            pl.BlockSpec((n_res, tokens, 2 * d), lambda i: (0, 0, h)),
        ]

    arrived, *parts = pl.pallas_call(
        functools.partial(first_kernel, most),
        grid=(1,),
        in_specs=[pl.BlockSpec(memory_space=pltpu.SMEM), *head_specs(0), whole(chunks[0])],
        out_specs=[in_hbm, *(whole(x) for x in parts_shape)],
        out_shape=[arrived_shape, *parts_shape],
        scratch_shapes=scratch,
        compiler_params=params,
        cost_estimate=cost,
    )(slots, queries, bias, resident, chunks[0])
    context = None
    pieces = [(c, k) for c in chunks[1:-1] for k in range(c.shape[2] // (2 * d))]
    for h, (late, piece) in enumerate(pieces, 1):
        carried = [arrived] if context is None else [arrived, context]
        arrived, context, *parts = pl.pallas_call(
            functools.partial(middle_kernel, most, (2 * h - 1) * d),
            grid=(1,),
            in_specs=[
                *head_specs(h),
                pl.BlockSpec((cap, tokens, 2 * d), lambda i, piece=piece: (0, 0, piece)),
                *(whole(x) for x in parts),
                *[in_hbm, anywhere][: len(carried)],
            ],
            out_specs=[
                in_hbm,
                pl.BlockSpec((requests, d), lambda i, h=h: (0, h - 1)),
                *(whole(x) for x in parts_shape),
            ],
            out_shape=[arrived_shape, context_shape, *parts_shape],
            scratch_shapes=scratch,
            input_output_aliases={7 + i: i for i in range(len(carried))},
            compiler_params=params,
            cost_estimate=cost,
        )(queries, bias, resident, late, *parts, *carried)
    late = chunks[-1]
    n_parts = cap // math.gcd(cap, 2)
    sems = pltpu.SemaphoreType.DMA((n_parts,))
    return pl.pallas_call(
        functools.partial(last_kernel, (2 * last + 1) * d),
        in_specs=[in_vmem, in_vmem, in_vmem, anywhere, in_hbm, in_hbm],
        out_specs=[in_hbm, in_hbm],
        out_shape=[arrived_shape, context_shape],
        scratch_shapes=[
            pltpu.SemaphoreType.DMA,
            pltpu.VMEM(late.shape, late.dtype),
            pltpu.VMEM((requests, d), context.dtype),
            sems,
            sems,
        ],
        input_output_aliases={4: 0, 5: 1},
        compiler_params=params,
        cost_estimate=pl.CostEstimate(
            flops=2 * requests * cap * tokens * d,
            bytes_accessed=4 * cap * tokens * d,
            transcendentals=0,
        ),
    )(*parts, late, arrived, context)


def two_ways(distance, n):
    return n <= RADIX and n % 2 == 0 and distance % 2 == 1 and 2 < distance < n - 2


def send(distance, chunks):
    n = lax.axis_size("dp")
    if distance == 0:
        return list(chunks)

    def route(chunk, step_of):
        return lax.ppermute(chunk, "dp", [(i, step_of(i) % n) for i in range(n)])

    def direct(chunk):
        return route(chunk, lambda i: i + distance)

    if not two_ways(distance, n):
        return [direct(c) for c in chunks]
    pairs = n // 2
    far, near = (distance + 1) // 2, (distance - 1) // 2
    odd_is_far = min(far, pairs - far) > min(near, pairs - near)
    far_side = 1 if odd_is_far else 0
    rest = distance + 1 if odd_is_far else distance - 1
    *chunks, halfway, final = chunks
    first, *chunks, final = [direct(c) for c in (*chunks, final)]
    halfway = route(halfway, lambda i: i ^ 1 if i % 2 == far_side else i + distance)
    first, _ = lax.optimization_barrier((first, halfway))
    halfway = route(halfway, lambda i: i if i % 2 == far_side else i + rest)
    return [first, *chunks, halfway, final]


def offset_digits(n):
    digits = []
    place = 1
    while place < n:
        digits.append((place, min(RADIX, -(-n // place))))
        place *= RADIX
    return digits


def quotient(value, by):
    if by & (by - 1) == 0:
        return lax.shift_right_logical(value, by.bit_length() - 1)
    return lax.div(value, by)


def local(new_pages, page_dest, resident, queries, page_table, cross_len):
    n_groups = lax.axis_size("dp")
    cap, tokens, _ = new_pages.shape
    d = HEAD_DIM
    heads = queries.shape[1] // d
    n_res = resident.shape[0]
    offset = quotient(page_dest[0], cap)

    def bias_of(page_table, cross_len):
        slots = jnp.arange(n_res + cap, dtype=jnp.int32)
        within = jnp.arange(page_table.shape[1], dtype=jnp.int32)[None, :] < cross_len[:, None]
        member = (page_table[:, :, None] == slots[None, None, :]) & within[:, :, None]
        bias = jnp.where(jnp.any(member, axis=1), 0.0, -jnp.inf).astype(jnp.float32)
        return jnp.repeat(bias, tokens, axis=1)

    blocks = [((2 * h - 1) * d, 2 * d) for h in range(1, heads)] + [((2 * heads - 1) * d, d)]

    digits = offset_digits(n_groups)
    last = len(digits) - 1

    def step(distance, index, carry, new_pages, page_dest, resident, queries, page_table, cross_len):
        if index == 0:
            order = list(range(len(blocks)))
            if two_ways(distance, n_groups):
                order.insert(0, order.pop(-2))
            after = new_pages[:, :, :d]
            carry = [after] + [None] * len(blocks)
            for c in order:
                after = carry[c + 1] = stage(new_pages, page_dest, *blocks[c], after)
        carry = send(distance, carry)
        if index < last:
            return tuple(carry)
        source = lax.rem(lax.axis_index("dp") - quotient(page_dest[0], cap) + n_groups, n_groups)
        slots = lax.rem(lax.dynamic_slice_in_dim(page_dest, source * cap, cap), cap)
        most = LARGE_GROUP if two_ways(distance, n_groups) else GROUP
        return attend(most, carry, resident, queries, bias_of(page_table, cross_len), slots)

    carry = ()
    for index, (place, base) in enumerate(digits):
        digit = quotient(offset, place)
        first = 1 if last == 0 else 0
        if index < last:
            digit = lax.rem(digit, base)
        carry = lax.switch(
            digit - first,
            [functools.partial(step, k * place, index) for k in range(first, base)],
            carry, new_pages, page_dest, resident, queries, page_table, cross_len,
        )
    return carry


def solution(mesh):
    return jax.shard_map(
        local,
        mesh=mesh,
        in_specs=(
            P("dp", None, "tensor"),
            P(),
            P("dp", None, "tensor"),
            P("dp", "tensor"),
            P("dp", None),
            P("dp"),
        ),
        out_specs=(P("dp", None, "tensor"), P("dp", "tensor")),
        check_vma=False,
    )
```

```python
import functools
import math

import jax
import jax.numpy as jnp
from jax import lax
from jax.experimental import pallas as pl
from jax.experimental.pallas import tpu as pltpu
from jax.sharding import PartitionSpec as P

HEAD_DIM = 256
RADIX = 8
VMEM_LIMIT = 8 * 1024 * 1024
GROUP = 1
LARGE_GROUP = 4


def stage_kernel(start, dest_ref, pages_ref, _, out_ref, sems):
    cap = pages_ref.shape[0]
    first = lax.axis_index("dp") * cap

    def copy(j):
        source = pages_ref.at[j, :, pl.ds(start, out_ref.shape[2])]
        slot = lax.rem(dest_ref[first + j], cap)
        return pltpu.make_async_copy(source, out_ref.at[slot], sems.at[j])

    pl.loop(0, cap)(lambda j: copy(j).start())
    pl.loop(0, cap)(lambda j: copy(j).wait())


def stage(new_pages, page_dest, start, width, after):
    cap, tokens, _ = new_pages.shape
    return pl.pallas_call(
        functools.partial(stage_kernel, start),
        in_specs=[
            pl.BlockSpec(memory_space=pltpu.SMEM),
            pl.BlockSpec(memory_space=pl.ANY),
            pl.BlockSpec(memory_space=pl.ANY),
        ],
        out_specs=pl.BlockSpec(memory_space=pltpu.VMEM),
        out_shape=jax.ShapeDtypeStruct((cap, tokens, width), new_pages.dtype),
        scratch_shapes=[pltpu.SemaphoreType.DMA((cap,))],
        cost_estimate=pl.CostEstimate(
            flops=0, bytes_accessed=4 * cap * tokens * width, transcendentals=0
        ),
    )(page_dest, new_pages, after)


def nt_dot(a, b):
    return lax.dot_general(a, b, (((1,), (1,)), ((), ())), preferred_element_type=jnp.float32)


def dot(a, b):
    return jnp.dot(a, b, preferred_element_type=jnp.float32)


def page_rows(ref, first, pages, start, width):
    block = ref[pl.ds(first, pages), :, start : start + width]
    return block.reshape(pages * ref.shape[1], width)


def weigh(most, q_ref, bias_ref, res_ref, keys_ref, start, scores_ref, slots_ref=None):
    d = q_ref.shape[1]
    n_res, tokens, _ = res_ref.shape
    q = q_ref[...]

    def score(ref, i, group, column, to):
        columns = pl.ds(pl.multiple_of(to * tokens, tokens), group * tokens)
        keys = page_rows(ref, i * group, group, column, d)
        scores_ref[:, columns] = nt_dot(q, keys) + bias_ref[:, columns]

    group = math.gcd(n_res, most)
    pl.loop(0, n_res // group)(lambda i: score(res_ref, i, group, 0, i * group))
    cap = keys_ref.shape[0]
    if slots_ref is None:
        group = math.gcd(cap, most)
        pl.loop(0, cap // group)(
            lambda i: score(keys_ref, i, group, start, n_res + i * group)
        )
    else:
        pl.loop(0, cap)(lambda i: score(keys_ref, i, 1, start, n_res + slots_ref[i]))
    scores = scores_ref[...]
    prob = jnp.exp(scores - jnp.max(scores, axis=1, keepdims=True))
    scores_ref[...] = prob
    return jnp.sum(prob, axis=1, keepdims=True)


def begin_head(
    most, q_ref, bias_ref, res_ref, keys_ref, start, scores_ref, out_refs, slots_ref=None
):
    weights_ref, summed_ref, total_ref = out_refs
    d = q_ref.shape[1]
    n_res, tokens, _ = res_ref.shape
    total = weigh(most, q_ref, bias_ref, res_ref, keys_ref, start, scores_ref, slots_ref)
    total_ref[...] = jnp.broadcast_to(total, total_ref.shape)
    weights_ref[...] = scores_ref[:, n_res * tokens :].astype(weights_ref.dtype)
    group = math.gcd(n_res, most)

    def add(i, summed):
        columns = pl.ds(pl.multiple_of(i * group * tokens, tokens), group * tokens)
        early = scores_ref[:, columns].astype(weights_ref.dtype)
        return summed + dot(early, page_rows(res_ref, i * group, group, d, d))

    zero = jnp.zeros(summed_ref.shape, jnp.float32)
    summed_ref[...] = lax.fori_loop(0, n_res // group, add, zero)


def first_kernel(
    most, slots_ref, q_ref, bias_ref, res_ref, keys_ref,
    arrived_ref, weights_ref, summed_ref, total_ref, scores_ref, sems,
):
    cap = keys_ref.shape[0]

    def copy(j):
        target = arrived_ref.at[slots_ref[j], :, pl.ds(0, q_ref.shape[1])]
        return pltpu.make_async_copy(keys_ref.at[j], target, sems.at[j])

    pl.loop(0, cap)(lambda j: copy(j).start())
    out_refs = (weights_ref, summed_ref, total_ref)
    begin_head(most, q_ref, bias_ref, res_ref, keys_ref, 0, scores_ref, out_refs, slots_ref)
    pl.loop(0, cap)(lambda j: copy(j).wait())


def middle_kernel(
    most, start, q_ref, bias_ref, res_ref, late_ref,
    old_weights_ref, old_summed_ref, old_total_ref, *rest,
):
    arrived_ref, context_ref, weights_ref, summed_ref, total_ref, scores_ref, sems = rest[-7:]
    cap, _, width = late_ref.shape
    d = q_ref.shape[1]
    group = math.gcd(cap, most)

    def copy(j):
        target = arrived_ref.at[j, :, pl.ds(start, width)]
        return pltpu.make_async_copy(late_ref.at[j], target, sems.at[j])

    pl.loop(0, cap)(lambda j: copy(j).start())

    def add(i, summed):
        tokens = group * late_ref.shape[1]
        weights = old_weights_ref[:, pl.ds(pl.multiple_of(i * tokens, tokens), tokens)]
        return summed + dot(weights, page_rows(late_ref, i * group, group, 0, d))

    summed = lax.fori_loop(0, cap // group, add, old_summed_ref[...])
    context_ref[...] = (summed / old_total_ref[...]).astype(context_ref.dtype)
    out_refs = (weights_ref, summed_ref, total_ref)
    begin_head(most, q_ref, bias_ref, res_ref, late_ref, d, scores_ref, out_refs)
    pl.loop(0, cap)(lambda j: copy(j).wait())


def last_kernel(start, weights_ref, summed_ref, total_ref, late_ref, *rest):
    arrived_ref, context_ref, sem, held, head, in_sems, out_sems = rest[-7:]
    pages, tokens, width = late_ref.shape
    parts = in_sems.shape[0]
    size = pages // parts

    def part(ref, i):
        return ref.at[pl.ds(i * size, size)]

    def copy_in(i):
        return pltpu.make_async_copy(part(late_ref, i), part(held, i), in_sems.at[i])

    def copy_out(i):
        target = part(arrived_ref, i).at[:, :, pl.ds(start, width)]
        return pltpu.make_async_copy(part(held, i), target, out_sems.at[i])

    for i in range(parts):
        copy_in(i).start()
    summed = summed_ref[...]
    span = size * tokens
    for i in range(parts):
        copy_in(i).wait()
        copy_out(i).start()
        block = held[i * size : (i + 1) * size].reshape(span, width)
        summed += dot(weights_ref[:, i * span : (i + 1) * span], block)
    head[...] = (summed / total_ref[...]).astype(head.dtype)
    columns = pl.ds((start - width) // 2, width)
    finish = pltpu.make_async_copy(head, context_ref.at[:, columns], sem)
    finish.start()
    for i in range(parts):
        copy_out(i).wait()
    finish.wait()


def whole(array):
    return pl.BlockSpec(array.shape, lambda i: (0,) * array.ndim)


def attend(most, chunks, resident, queries, bias, slots):
    d = HEAD_DIM
    requests, width = queries.shape
    last = width // d - 1
    n_res, tokens, _ = resident.shape
    cap = chunks[0].shape[0]
    pool = (n_res + cap) * tokens
    in_hbm = pl.BlockSpec(memory_space=pltpu.HBM)
    in_vmem = pl.BlockSpec(memory_space=pltpu.VMEM)
    anywhere = pl.BlockSpec(memory_space=pl.ANY)
    arrived_shape = jax.ShapeDtypeStruct((cap, tokens, 2 * width), resident.dtype)
    context_shape = jax.ShapeDtypeStruct((requests, width), jnp.bfloat16)
    parts_shape = [
        jax.ShapeDtypeStruct((requests, cap * tokens), jnp.bfloat16),
        jax.ShapeDtypeStruct((requests, d), jnp.float32),
        jax.ShapeDtypeStruct((requests, d), jnp.float32),
    ]
    scratch = [pltpu.VMEM((requests, pool), jnp.float32), pltpu.SemaphoreType.DMA((cap,))]
    params = pltpu.CompilerParams(vmem_limit_bytes=VMEM_LIMIT)
    cost = pl.CostEstimate(
        flops=4 * requests * pool * d,
        bytes_accessed=6 * pool * d,
        transcendentals=requests * pool,
    )

    def head_specs(h):
        return [
            pl.BlockSpec((requests, d), lambda i: (0, h)),
            whole(bias),
            pl.BlockSpec((n_res, tokens, 2 * d), lambda i: (0, 0, h)),
        ]

    arrived, *parts = pl.pallas_call(
        functools.partial(first_kernel, most),
        grid=(1,),
        in_specs=[pl.BlockSpec(memory_space=pltpu.SMEM), *head_specs(0), whole(chunks[0])],
        out_specs=[in_hbm, *(whole(x) for x in parts_shape)],
        out_shape=[arrived_shape, *parts_shape],
        scratch_shapes=scratch,
        compiler_params=params,
        cost_estimate=cost,
    )(slots, queries, bias, resident, chunks[0])
    context = None
    pieces = [(c, k) for c in chunks[1:-1] for k in range(c.shape[2] // (2 * d))]
    for h, (late, piece) in enumerate(pieces, 1):
        carried = [arrived] if context is None else [arrived, context]
        arrived, context, *parts = pl.pallas_call(
            functools.partial(middle_kernel, most, (2 * h - 1) * d),
            grid=(1,),
            in_specs=[
                *head_specs(h),
                pl.BlockSpec((cap, tokens, 2 * d), lambda i, piece=piece: (0, 0, piece)),
                *(whole(x) for x in parts),
                *[in_hbm, anywhere][: len(carried)],
            ],
            out_specs=[
                in_hbm,
                pl.BlockSpec((requests, d), lambda i, h=h: (0, h - 1)),
                *(whole(x) for x in parts_shape),
            ],
            out_shape=[arrived_shape, context_shape, *parts_shape],
            scratch_shapes=scratch,
            input_output_aliases={7 + i: i for i in range(len(carried))},
            compiler_params=params,
            cost_estimate=cost,
        )(queries, bias, resident, late, *parts, *carried)
    late = chunks[-1]
    n_parts = cap // math.gcd(cap, 2)
    sems = pltpu.SemaphoreType.DMA((n_parts,))
    return pl.pallas_call(
        functools.partial(last_kernel, (2 * last + 1) * d),
        in_specs=[in_vmem, in_vmem, in_vmem, anywhere, in_hbm, in_hbm],
        out_specs=[in_hbm, in_hbm],
        out_shape=[arrived_shape, context_shape],
        scratch_shapes=[
            pltpu.SemaphoreType.DMA,
            pltpu.VMEM(late.shape, late.dtype),
            pltpu.VMEM((requests, d), context.dtype),
            sems,
            sems,
        ],
        input_output_aliases={4: 0, 5: 1},
        compiler_params=params,
        cost_estimate=pl.CostEstimate(
            flops=2 * requests * cap * tokens * d,
            bytes_accessed=4 * cap * tokens * d,
            transcendentals=0,
        ),
    )(*parts, late, arrived, context)


def two_ways(distance, n):
    return n <= RADIX and n % 2 == 0 and distance % 2 == 1 and 2 < distance < n - 2


def send(distance, chunks):
    n = lax.axis_size("dp")
    if distance == 0:
        return list(chunks)

    def route(chunk, step_of):
        return lax.ppermute(chunk, "dp", [(i, step_of(i) % n) for i in range(n)])

    def direct(chunk):
        return route(chunk, lambda i: i + distance)

    if not two_ways(distance, n):
        return [direct(c) for c in chunks]
    pairs = n // 2
    far, near = (distance + 1) // 2, (distance - 1) // 2
    odd_is_far = min(far, pairs - far) > min(near, pairs - near)
    far_side = 1 if odd_is_far else 0
    rest = distance + 1 if odd_is_far else distance - 1
    *chunks, halfway, final = chunks
    first, *chunks, final = [direct(c) for c in (*chunks, final)]
    halfway = route(halfway, lambda i: i ^ 1 if i % 2 == far_side else i + distance)
    first, _ = lax.optimization_barrier((first, halfway))
    halfway = route(halfway, lambda i: i if i % 2 == far_side else i + rest)
    return [first, *chunks, halfway, final]


def offset_digits(n):
    digits = []
    place = 1
    while place < n:
        digits.append((place, min(RADIX, -(-n // place))))
        place *= RADIX
    return digits


def quotient(value, by):
    if by & (by - 1) == 0:
        return lax.shift_right_logical(value, by.bit_length() - 1)
    return lax.div(value, by)


def local(new_pages, page_dest, resident, queries, page_table, cross_len):
    n_groups = lax.axis_size("dp")
    cap, tokens, _ = new_pages.shape
    d = HEAD_DIM
    heads = queries.shape[1] // d
    n_res = resident.shape[0]
    offset = quotient(page_dest[0], cap)

    def bias_of(page_table, cross_len):
        slots = jnp.arange(n_res + cap, dtype=jnp.int32)
        within = jnp.arange(page_table.shape[1], dtype=jnp.int32)[None, :] < cross_len[:, None]
        member = (page_table[:, :, None] == slots[None, None, :]) & within[:, :, None]
        bias = jnp.where(jnp.any(member, axis=1), 0.0, -jnp.inf).astype(jnp.float32)
        return jnp.repeat(bias, tokens, axis=1)

    blocks = [((2 * h - 1) * d, 2 * d) for h in range(1, heads)] + [((2 * heads - 1) * d, d)]

    digits = offset_digits(n_groups)
    last = len(digits) - 1

    def step(distance, index, carry, new_pages, page_dest, resident, queries, page_table, cross_len):
        if index == 0:
            order = list(range(len(blocks)))
            if two_ways(distance, n_groups):
                order.insert(0, order.pop(-2))
            (after,) = carry
            carry = [after] + [None] * len(blocks)
            for c in order:
                after = carry[c + 1] = stage(new_pages, page_dest, *blocks[c], after)
        carry = send(distance, carry)
        if index < last:
            return tuple(carry)
        source = lax.rem(lax.axis_index("dp") - quotient(page_dest[0], cap) + n_groups, n_groups)
        slots = lax.rem(lax.dynamic_slice_in_dim(page_dest, source * cap, cap), cap)
        most = LARGE_GROUP if two_ways(distance, n_groups) else GROUP
        return attend(most, carry, resident, queries, bias_of(page_table, cross_len), slots)

    carry = (lax.optimization_barrier(new_pages[:, :, :d]),)
    for index, (place, base) in enumerate(digits):
        digit = quotient(offset, place)
        first = 1 if last == 0 else 0
        if index < last:
            digit = lax.rem(digit, base)
        carry = lax.switch(
            digit - first,
            [functools.partial(step, k * place, index) for k in range(first, base)],
            carry, new_pages, page_dest, resident, queries, page_table, cross_len,
        )
    return carry


def solution(mesh):
    return jax.shard_map(
        local,
        mesh=mesh,
        in_specs=(
            P("dp", None, "tensor"),
            P(),
            P("dp", None, "tensor"),
            P("dp", "tensor"),
            P("dp", None),
            P("dp"),
        ),
        out_specs=(P("dp", None, "tensor"), P("dp", "tensor")),
        check_vma=False,
    )
```

```python
import functools
import math

import jax
import jax.numpy as jnp
from jax import lax
from jax.experimental import pallas as pl
from jax.experimental.pallas import tpu as pltpu
from jax.sharding import PartitionSpec as P

HEAD_DIM = 256
RADIX = 8
VMEM_LIMIT = 8 * 1024 * 1024
GROUP = 1
LARGE_GROUP = 4


def stage_kernel(start, dest_ref, pages_ref, _, out_ref, sems):
    cap = pages_ref.shape[0]
    first = lax.axis_index("dp") * cap

    def copy(j):
        source = pages_ref.at[j, :, pl.ds(start, out_ref.shape[2])]
        slot = lax.rem(dest_ref[first + j], cap)
        return pltpu.make_async_copy(source, out_ref.at[slot], sems.at[j])

    pl.loop(0, cap)(lambda j: copy(j).start())
    pl.loop(0, cap)(lambda j: copy(j).wait())


def stage(new_pages, page_dest, start, width, after):
    cap, tokens, _ = new_pages.shape
    return pl.pallas_call(
        functools.partial(stage_kernel, start),
        in_specs=[
            pl.BlockSpec(memory_space=pltpu.SMEM),
            pl.BlockSpec(memory_space=pl.ANY),
            pl.BlockSpec(memory_space=pl.ANY),
        ],
        out_specs=pl.BlockSpec(memory_space=pltpu.VMEM),
        out_shape=jax.ShapeDtypeStruct((cap, tokens, width), new_pages.dtype),
        scratch_shapes=[pltpu.SemaphoreType.DMA((cap,))],
        cost_estimate=pl.CostEstimate(
            flops=0, bytes_accessed=4 * cap * tokens * width, transcendentals=0
        ),
    )(page_dest, new_pages, after)


def nt_dot(a, b):
    return lax.dot_general(a, b, (((1,), (1,)), ((), ())), preferred_element_type=jnp.float32)


def dot(a, b):
    return jnp.dot(a, b, preferred_element_type=jnp.float32)


def page_rows(ref, first, pages, start, width):
    block = ref[pl.ds(first, pages), :, start : start + width]
    return block.reshape(pages * ref.shape[1], width)


def weigh(most, q_ref, bias_ref, res_ref, keys_ref, start, scores_ref, slots_ref=None):
    d = q_ref.shape[1]
    n_res, tokens, _ = res_ref.shape
    q = q_ref[...]

    def score(ref, i, group, column, to):
        columns = pl.ds(pl.multiple_of(to * tokens, tokens), group * tokens)
        keys = page_rows(ref, i * group, group, column, d)
        scores_ref[:, columns] = nt_dot(q, keys) + bias_ref[:, columns]

    group = math.gcd(n_res, most)
    pl.loop(0, n_res // group)(lambda i: score(res_ref, i, group, 0, i * group))
    cap = keys_ref.shape[0]
    if slots_ref is None:
        group = math.gcd(cap, most)
        pl.loop(0, cap // group)(
            lambda i: score(keys_ref, i, group, start, n_res + i * group)
        )
    else:
        pl.loop(0, cap)(lambda i: score(keys_ref, i, 1, start, n_res + slots_ref[i]))
    scores = scores_ref[...]
    prob = jnp.exp(scores - jnp.max(scores, axis=1, keepdims=True))
    scores_ref[...] = prob
    return jnp.sum(prob, axis=1, keepdims=True)


def begin_head(
    most, q_ref, bias_ref, res_ref, keys_ref, start, scores_ref, out_refs, slots_ref=None
):
    weights_ref, summed_ref, total_ref = out_refs
    d = q_ref.shape[1]
    n_res, tokens, _ = res_ref.shape
    total = weigh(most, q_ref, bias_ref, res_ref, keys_ref, start, scores_ref, slots_ref)
    total_ref[...] = jnp.broadcast_to(total, total_ref.shape)
    weights_ref[...] = scores_ref[:, n_res * tokens :].astype(weights_ref.dtype)
    group = math.gcd(n_res, most)

    def add(i, summed):
        columns = pl.ds(pl.multiple_of(i * group * tokens, tokens), group * tokens)
        early = scores_ref[:, columns].astype(weights_ref.dtype)
        return summed + dot(early, page_rows(res_ref, i * group, group, d, d))

    zero = jnp.zeros(summed_ref.shape, jnp.float32)
    summed_ref[...] = lax.fori_loop(0, n_res // group, add, zero)


def first_kernel(
    most, slots_ref, q_ref, bias_ref, res_ref, keys_ref,
    arrived_ref, weights_ref, summed_ref, total_ref, scores_ref, sems,
):
    cap = keys_ref.shape[0]

    def copy(j):
        target = arrived_ref.at[slots_ref[j], :, pl.ds(0, q_ref.shape[1])]
        return pltpu.make_async_copy(keys_ref.at[j], target, sems.at[j])

    pl.loop(0, cap)(lambda j: copy(j).start())
    out_refs = (weights_ref, summed_ref, total_ref)
    begin_head(most, q_ref, bias_ref, res_ref, keys_ref, 0, scores_ref, out_refs, slots_ref)
    pl.loop(0, cap)(lambda j: copy(j).wait())


def middle_kernel(
    most, start, q_ref, bias_ref, res_ref, late_ref,
    old_weights_ref, old_summed_ref, old_total_ref, *rest,
):
    arrived_ref, context_ref, weights_ref, summed_ref, total_ref, scores_ref, sems = rest[-7:]
    cap, _, width = late_ref.shape
    d = q_ref.shape[1]
    group = math.gcd(cap, most)

    def copy(j):
        target = arrived_ref.at[j, :, pl.ds(start, width)]
        return pltpu.make_async_copy(late_ref.at[j], target, sems.at[j])

    pl.loop(0, cap)(lambda j: copy(j).start())

    def add(i, summed):
        tokens = group * late_ref.shape[1]
        weights = old_weights_ref[:, pl.ds(pl.multiple_of(i * tokens, tokens), tokens)]
        return summed + dot(weights, page_rows(late_ref, i * group, group, 0, d))

    summed = lax.fori_loop(0, cap // group, add, old_summed_ref[...])
    context_ref[...] = (summed / old_total_ref[...]).astype(context_ref.dtype)
    out_refs = (weights_ref, summed_ref, total_ref)
    begin_head(most, q_ref, bias_ref, res_ref, late_ref, d, scores_ref, out_refs)
    pl.loop(0, cap)(lambda j: copy(j).wait())


def last_kernel(start, weights_ref, summed_ref, total_ref, late_ref, *rest):
    arrived_ref, context_ref, sem, held, head, in_sems, out_sems = rest[-7:]
    pages, tokens, width = late_ref.shape
    parts = in_sems.shape[0]
    size = pages // parts

    def part(ref, i):
        return ref.at[pl.ds(i * size, size)]

    def copy_in(i):
        return pltpu.make_async_copy(part(late_ref, i), part(held, i), in_sems.at[i])

    def copy_out(i):
        target = part(arrived_ref, i).at[:, :, pl.ds(start, width)]
        return pltpu.make_async_copy(part(held, i), target, out_sems.at[i])

    for i in range(parts):
        copy_in(i).start()
    summed = summed_ref[...]
    span = size * tokens
    for i in range(parts):
        copy_in(i).wait()
        copy_out(i).start()
        block = held[i * size : (i + 1) * size].reshape(span, width)
        summed += dot(weights_ref[:, i * span : (i + 1) * span], block)
    head[...] = (summed / total_ref[...]).astype(head.dtype)
    columns = pl.ds((start - width) // 2, width)
    finish = pltpu.make_async_copy(head, context_ref.at[:, columns], sem)
    finish.start()
    for i in range(parts):
        copy_out(i).wait()
    finish.wait()


def whole(array):
    return pl.BlockSpec(array.shape, lambda i: (0,) * array.ndim)


def attend(most, chunks, resident, queries, bias, slots):
    d = HEAD_DIM
    requests, width = queries.shape
    last = width // d - 1
    n_res, tokens, _ = resident.shape
    cap = chunks[0].shape[0]
    pool = (n_res + cap) * tokens
    in_hbm = pl.BlockSpec(memory_space=pltpu.HBM)
    in_vmem = pl.BlockSpec(memory_space=pltpu.VMEM)
    anywhere = pl.BlockSpec(memory_space=pl.ANY)
    arrived_shape = jax.ShapeDtypeStruct((cap, tokens, 2 * width), resident.dtype)
    context_shape = jax.ShapeDtypeStruct((requests, width), jnp.bfloat16)
    parts_shape = [
        jax.ShapeDtypeStruct((requests, cap * tokens), jnp.bfloat16),
        jax.ShapeDtypeStruct((requests, d), jnp.float32),
        jax.ShapeDtypeStruct((requests, d), jnp.float32),
    ]
    scratch = [pltpu.VMEM((requests, pool), jnp.float32), pltpu.SemaphoreType.DMA((cap,))]
    params = pltpu.CompilerParams(vmem_limit_bytes=VMEM_LIMIT)
    cost = pl.CostEstimate(
        flops=4 * requests * pool * d,
        bytes_accessed=6 * pool * d,
        transcendentals=requests * pool,
    )

    def head_specs(h):
        return [
            pl.BlockSpec((requests, d), lambda i: (0, h)),
            whole(bias),
            pl.BlockSpec((n_res, tokens, 2 * d), lambda i: (0, 0, h)),
        ]

    arrived, *parts = pl.pallas_call(
        functools.partial(first_kernel, most),
        grid=(1,),
        in_specs=[pl.BlockSpec(memory_space=pltpu.SMEM), *head_specs(0), whole(chunks[0])],
        out_specs=[in_hbm, *(whole(x) for x in parts_shape)],
        out_shape=[arrived_shape, *parts_shape],
        scratch_shapes=scratch,
        compiler_params=params,
        cost_estimate=cost,
    )(slots, queries, bias, resident, chunks[0])
    context = None
    pieces = [(c, k) for c in chunks[1:-1] for k in range(c.shape[2] // (2 * d))]
    for h, (late, piece) in enumerate(pieces, 1):
        carried = [arrived] if context is None else [arrived, context]
        arrived, context, *parts = pl.pallas_call(
            functools.partial(middle_kernel, most, (2 * h - 1) * d),
            grid=(1,),
            in_specs=[
                *head_specs(h),
                pl.BlockSpec((cap, tokens, 2 * d), lambda i, piece=piece: (0, 0, piece)),
                *(whole(x) for x in parts),
                *[in_hbm, anywhere][: len(carried)],
            ],
            out_specs=[
                in_hbm,
                pl.BlockSpec((requests, d), lambda i, h=h: (0, h - 1)),
                *(whole(x) for x in parts_shape),
            ],
            out_shape=[arrived_shape, context_shape, *parts_shape],
            scratch_shapes=scratch,
            input_output_aliases={7 + i: i for i in range(len(carried))},
            compiler_params=params,
            cost_estimate=cost,
        )(queries, bias, resident, late, *parts, *carried)
    late = chunks[-1]
    n_parts = cap
    sems = pltpu.SemaphoreType.DMA((n_parts,))
    return pl.pallas_call(
        functools.partial(last_kernel, (2 * last + 1) * d),
        in_specs=[in_vmem, in_vmem, in_vmem, anywhere, in_hbm, in_hbm],
        out_specs=[in_hbm, in_hbm],
        out_shape=[arrived_shape, context_shape],
        scratch_shapes=[
            pltpu.SemaphoreType.DMA,
            pltpu.VMEM(late.shape, late.dtype),
            pltpu.VMEM((requests, d), context.dtype),
            sems,
            sems,
        ],
        input_output_aliases={4: 0, 5: 1},
        compiler_params=params,
        cost_estimate=pl.CostEstimate(
            flops=2 * requests * cap * tokens * d,
            bytes_accessed=4 * cap * tokens * d,
            transcendentals=0,
        ),
    )(*parts, late, arrived, context)


def two_ways(distance, n):
    return n <= RADIX and n % 2 == 0 and distance % 2 == 1 and 2 < distance < n - 2


def send(distance, chunks):
    n = lax.axis_size("dp")
    if distance == 0:
        return list(chunks)

    def route(chunk, step_of):
        return lax.ppermute(chunk, "dp", [(i, step_of(i) % n) for i in range(n)])

    def direct(chunk):
        return route(chunk, lambda i: i + distance)

    if not two_ways(distance, n):
        return [direct(c) for c in chunks]
    pairs = n // 2
    far, near = (distance + 1) // 2, (distance - 1) // 2
    odd_is_far = min(far, pairs - far) > min(near, pairs - near)
    far_side = 1 if odd_is_far else 0
    rest = distance + 1 if odd_is_far else distance - 1
    *chunks, halfway, final = chunks
    first, *chunks, final = [direct(c) for c in (*chunks, final)]
    halfway = route(halfway, lambda i: i ^ 1 if i % 2 == far_side else i + distance)
    first, _ = lax.optimization_barrier((first, halfway))
    halfway = route(halfway, lambda i: i if i % 2 == far_side else i + rest)
    return [first, *chunks, halfway, final]


def offset_digits(n):
    digits = []
    place = 1
    while place < n:
        digits.append((place, min(RADIX, -(-n // place))))
        place *= RADIX
    return digits


def quotient(value, by):
    if by & (by - 1) == 0:
        return lax.shift_right_logical(value, by.bit_length() - 1)
    return lax.div(value, by)


def local(new_pages, page_dest, resident, queries, page_table, cross_len):
    n_groups = lax.axis_size("dp")
    cap, tokens, _ = new_pages.shape
    d = HEAD_DIM
    heads = queries.shape[1] // d
    n_res = resident.shape[0]
    offset = quotient(page_dest[0], cap)

    def bias_of(page_table, cross_len):
        slots = jnp.arange(n_res + cap, dtype=jnp.int32)
        within = jnp.arange(page_table.shape[1], dtype=jnp.int32)[None, :] < cross_len[:, None]
        member = (page_table[:, :, None] == slots[None, None, :]) & within[:, :, None]
        bias = jnp.where(jnp.any(member, axis=1), 0.0, -jnp.inf).astype(jnp.float32)
        return jnp.repeat(bias, tokens, axis=1)

    blocks = [((2 * h - 1) * d, 2 * d) for h in range(1, heads)] + [((2 * heads - 1) * d, d)]

    digits = offset_digits(n_groups)
    last = len(digits) - 1

    def step(distance, index, carry, new_pages, page_dest, resident, queries, page_table, cross_len):
        if index == 0:
            order = list(range(len(blocks)))
            if two_ways(distance, n_groups):
                order.insert(0, order.pop(-2))
            after = new_pages[:, :, :d]
            carry = [after] + [None] * len(blocks)
            for c in order:
                after = carry[c + 1] = stage(new_pages, page_dest, *blocks[c], after)
        carry = send(distance, carry)
        if index < last:
            return tuple(carry)
        source = lax.rem(lax.axis_index("dp") - quotient(page_dest[0], cap) + n_groups, n_groups)
        slots = lax.rem(lax.dynamic_slice_in_dim(page_dest, source * cap, cap), cap)
        most = LARGE_GROUP if two_ways(distance, n_groups) else GROUP
        return attend(most, carry, resident, queries, bias_of(page_table, cross_len), slots)

    carry = ()
    for index, (place, base) in enumerate(digits):
        digit = quotient(offset, place)
        first = 1 if last == 0 else 0
        if index < last:
            digit = lax.rem(digit, base)
        carry = lax.switch(
            digit - first,
            [functools.partial(step, k * place, index) for k in range(first, base)],
            carry, new_pages, page_dest, resident, queries, page_table, cross_len,
        )
    return carry


def solution(mesh):
    return jax.shard_map(
        local,
        mesh=mesh,
        in_specs=(
            P("dp", None, "tensor"),
            P(),
            P("dp", None, "tensor"),
            P("dp", "tensor"),
            P("dp", None),
            P("dp"),
        ),
        out_specs=(P("dp", None, "tensor"), P("dp", "tensor")),
        check_vma=False,
    )
```
